32 devices in a mesh: dp: 8 (over z, y), mp: 4 (over x, core).
Axes of the slice: x: 2, y: 2, z: 4, core: 2. Of those that a mesh axis runs over, the one named last changes fastest.
Arguments:
- frames: bfloat16 [8192, 320], P('dp'), may hold values from -6 to 6
- lengths: int32 [8, 128], P('dp'), may hold values from 0 to 15, as said below
- destinations: int32 [8, 128], P('dp'), may hold values from 0 to 7, as said below
- offsets: int32 [8, 128], P('dp'), may hold values from 0 to 255, as said below
- in_weight: bfloat16 [320, 1536], P(None, 'mp'), may hold values from -0.3125 to 0.3125
- depth_weight: bfloat16 [31, 1536], P(None, 'mp'), may hold values from -1 to 1
- out_weight: bfloat16 [1536, 1536], P(None, 'mp'), may hold values from -0.15625 to 0.15625
- cotangent: bfloat16 [2048, 1536], P('dp', 'mp'), may hold values from -6 to 6
Outputs:
- output: bfloat16 [2048, 1536], P('dp', 'mp')
- in_weight_gradient: float32 [320, 1536], P(None, 'mp')
- depth_gradient: float32 [31, 1536], P(None, 'mp')
- out_weight_gradient: float32 [1536, 1536], P('dp', 'mp')
The draws below stay inside these ranges and needn't reach their ends.
Inputs may be any that keep to these rules, and one draw needn't show every extreme that they name: Used entries of a device's list come first and have lengths of 1 or more; later entries have length 0; some utterance has exactly 15 rows. `destinations`: A device's utterances for one destination stand together and fill exactly 128 rows; unused entries name device 0; some device sends to every device. `offsets`: the utterances sent to one device tile its 256 rows exactly; unused entries have offset 0; on every device some utterance starts at row 255.
All inputs are finite; a program needn't handle non-finite values.
Results may differ from the reference program's by a relative error of at most 0.014.
Values may be sent and summed in bfloat16 or wider, within the bound.
A program may use at most 64 MiB of HBM per device.

```python
import math
import jax
import jax.numpy as jnp
from jax import lax

D = 1536
FEAT = 320
KERNEL = 31
PAIR_ROWS = 16
PAIRS = 16
ROWS = 256
SOURCE_ROW_COUNT = 1024
TOKENS = 2048
N_DP = 8
N_MP = 4


def routing_tables(key):
    base_key = jax.random.fold_in(key, 11)
    ranking_key, heavy_key, length_key = jax.random.split(base_key, 3)
    sources = min(PAIRS, N_DP // 4)
    per_slot = PAIRS // sources
    entries = 2 * N_DP * per_slot
    device_numbers = jnp.arange(N_DP, dtype=jnp.int32)
    ordering_numbers = jax.random.permutation(heavy_key, N_DP)
    extra_rank_order = jnp.where(device_numbers == 0, 2 ** 23, jnp.where(device_numbers <= N_DP // 8, 2 ** 19, 0)).astype(jnp.int32)
    extra_score_values = jnp.zeros((N_DP,), jnp.int32).at[ordering_numbers].set(extra_rank_order)
    priority_scores = jax.random.randint(ranking_key, (N_DP, N_DP), 0, 2 ** 20, dtype=jnp.int32) + extra_score_values[None, :]
    priority_scores = priority_scores * N_DP + device_numbers[None, :]
    chosen = lax.top_k(priority_scores, sources)[1].astype(jnp.int32)
    first_part = jax.random.randint(length_key, (N_DP, PAIRS), 1, PAIR_ROWS, dtype=jnp.int32)
    first_part = first_part.at[:, 0].set(1)
    first_part = first_part.at[:, PAIRS - 1].set(PAIR_ROWS - 1)
    chosen_mask = jnp.zeros((N_DP, N_DP), jnp.int32).at[device_numbers[:, None], chosen].set(1)
    rank_table = jnp.cumsum(chosen_mask, axis=0, dtype=jnp.int32) - 1
    grid_shape = (N_DP, sources, per_slot, 2)
    dest_grid = jnp.broadcast_to(device_numbers[:, None, None, None], grid_shape)
    slot_grid = jnp.broadcast_to(jnp.arange(sources, dtype=jnp.int32)[None, :, None, None], grid_shape)
    inner_pair = jnp.broadcast_to(jnp.arange(per_slot, dtype=jnp.int32)[None, None, :, None], grid_shape)
    member_side = jnp.broadcast_to(jnp.arange(2, dtype=jnp.int32)[None, None, None, :], grid_shape)
    source_grid = jnp.broadcast_to(chosen[:, :, None, None], grid_shape)
    rank_grid = rank_table[dest_grid, source_grid]
    pair_index = slot_grid * per_slot + inner_pair
    entry_index = (rank_grid * per_slot + inner_pair) * 2 + member_side
    first_len = first_part[dest_grid, pair_index]
    length_grid = jnp.where(member_side == 0, first_len, PAIR_ROWS - first_len).astype(jnp.int32)
    offset_grid = (pair_index * PAIR_ROWS + member_side * first_len).astype(jnp.int32)
    empty_table = jnp.zeros((N_DP, entries), jnp.int32)
    lengths = empty_table.at[source_grid, entry_index].set(length_grid)
    destinations = empty_table.at[source_grid, entry_index].set(dest_grid)
    offsets = empty_table.at[source_grid, entry_index].set(offset_grid)
    return (lengths, destinations, offsets)


def draw_lengths(key, part):
    return routing_tables(key)[0]


def draw_destinations(key, part):
    return routing_tables(key)[1]


def draw_offsets(key, part):
    return routing_tables(key)[2]


def with_spikes(values, stream_key, source, target, parts, factor):
    owner, partner = [(jnp.arange(values.shape[position]) // (values.shape[position] // parts)).reshape([-1 if axis == position else 1 for axis in range(values.ndim)]) for position in (source, target)]
    chosen = jax.random.permutation(stream_key, parts)[partner]
    strong = (owner == chosen) | (owner == (partner + parts // 2) % parts)
    return jnp.where(strong, factor * values, values)


def level_of(stream_key, dims, cuts, least, high):
    def one(position, parts):
        heights = jax.random.uniform(jax.random.fold_in(jax.random.fold_in(stream_key, 6), position), (parts,), jnp.float32, least / len(cuts), high / len(cuts))
        return jnp.repeat(jnp.exp(heights), dims[position] // parts).reshape((-1,) + (1,) * (len(dims) - position - 1))

    factor_of = one(*cuts[0])
    for cut in cuts[1:]:
        factor_of = factor_of * one(*cut)
    return factor_of


def scatter_about(stream_key, dims, deviation, reach, cuts=(), kind=jnp.bfloat16):
    gain = level_of(stream_key, dims, cuts, -0.22, 0.18) if cuts else 1.0
    values = jax.random.normal(stream_key, dims, jnp.float32) * deviation * gain
    return jnp.minimum(jnp.maximum(values, -reach), reach).astype(kind)


def noise_with(own_key, extent, width, limit, shards, heavy, kind=jnp.bfloat16):
    values = width * jax.random.normal(own_key, extent, jnp.float32)
    if shards:
        values = values * level_of(own_key, extent, shards, -0.22, 0.18)
    return jnp.clip(with_spikes(values, jax.random.fold_in(own_key, 3), *heavy), -limit, limit).astype(kind)


def setup_inputs(seed: int = 0) -> dict:
    splits = jax.random.split(jax.random.key(seed), 9)
    return {
        "frames": scatter_about(splits[0], (N_DP * SOURCE_ROW_COUNT, FEAT), 1.0, 6.0, ((0, 8),)),
        "lengths": draw_lengths(jax.random.fold_in(splits[8], 71), 0),
        "destinations": draw_destinations(jax.random.fold_in(splits[8], 71), 0),
        "offsets": draw_offsets(jax.random.fold_in(splits[8], 71), 0),
        "in_weight": scatter_about(splits[4], (FEAT, D), FEAT ** -0.5, 0.3125, ((1, 4),)),
        "depth_weight": scatter_about(splits[5], (KERNEL, D), KERNEL ** -0.5, 1.0, ((1, 4),)),
        "out_weight": scatter_about(splits[6], (D, D), D ** -0.5, 0.15625, ((1, 4),)),
        "cotangent": noise_with(splits[7], (TOKENS, D), 1.0, 6.0, ((0, 8), (1, 4)), (0, 1, 8, 2.0)),
    }


def depth_conv(values, weights, labels, direction):
    center = (KERNEL - 1) // 2
    length = values.shape[0]
    padded = jnp.pad(values, ((center, center), (0, 0)))
    padded_labels = jnp.pad(labels, (center, center), constant_values=-1)
    result = jnp.zeros(values.shape, jnp.float32)
    for tap_index in range(KERNEL):
        start = center + direction * (tap_index - center)
        matches = (padded_labels[start:start + length] == labels)[:, None]
        taken = weights[tap_index][None, :] * padded[start:start + length]
        result = result + jnp.where(matches, taken, jnp.zeros_like(taken))
    return result

def tap_sums(grads, values, labels):
    center = (KERNEL - 1) // 2
    length = values.shape[0]
    padded = jnp.pad(values, ((center, center), (0, 0)))
    padded_labels = jnp.pad(labels, (center, center), constant_values=-1)
    rows_list = []
    for tap_index in range(KERNEL):
        start = tap_index
        matches = (padded_labels[start:start + length] == labels)[:, None]
        taken = grads * padded[start:start + length]
        rows_list.append(lax.optimization_barrier(jnp.sum(jnp.where(matches, taken, jnp.zeros_like(taken)), axis=0)))
    return jnp.stack(rows_list, 0)

def source_targets(items):
    lengths_row, dests_row, offsets_row, source = items
    entries = lengths_row.shape[0]
    end_rows = jnp.cumsum(lengths_row, dtype=jnp.int32)
    begins = end_rows - lengths_row
    row_ids = jnp.arange(SOURCE_ROW_COUNT, dtype=jnp.int32)
    owner_index = lax.optimization_barrier(jnp.sum((end_rows[None, :] <= row_ids[:, None]).astype(jnp.int32), axis=1, dtype=jnp.int32))
    occupied_rows = owner_index < entries
    clamped = jnp.minimum(owner_index, entries - 1).astype(jnp.int32)
    target = dests_row[clamped] * ROWS + offsets_row[clamped] + row_ids - begins[clamped]
    target = jnp.where(occupied_rows, target, N_DP * ROWS).astype(jnp.int32)
    row_label = (source * entries + clamped).astype(jnp.int32)
    return (target, row_label)

def reference(frames, lengths, destinations, offsets, in_weight, depth_weight, out_weight, cotangent):
    all_rows = N_DP * ROWS
    device_numbers = jnp.arange(N_DP, dtype=jnp.int32)
    targets, labels = lax.map(source_targets, (lengths, destinations, offsets, device_numbers))
    flat_targets = targets.reshape(-1)
    packed = jnp.zeros((all_rows + 1, FEAT), frames.dtype).at[flat_targets].set(frames)[:all_rows]
    packed_labels = jnp.full((all_rows + 1,), -1, jnp.int32).at[flat_targets].set(labels.reshape(-1))[:all_rows]
    hidden = jnp.dot(packed, in_weight, preferred_element_type=jnp.float32).astype(jnp.bfloat16)
    hidden_wide = hidden.astype(jnp.float32)
    taps = depth_weight.astype(jnp.float32)
    convolved = depth_conv(hidden_wide, taps, packed_labels, 1)
    activated = jax.nn.silu(convolved).astype(jnp.bfloat16)
    shard_width = D // N_MP
    branch = jnp.zeros((all_rows, D), jnp.float32)
    for shard_index in range(N_MP):
        lower = shard_index * shard_width
        partial_sum = jnp.dot(activated[:, lower:lower + shard_width], out_weight[:, lower:lower + shard_width].T, preferred_element_type=jnp.float32)
        rounded = lax.optimization_barrier(partial_sum.astype(jnp.bfloat16))
        branch = branch + rounded.astype(jnp.float32)
    output = (hidden_wide + branch).astype(jnp.bfloat16)
    grad_scale = 1.0 / math.sqrt(all_rows)
    grad_activated = jnp.dot(cotangent, out_weight, preferred_element_type=jnp.float32)
    sigmoid_value = jax.nn.sigmoid(convolved)
    grad_convolved = grad_activated * sigmoid_value * (1.0 + convolved * (1.0 - sigmoid_value))
    grad_hidden = (cotangent.astype(jnp.float32) + depth_conv(grad_convolved, taps, packed_labels, -1)).astype(jnp.bfloat16)
    out_weight_gradient = grad_scale * jnp.dot(cotangent.T, activated, preferred_element_type=jnp.float32)
    depth_gradient = grad_scale * tap_sums(grad_convolved, hidden_wide, packed_labels)
    in_weight_gradient = grad_scale * jnp.dot(packed.T, grad_hidden, preferred_element_type=jnp.float32)
    return (output, in_weight_gradient, depth_gradient, out_weight_gradient)
```

```python
import functools
import math

import jax
import jax.numpy as jnp
from jax import lax
from jax.experimental import pallas as pl
from jax.experimental.pallas import tpu as pltpu
from jax.sharding import PartitionSpec as P

KERNEL = 31
ROWS = 256
MESH = pl.DeviceIdType.MESH


def depth_conv(values, weights, labels, direction):
    center = (KERNEL - 1) // 2
    length = values.shape[0]
    padded = jnp.pad(values, ((center, center), (0, 0)))
    padded_labels = jnp.pad(labels, (center, center), constant_values=-1)
    result = jnp.zeros(values.shape, jnp.float32)
    for tap_index in range(KERNEL):
        start = center + direction * (tap_index - center)
        matches = (padded_labels[start : start + length] == labels)[:, None]
        taken = weights[tap_index][None, :] * padded[start : start + length]
        result = result + jnp.where(matches, taken, jnp.zeros_like(taken))
    return result


def tap_sums(grads, values, labels):
    center = (KERNEL - 1) // 2
    length = values.shape[0]
    padded = jnp.pad(values, ((center, center), (0, 0)))
    padded_labels = jnp.pad(labels, (center, center), constant_values=-1)
    rows_list = []
    for tap_index in range(KERNEL):
        matches = (padded_labels[tap_index : tap_index + length] == labels)[:, None]
        taken = grads * padded[tap_index : tap_index + length]
        rows_list.append(jnp.sum(jnp.where(matches, taken, jnp.zeros_like(taken)), axis=0))
    return jnp.stack(rows_list, 0)


def per_device(
    frames, lengths, destinations, offsets, in_weight, depth_weight, out_weight, cotangent
):
    dp_count = lax.axis_size("dp")
    src_rows = frames.shape[0]
    features = frames.shape[1]
    slot_rows = src_rows // dp_count
    entries = lengths.shape[1]
    lengths_row = lengths[0]
    end_rows = jnp.cumsum(lengths_row, dtype=jnp.int32)
    begins = end_rows - lengths_row
    row_ids = jnp.arange(src_rows, dtype=jnp.int32)
    owner_table = (begins[None, :] <= row_ids[:, None]) & (row_ids[:, None] < end_rows[None, :])
    occupied_rows = jnp.any(owner_table, axis=1)
    onehot = owner_table.astype(jnp.int32)

    def lookup(table):
        return jnp.sum(onehot * table[None, :], axis=1, dtype=jnp.int32)

    owner_index = lookup(jnp.arange(entries, dtype=jnp.int32))
    target = lookup(offsets[0]) + row_ids - lookup(begins)
    dest_row = lookup(destinations[0])
    source = lax.axis_index("dp")
    row_label = source * entries + owner_index
    dump_index = dp_count * slot_rows
    slot_index = jnp.where(occupied_rows, dest_row * slot_rows + row_ids % slot_rows, dump_index)
    send_frames = (
        jnp.zeros((dump_index + 1, features), frames.dtype)
        .at[slot_index]
        .set(frames)[:dump_index]
        .reshape(dp_count, slot_rows, features)
    )
    send_target = (
        jnp.full((dump_index + 1,), ROWS, jnp.int32)
        .at[slot_index]
        .set(target)[:dump_index]
        .reshape(dp_count, slot_rows)
    )
    send_label = (
        jnp.full((dump_index + 1,), -1, jnp.int32)
        .at[slot_index]
        .set(row_label)[:dump_index]
        .reshape(dp_count, slot_rows)
    )
    got_frames, got_target, got_label = (
        lax.all_to_all(send_frames, "dp", split_axis=0, concat_axis=0, tiled=True),
        lax.all_to_all(send_target, "dp", split_axis=0, concat_axis=0, tiled=True),
        lax.all_to_all(send_label, "dp", split_axis=0, concat_axis=0, tiled=True),
    )
    flat_target = got_target.reshape(-1)
    packed = (
        jnp.zeros((ROWS + 1, features), frames.dtype)
        .at[flat_target]
        .set(got_frames.reshape(-1, features))[:ROWS]
    )
    packed_labels = (
        jnp.full((ROWS + 1,), -1, jnp.int32).at[flat_target].set(got_label.reshape(-1))[:ROWS]
    )
    hidden = jnp.dot(packed, in_weight, preferred_element_type=jnp.float32).astype(jnp.bfloat16)
    hidden_wide = hidden.astype(jnp.float32)
    taps = depth_weight.astype(jnp.float32)
    convolved = depth_conv(hidden_wide, taps, packed_labels, 1)
    activated = jax.nn.silu(convolved).astype(jnp.bfloat16)
    partial_sum = lax.dot_general(
        activated, out_weight, (((1,), (1,)), ((), ())), preferred_element_type=jnp.float32
    )
    branch = lax.psum_scatter(
        partial_sum.astype(jnp.bfloat16), "mp", scatter_dimension=1, tiled=True
    ).astype(jnp.float32)
    output = (hidden_wide + branch).astype(jnp.bfloat16)
    cotangent_full = lax.all_gather(cotangent, "mp", axis=1, tiled=True)
    grad_scale = 1.0 / math.sqrt(dp_count * ROWS)
    grad_activated = jnp.dot(cotangent_full, out_weight, preferred_element_type=jnp.float32)
    sigmoid_value = jax.nn.sigmoid(convolved)
    grad_convolved = grad_activated * sigmoid_value * (1.0 + convolved * (1.0 - sigmoid_value))
    grad_hidden = (
        cotangent.astype(jnp.float32) + depth_conv(grad_convolved, taps, packed_labels, -1)
    ).astype(jnp.bfloat16)
    out_weight_gradient = lax.psum_scatter(
        grad_scale
        * lax.dot_general(
            cotangent_full, activated, (((0,), (0,)), ((), ())), preferred_element_type=jnp.float32
        ),
        "dp",
        scatter_dimension=0,
        tiled=True,
    )
    term_in = grad_scale * lax.dot_general(
        packed, grad_hidden, (((0,), (0,)), ((), ())), preferred_element_type=jnp.float32
    )
    term_depth = grad_scale * tap_sums(grad_convolved, hidden_wide, packed_labels)
    in_weight_gradient, depth_gradient = lax.psum((term_in, term_depth), "dp")
    return (output, in_weight_gradient, depth_gradient, out_weight_gradient)


def fused_kernel(
    n_dp, n_mp, scale,
    frames, lens, dests, offs, w_in, w_depth, w_out, cot,
    out_ref, gin_ref, gdep_ref, gout_ref,
    tables, slots, got, comp_all, cot_all, cot_t, packed, lab_pad, masks, taps, hpad, act, gact, gpad, ghid,
    part, part_got, dy_send, dy_got, dz_send, dz_got, dz_own, gfull, gs, ggot, gall,
    tab_s, tab_r, fr_s, fr_r, cp_s, cp_r, ct_s, ct_r, pt_s, pt_r, dy_s, dy_r, dz_s, dz_r, gr_s, gr_r, ga_s, ga_r,
):
    f32, bf16 = jnp.float32, jnp.bfloat16
    me = lax.axis_index("dp")
    mine = lax.axis_index("mp")
    src_rows, features = frames.shape
    slot_rows = src_rows // n_dp
    quarter = slot_rows // n_mp
    sources = ROWS // slot_rows
    width = cot.shape[1]
    entries = lens.shape[1]
    block = gout_ref.shape[0]
    strip = gs.shape[1]
    centre = (KERNEL - 1) // 2
    pad = 16
    n_z = n_dp // 2
    zi, yi = me // 2, lax.rem(me, 2)
    chunk = 64

    def dp_peer(k):
        return lax.rem(me + k, n_dp)

    def dp_from(k):
        return lax.rem(me + n_dp - k, n_dp)

    def mp_peer(k):
        return lax.rem(mine + k, n_mp)

    def mp_from(k):
        return lax.rem(mine + n_mp - k, n_mp)

    def send(src, dst, ssem, rsem, **where):
        return pltpu.make_async_remote_copy(
            src_ref=src, dst_ref=dst, send_sem=ssem, recv_sem=rsem, device_id=where, device_id_type=MESH
        )

    barrier = pltpu.get_barrier_semaphore()
    for k in range(1, n_dp):
        pl.semaphore_signal(barrier, inc=1, device_id={"dp": dp_peer(k)}, device_id_type=MESH)
    for k in range(1, n_mp):
        pl.semaphore_signal(barrier, inc=1, device_id={"mp": mp_peer(k)}, device_id_type=MESH)

    len_f = lens[...].astype(f32)
    dest_f = dests[...].astype(f32)
    off_f = offs[...].astype(f32)
    before = (
        lax.broadcasted_iota(jnp.int32, (entries, entries), 0) < lax.broadcasted_iota(jnp.int32, (entries, entries), 1)
    )
    begin_f = jnp.dot(
        jnp.broadcast_to(len_f, (8, entries)).astype(bf16), jnp.where(before, 1.0, 0.0).astype(bf16),
        preferred_element_type=f32,
    )[0:1]
    tables[me] = jnp.concatenate([len_f, dest_f, off_f, begin_f, jnp.zeros((4, entries), f32)], 0)
    row = lax.broadcasted_iota(jnp.int32, (n_dp * quarter, 1), 0)
    row_dest = (row // quarter).astype(f32)
    row_in = lax.rem(row, quarter).astype(f32)
    first = jnp.min(jnp.where((dest_f == row_dest) & (len_f > 0.0), begin_f, 1e6), axis=1, keepdims=True)
    wanted = first + row_in + (mine * quarter).astype(f32)
    cols = lax.broadcasted_iota(jnp.int32, (n_dp * quarter, src_rows), 1).astype(f32)
    pick = jnp.where(cols == wanted, 1.0, 0.0).astype(bf16)
    chosen = jnp.dot(pick, frames[...], preferred_element_type=f32).astype(bf16)
    for d in range(n_dp):
        slots[d] = chosen[d * quarter : (d + 1) * quarter]
    got[me] = slots[me]
    cot_all[mine] = cot[...]

    pl.semaphore_wait(barrier, n_dp - 1 + n_mp - 1)
    tab_c, fr_c, ct_c = [], [], []
    for k in range(1, n_dp):
        c = send(tables.at[me], tables.at[me], tab_s.at[k], tab_r.at[k], dp=dp_peer(k))
        c.start()
        tab_c.append(c)
    for k in range(1, n_dp):
        c = send(slots.at[dp_peer(k)], got.at[me], fr_s.at[k], fr_r.at[k], dp=dp_peer(k))
        c.start()
        fr_c.append(c)
    for k in range(1, n_mp):
        c = send(cot, cot_all.at[mine], ct_s.at[k], ct_r.at[k], mp=mp_peer(k))
        c.start()
        ct_c.append(c)

    taps[0:KERNEL] = w_depth[...].astype(f32)
    for ref in (hpad, gpad):
        ref[0:pad] = jnp.zeros((pad, width), f32)
        ref[pad + ROWS :] = jnp.zeros((pad, width), f32)
    gfull[...] = jnp.zeros_like(gfull)

    def arrived(dst, ssem, rsem, **where):
        send(dst, dst, ssem, rsem, **where).wait_recv()

    for k in range(1, n_dp):
        src = dp_from(k)
        arrived(tables.at[src], tab_s.at[k], tab_r.at[k], dp=src)

    here = me.astype(f32)
    t_row = lax.broadcasted_iota(jnp.int32, (ROWS, 1), 0).astype(f32)
    lane = lax.broadcasted_iota(jnp.int32, (1, entries), 1).astype(f32)
    shift = jnp.zeros((ROWS, entries), f32)
    order = jnp.zeros((ROWS, entries), f32)
    label = jnp.zeros((ROWS, entries), f32)
    rank = jnp.zeros((1, 1), f32)
    selectors = []
    for s in range(n_dp):
        table = tables[s]
        t_len, t_dest, t_off, t_begin = table[0:1], table[1:2], table[2:3], table[3:4]
        to_me = (t_dest == here) & (t_len > 0.0)
        valid = jnp.max(jnp.where(to_me, 1.0, 0.0), axis=1, keepdims=True)
        match = to_me & (t_off <= t_row) & (t_row < t_off + t_len)
        inside = t_begin - slot_rows * jnp.floor(t_begin / slot_rows)
        shift = shift + jnp.where(match, inside - t_off, 0.0)
        order = order + jnp.where(match, rank, 0.0)
        label = label + jnp.where(match, s * entries + lane, 0.0)
        selectors.append([jnp.where((valid > 0.0) & (rank == r), 1.0, 0.0) for r in range(sources)])
        rank = rank + valid
    q = jnp.sum(shift, axis=1, keepdims=True) + t_row
    rank_of = jnp.sum(order, axis=1, keepdims=True)
    q_part = jnp.floor(q / quarter)
    place = q_part * (sources * quarter) + rank_of * quarter + (q - q_part * quarter)
    spots = lax.broadcasted_iota(jnp.int32, (ROWS, ROWS), 1).astype(f32)
    pick_rows = jnp.where(spots == place, 1.0, 0.0).astype(bf16)
    lab_pad[0:pad] = jnp.full((pad, 128), -1.0, f32)
    lab_pad[pad + ROWS :] = jnp.full((pad, 128), -1.0, f32)
    lab_pad[pad : pad + ROWS] = jnp.broadcast_to(jnp.sum(label, axis=1, keepdims=True), (ROWS, 128))
    for j in range(KERNEL):
        start = pad + j - centre
        masks[j] = jnp.where(lab_pad[start : start + ROWS] == lab_pad[pad : pad + ROWS], 1.0, 0.0)

    for k in range(1, n_dp):
        src = dp_from(k)
        arrived(got.at[src], fr_s.at[k], fr_r.at[k], dp=src)
    picked = [jnp.zeros((quarter, features), f32) for _ in range(sources)]
    for s in range(n_dp):
        rows_s = got[s].astype(f32)
        for r in range(sources):
            picked[r] = picked[r] + selectors[s][r] * rows_s
    comp_all[mine] = jnp.concatenate(picked, 0).astype(bf16)
    cp_c = []
    for k in range(1, n_mp):
        c = send(comp_all.at[mine], comp_all.at[mine], cp_s.at[k], cp_r.at[k], mp=mp_peer(k))
        c.start()
        cp_c.append(c)

    for k in range(1, n_mp):
        src = mp_from(k)
        arrived(cot_all.at[src], ct_s.at[k], ct_r.at[k], mp=src)
    for b in range(n_mp):
        cot_t[b * width : (b + 1) * width] = cot_all[b].T
    for b in range(n_mp):
        term = jnp.dot(cot_all[b], w_out[b * width : (b + 1) * width], preferred_element_type=f32)
        gact[...] = term if b == 0 else gact[...] + term

    for k in range(1, n_mp):
        src = mp_from(k)
        arrived(comp_all.at[src], cp_s.at[k], cp_r.at[k], mp=src)
    everything = jnp.concatenate([comp_all[b] for b in range(n_mp)], 0)
    packed[...] = jnp.dot(pick_rows, everything, preferred_element_type=f32).astype(bf16)
    hpad[pad : pad + ROWS] = jnp.dot(packed[...], w_in[...], preferred_element_type=f32).astype(bf16).astype(f32)

    def columns(c):
        return pl.ds(pl.multiple_of(c * 128, 128), 128)

    def conv(values, direction, emit):
        def body(c, carry):
            cs = columns(c)
            weights = taps[:, cs]
            for base in range(0, ROWS, chunk):
                total = jnp.zeros((chunk, 128), f32)
                for j in range(KERNEL):
                    start = pad + base + direction * (j - centre)
                    mask = masks[j if direction == 1 else KERNEL - 1 - j, base : base + chunk]
                    total = total + weights[j : j + 1] * (values[start : start + chunk, cs] * mask)
                emit(base, cs, total)
            return carry

        lax.fori_loop(0, width // 128, body, 0)

    def forward(base, cs, total):
        rows = slice(base, base + chunk)
        gate = 1.0 / (1.0 + jnp.exp(-total))
        act[rows, cs] = (total * gate).astype(bf16)
        gpad[pad + base : pad + base + chunk, cs] = gact[rows, cs] * gate * (1.0 + total * (1.0 - gate))

    conv(hpad, 1, forward)

    def dw_rows(d):
        at = pl.ds(pl.multiple_of(d * block, 64), block)
        return jnp.dot(cot_t[at], act[...], preferred_element_type=f32)

    z_order = [2, 1, 3, 0] if n_z == 4 else list(range(1, n_z)) + [0]
    dy_c, dz_c, pt_c = [], [], []
    for kz in z_order:
        zt = lax.rem(zi + kz, n_z)
        dy_send[kz] = dw_rows(2 * zt + 1 - yi).astype(bf16)
        c = send(dy_send.at[kz], dy_got.at[kz], dy_s.at[kz], dy_r.at[kz], dp=2 * zi + 1 - yi)
        c.start()
        dy_c.append(c)
    for k in [2, 3, 1, 0] if n_mp == 4 else list(range(1, n_mp)) + [0]:
        at = pl.ds(pl.multiple_of(mp_peer(k) * width, 128), width)
        part[k] = lax.dot_general(
            act[...], w_out[at], (((1,), (1,)), ((), ())), preferred_element_type=f32
        ).astype(bf16)
        if k:
            c = send(part.at[k], part_got.at[k], pt_s.at[k], pt_r.at[k], mp=mp_peer(k))
            c.start()
            pt_c.append(c)

    def tap_body(c, carry):
        cs = columns(c)
        for j in range(KERNEL):
            total = jnp.zeros((chunk, 128), f32)
            for base in range(0, ROWS, chunk):
                start = pad + base + j - centre
                total = total + gpad[pad + base : pad + base + chunk, cs] * (
                    hpad[start : start + chunk, cs] * masks[j, base : base + chunk]
                )
            gfull[features + j : features + j + 1, cs] = jnp.sum(total, axis=0, keepdims=True)
        return carry

    def backward(base, cs, total):
        rows = slice(base, base + chunk)
        ghid[rows, cs] = (cot[rows, cs].astype(f32) + total).astype(bf16)

    def dz_step(kz):
        zt = lax.rem(zi + kz, n_z)
        arrived(dy_got.at[kz], dy_s.at[kz], dy_r.at[kz], dp=2 * zi + 1 - yi)
        total = dw_rows(2 * zt + yi) + dy_got[kz].astype(f32)
        if kz:
            dz_send[kz] = total.astype(bf16)
            c = send(dz_send.at[kz], dz_got.at[kz], dz_s.at[kz], dz_r.at[kz], dp=2 * zt + yi)
            c.start()
            dz_c.append(c)
        else:
            dz_own[...] = total

    conv(gpad, -1, backward)
    dz_step(z_order[0])
    lax.fori_loop(0, width // 128, tap_body, 0)
    gfull[0:features] = lax.dot_general(
        packed[...], ghid[...], (((0,), (0,)), ((), ())), preferred_element_type=f32
    )
    for d in range(n_dp):
        gs[d] = gfull[d * strip : (d + 1) * strip].astype(bf16)
    gr_c, ga_c = [], []
    for k in range(1, n_dp):
        c = send(gs.at[dp_peer(k)], ggot.at[k], gr_s.at[k], gr_r.at[k], dp=dp_peer(k))
        c.start()
        gr_c.append(c)
    for kz in z_order[1:]:
        dz_step(kz)
    total = gfull[pl.ds(pl.multiple_of(me * strip, 16), strip)]
    for k in range(1, n_dp):
        arrived(ggot.at[k], gr_s.at[k], gr_r.at[k], dp=dp_from(k))
        total = total + ggot[k].astype(f32)
    gall[me] = total.astype(bf16)
    for k in range(1, n_dp):
        c = send(gall.at[me], gall.at[me], ga_s.at[k], ga_r.at[k], dp=dp_peer(k))
        c.start()
        ga_c.append(c)

    branch = part[0].astype(f32)
    for k in range(1, n_mp):
        arrived(part_got.at[k], pt_s.at[k], pt_r.at[k], mp=mp_from(k))
        branch = branch + part_got[k].astype(f32)
    out_ref[...] = (hpad[pad : pad + ROWS] + branch).astype(out_ref.dtype)
    total = dz_own[...]
    for kz in range(1, n_z):
        src = 2 * lax.rem(zi + n_z - kz, n_z) + yi
        arrived(dz_got.at[kz], dz_s.at[kz], dz_r.at[kz], dp=src)
        total = total + dz_got[kz].astype(f32)
    gout_ref[...] = scale * total
    for k in range(1, n_dp):
        src = dp_from(k)
        arrived(gall.at[src], ga_s.at[k], ga_r.at[k], dp=src)
    sums = scale * jnp.concatenate([gall[d].astype(f32) for d in range(n_dp)], 0)
    gin_ref[...] = sums[0:features]
    gdep_ref[...] = sums[features : features + KERNEL]
    for c in tab_c + fr_c + ct_c + cp_c + dy_c + pt_c + dz_c + gr_c + ga_c:
        c.wait_send()


def fused(frames, lengths, destinations, offsets, in_weight, depth_weight, out_weight, cotangent):
    n_dp, n_mp = lax.axis_size("dp"), lax.axis_size("mp")
    src_rows, features = frames.shape
    entries = lengths.shape[1]
    width = cotangent.shape[1]
    model = out_weight.shape[0]
    block = model // n_dp
    quarter = src_rows // n_dp // n_mp
    sources = ROWS * n_dp // src_rows
    strip = -(-(features + KERNEL) // (16 * n_dp)) * 16
    n_z = n_dp // 2
    f32, bf16 = jnp.float32, jnp.bfloat16
    vm = pltpu.VMEM
    scratch = [
        vm((n_dp, 8, entries), f32),
        vm((n_dp, quarter, features), bf16),
        vm((n_dp, quarter, features), bf16),
        vm((n_mp, sources * quarter, features), bf16),
        vm((n_mp, ROWS, width), bf16),
        vm((model, ROWS), bf16),
        vm((ROWS, features), bf16),
        vm((ROWS + 32, 128), f32),
        vm((KERNEL, ROWS, 128), f32),
        vm((32, width), f32),
        vm((ROWS + 32, width), f32),
        vm((ROWS, width), bf16),
        vm((ROWS, width), f32),
        vm((ROWS + 32, width), f32),
        vm((ROWS, width), bf16),
        vm((n_mp, ROWS, width), bf16),
        vm((n_mp, ROWS, width), bf16),
        vm((n_z, block, width), bf16),
        vm((n_z, block, width), bf16),
        vm((n_z, block, width), bf16),
        vm((n_z, block, width), bf16),
        vm((block, width), f32),
        vm((n_dp * strip, width), f32),
        vm((n_dp, strip, width), bf16),
        vm((n_dp, strip, width), bf16),
        vm((n_dp, strip, width), bf16),
    ]
    for count in (n_dp, n_dp, n_mp, n_mp, n_mp, n_z, n_z, n_dp, n_dp):
        scratch += [pltpu.SemaphoreType.DMA((count,)), pltpu.SemaphoreType.DMA((count,))]
    whole = pl.BlockSpec(memory_space=pltpu.VMEM)
    return pl.pallas_call(
        functools.partial(fused_kernel, n_dp, n_mp, 1.0 / math.sqrt(n_dp * ROWS)),
        out_shape=(
            jax.ShapeDtypeStruct((ROWS, width), bf16),
            jax.ShapeDtypeStruct((features, width), f32),
            jax.ShapeDtypeStruct((KERNEL, width), f32),
            jax.ShapeDtypeStruct((block, width), f32),
        ),
        in_specs=[whole] * 8,
        out_specs=(whole,) * 4,
        scratch_shapes=scratch,
        compiler_params=pltpu.CompilerParams(
            collective_id=0, has_side_effects=True, vmem_limit_bytes=48 * 1024 * 1024
        ),
    )(frames, lengths, destinations, offsets, in_weight, depth_weight, out_weight, cotangent)


def solution(mesh):
    small = mesh.shape["dp"] <= 16 and mesh.shape["dp"] % 2 == 0
    placed = (
        P("dp", None),
        P("dp", None),
        P("dp", None),
        P("dp", None),
        P(None, "mp"),
        P(None, "mp"),
        P(None, "mp"),
        P("dp", "mp"),
    )
    return jax.shard_map(
        fused if small else per_device,
        mesh=mesh,
        in_specs=placed,
        out_specs=(P("dp", "mp"), P(None, "mp"), P(None, "mp"), P("dp", "mp")),
        check_vma=False,
    )
```

```python
import functools
import math

import jax
import jax.numpy as jnp
from jax import lax
from jax.experimental import pallas as pl
from jax.experimental.pallas import tpu as pltpu
from jax.sharding import PartitionSpec as P

KERNEL = 31
ROWS = 256
MESH = pl.DeviceIdType.MESH


def depth_conv(values, weights, labels, direction):
    center = (KERNEL - 1) // 2
    length = values.shape[0]
    padded = jnp.pad(values, ((center, center), (0, 0)))
    padded_labels = jnp.pad(labels, (center, center), constant_values=-1)
    result = jnp.zeros(values.shape, jnp.float32)
    for tap_index in range(KERNEL):
        start = center + direction * (tap_index - center)
        matches = (padded_labels[start : start + length] == labels)[:, None]
        taken = weights[tap_index][None, :] * padded[start : start + length]
        result = result + jnp.where(matches, taken, jnp.zeros_like(taken))
    return result


def tap_sums(grads, values, labels):
    center = (KERNEL - 1) // 2
    length = values.shape[0]
    padded = jnp.pad(values, ((center, center), (0, 0)))
    padded_labels = jnp.pad(labels, (center, center), constant_values=-1)
    rows_list = []
    for tap_index in range(KERNEL):
        matches = (padded_labels[tap_index : tap_index + length] == labels)[:, None]
        taken = grads * padded[tap_index : tap_index + length]
        rows_list.append(jnp.sum(jnp.where(matches, taken, jnp.zeros_like(taken)), axis=0))
    return jnp.stack(rows_list, 0)


def per_device(
    frames, lengths, destinations, offsets, in_weight, depth_weight, out_weight, cotangent
):
    dp_count = lax.axis_size("dp")
    src_rows = frames.shape[0]
    features = frames.shape[1]
    slot_rows = src_rows // dp_count
    entries = lengths.shape[1]
    lengths_row = lengths[0]
    end_rows = jnp.cumsum(lengths_row, dtype=jnp.int32)
    begins = end_rows - lengths_row
    row_ids = jnp.arange(src_rows, dtype=jnp.int32)
    owner_table = (begins[None, :] <= row_ids[:, None]) & (row_ids[:, None] < end_rows[None, :])
    occupied_rows = jnp.any(owner_table, axis=1)
    onehot = owner_table.astype(jnp.int32)

    def lookup(table):
        return jnp.sum(onehot * table[None, :], axis=1, dtype=jnp.int32)

    owner_index = lookup(jnp.arange(entries, dtype=jnp.int32))
    target = lookup(offsets[0]) + row_ids - lookup(begins)
    dest_row = lookup(destinations[0])
    source = lax.axis_index("dp")
    row_label = source * entries + owner_index
    dump_index = dp_count * slot_rows
    slot_index = jnp.where(occupied_rows, dest_row * slot_rows + row_ids % slot_rows, dump_index)
    send_frames = (
        jnp.zeros((dump_index + 1, features), frames.dtype)
        .at[slot_index]
        .set(frames)[:dump_index]
        .reshape(dp_count, slot_rows, features)
    )
    send_target = (
        jnp.full((dump_index + 1,), ROWS, jnp.int32)
        .at[slot_index]
        .set(target)[:dump_index]
        .reshape(dp_count, slot_rows)
    )
    send_label = (
        jnp.full((dump_index + 1,), -1, jnp.int32)
        .at[slot_index]
        .set(row_label)[:dump_index]
        .reshape(dp_count, slot_rows)
    )
    got_frames, got_target, got_label = (
        lax.all_to_all(send_frames, "dp", split_axis=0, concat_axis=0, tiled=True),
        lax.all_to_all(send_target, "dp", split_axis=0, concat_axis=0, tiled=True),
        lax.all_to_all(send_label, "dp", split_axis=0, concat_axis=0, tiled=True),
    )
    flat_target = got_target.reshape(-1)
    packed = (
        jnp.zeros((ROWS + 1, features), frames.dtype)
        .at[flat_target]
        .set(got_frames.reshape(-1, features))[:ROWS]
    )
    packed_labels = (
        jnp.full((ROWS + 1,), -1, jnp.int32).at[flat_target].set(got_label.reshape(-1))[:ROWS]
    )
    hidden = jnp.dot(packed, in_weight, preferred_element_type=jnp.float32).astype(jnp.bfloat16)
    hidden_wide = hidden.astype(jnp.float32)
    taps = depth_weight.astype(jnp.float32)
    convolved = depth_conv(hidden_wide, taps, packed_labels, 1)
    activated = jax.nn.silu(convolved).astype(jnp.bfloat16)
    partial_sum = lax.dot_general(
        activated, out_weight, (((1,), (1,)), ((), ())), preferred_element_type=jnp.float32
    )
    branch = lax.psum_scatter(
        partial_sum.astype(jnp.bfloat16), "mp", scatter_dimension=1, tiled=True
    ).astype(jnp.float32)
    output = (hidden_wide + branch).astype(jnp.bfloat16)
    cotangent_full = lax.all_gather(cotangent, "mp", axis=1, tiled=True)
    grad_scale = 1.0 / math.sqrt(dp_count * ROWS)
    grad_activated = jnp.dot(cotangent_full, out_weight, preferred_element_type=jnp.float32)
    sigmoid_value = jax.nn.sigmoid(convolved)
    grad_convolved = grad_activated * sigmoid_value * (1.0 + convolved * (1.0 - sigmoid_value))
    grad_hidden = (
        cotangent.astype(jnp.float32) + depth_conv(grad_convolved, taps, packed_labels, -1)
    ).astype(jnp.bfloat16)
    out_weight_gradient = lax.psum_scatter(
        grad_scale
        * lax.dot_general(
            cotangent_full, activated, (((0,), (0,)), ((), ())), preferred_element_type=jnp.float32
        ),
        "dp",
        scatter_dimension=0,
        tiled=True,
    )
    term_in = grad_scale * lax.dot_general(
        packed, grad_hidden, (((0,), (0,)), ((), ())), preferred_element_type=jnp.float32
    )
    term_depth = grad_scale * tap_sums(grad_convolved, hidden_wide, packed_labels)
    in_weight_gradient, depth_gradient = lax.psum((term_in, term_depth), "dp")
    return (output, in_weight_gradient, depth_gradient, out_weight_gradient)


def fused_kernel(
    n_dp, n_mp, scale,
    frames_in, lens_in, dests_in, offs_in, w_in_in, w_depth_in, w_out_in, cot_in,
    out_ref, gin_ref, gdep_ref, gout_ref,
    frames, lens, dests, offs, w_in, w_depth, w_out, in_sem,
    tables, slots, got, comp_all, cot_all, cot_t, packed, lab_pad, masks, taps, hpad, act, gact, gpad, ghid,
    part, part_got, dy_send, dy_got, dz_send, dz_got, dz_own, gfull, tap_acc, gs, gy_got, gz_send, gz_got, gall,
    tab_s, tab_r, fr_s, fr_r, cp_s, cp_r, ct_s, ct_r, pt_s, pt_r, dy_s, dy_r, dz_s, dz_r, gy_s, gy_r, gz_s, gz_r, ga_s, ga_r, gb_s, gb_r,
):
    f32, bf16 = jnp.float32, jnp.bfloat16
    me = lax.axis_index("dp")
    mine = lax.axis_index("mp")
    features, src_rows = frames.shape
    slot_rows = src_rows // n_dp
    quarter = slot_rows // n_mp
    sources = ROWS // slot_rows
    width = cot_all.shape[2]
    entries = lens.shape[1]
    block = gout_ref.shape[0]
    strip = gs.shape[2]
    centre = (KERNEL - 1) // 2
    pad = 16
    n_z = n_dp // 2
    zi, yi = me // 2, lax.rem(me, 2)
    chunk = 64

    def dp_peer(k):
        return lax.rem(me + k, n_dp)

    def dp_from(k):
        return lax.rem(me + n_dp - k, n_dp)

    def mp_peer(k):
        return lax.rem(mine + k, n_mp)

    def mp_from(k):
        return lax.rem(mine + n_mp - k, n_mp)

    def send(src, dst, ssem, rsem, **where):
        return pltpu.make_async_remote_copy(
            src_ref=src, dst_ref=dst, send_sem=ssem, recv_sem=rsem, device_id=where, device_id_type=MESH
        )

    loads = [
        pltpu.make_async_copy(src, dst, in_sem.at[i])
        for i, (src, dst) in enumerate(
            [(lens_in, lens), (dests_in, dests), (offs_in, offs), (frames_in, frames), (cot_in, cot_all.at[mine]),
             (w_depth_in, w_depth), (w_in_in, w_in), (w_out_in, w_out)]
        )
    ]
    for load in loads:
        load.start()
    barrier = pltpu.get_barrier_semaphore()
    for k in range(1, n_dp):
        pl.semaphore_signal(barrier, inc=1, device_id={"dp": dp_peer(k)}, device_id_type=MESH)
    for k in range(1, n_mp):
        pl.semaphore_signal(barrier, inc=1, device_id={"mp": mp_peer(k)}, device_id_type=MESH)

    for load in loads[:3]:
        load.wait()
    len_f = lens[...].astype(f32)
    dest_f = dests[...].astype(f32)
    off_f = offs[...].astype(f32)
    before = (
        lax.broadcasted_iota(jnp.int32, (entries, entries), 0) < lax.broadcasted_iota(jnp.int32, (entries, entries), 1)
    )
    begin_f = jnp.dot(
        jnp.broadcast_to(len_f, (8, entries)).astype(bf16), jnp.where(before, 1.0, 0.0).astype(bf16),
        preferred_element_type=f32,
    )[0:1]
    tables[me] = jnp.concatenate([len_f, dest_f, off_f, begin_f, jnp.zeros((4, entries), f32)], 0)
    row = lax.broadcasted_iota(jnp.int32, (n_dp * quarter, 1), 0)
    row_dest = (row // quarter).astype(f32)
    row_in = lax.rem(row, quarter).astype(f32)
    first = jnp.min(jnp.where((dest_f == row_dest) & (len_f > 0.0), begin_f, 1e6), axis=1, keepdims=True)
    wanted = first + row_in + (mine * quarter).astype(f32)
    cols = lax.broadcasted_iota(jnp.int32, (n_dp * quarter, src_rows), 1).astype(f32)
    pick = jnp.where(cols == wanted, 1.0, 0.0).astype(bf16)
    loads[3].wait()
    chosen = lax.dot_general(
        pick, frames[...], (((1,), (1,)), ((), ())), preferred_element_type=f32
    ).astype(bf16)
    for d in range(n_dp):
        slots[d] = chosen[d * quarter : (d + 1) * quarter]
    got[me] = slots[me]

    pl.semaphore_wait(barrier, n_dp - 1 + n_mp - 1)
    tab_c, fr_c, ct_c = [], [], []
    for k in range(1, n_dp):
        c = send(tables.at[me], tables.at[me], tab_s.at[k], tab_r.at[k], dp=dp_peer(k))
        c.start()
        tab_c.append(c)
    for k in range(1, n_dp):
        c = send(slots.at[dp_peer(k)], got.at[me], fr_s.at[k], fr_r.at[k], dp=dp_peer(k))
        c.start()
        fr_c.append(c)
    sibling = mine + 1 - 2 * lax.rem(mine, 2)
    across = lax.rem(mine + 2, n_mp)
    for k, peer in ((0, across), (1, sibling)):
        c = send(cot_in, cot_all.at[mine], ct_s.at[k], ct_r.at[k], mp=peer)
        c.start()
        ct_c.append(c)
    for load in loads[4:]:
        load.wait()

    taps[0:KERNEL] = w_depth[...].astype(f32)
    for ref in (hpad, gpad):
        ref[0:pad] = jnp.zeros((pad, width), f32)
        ref[pad + ROWS :] = jnp.zeros((pad, width), f32)
    gfull[...] = jnp.zeros_like(gfull)

    def arrived(dst, ssem, rsem, **where):
        send(dst, dst, ssem, rsem, **where).wait_recv()

    for k in range(1, n_dp):
        src = dp_from(k)
        arrived(tables.at[src], tab_s.at[k], tab_r.at[k], dp=src)

    here = me.astype(f32)
    t_row = lax.broadcasted_iota(jnp.int32, (ROWS, 1), 0).astype(f32)
    lane = lax.broadcasted_iota(jnp.int32, (1, entries), 1).astype(f32)
    shift = jnp.zeros((ROWS, entries), f32)
    order = jnp.zeros((ROWS, entries), f32)
    label = jnp.zeros((ROWS, entries), f32)
    rank = jnp.zeros((1, 1), f32)
    selectors = []
    for s in range(n_dp):
        table = tables[s]
        t_len, t_dest, t_off, t_begin = table[0:1], table[1:2], table[2:3], table[3:4]
        to_me = (t_dest == here) & (t_len > 0.0)
        valid = jnp.max(jnp.where(to_me, 1.0, 0.0), axis=1, keepdims=True)
        match = to_me & (t_off <= t_row) & (t_row < t_off + t_len)
        inside = t_begin - slot_rows * jnp.floor(t_begin / slot_rows)
        shift = shift + jnp.where(match, inside - t_off, 0.0)
        order = order + jnp.where(match, rank, 0.0)
        label = label + jnp.where(match, s * entries + lane, 0.0)
        selectors.append([jnp.where((valid > 0.0) & (rank == r), 1.0, 0.0) for r in range(sources)])
        rank = rank + valid
    q = jnp.sum(shift, axis=1, keepdims=True) + t_row
    rank_of = jnp.sum(order, axis=1, keepdims=True)
    q_part = jnp.floor(q / quarter)
    place = q_part * (sources * quarter) + rank_of * quarter + (q - q_part * quarter)
    spots = lax.broadcasted_iota(jnp.int32, (ROWS, ROWS), 1).astype(f32)
    pick_rows = jnp.where(spots == place, 1.0, 0.0).astype(bf16)
    lab_pad[0:pad] = jnp.full((pad, 128), -1.0, f32)
    lab_pad[pad + ROWS :] = jnp.full((pad, 128), -1.0, f32)
    lab_pad[pad : pad + ROWS] = jnp.broadcast_to(jnp.sum(label, axis=1, keepdims=True), (ROWS, 128))
    for j in range(KERNEL):
        start = pad + j - centre
        masks[j] = jnp.where(lab_pad[start : start + ROWS] == lab_pad[pad : pad + ROWS], 1.0, 0.0)

    for k in range(1, n_dp):
        src = dp_from(k)
        arrived(got.at[src], fr_s.at[k], fr_r.at[k], dp=src)
    picked = [jnp.zeros((quarter, features), f32) for _ in range(sources)]
    for s in range(n_dp):
        rows_s = got[s].astype(f32)
        for r in range(sources):
            picked[r] = picked[r] + selectors[s][r] * rows_s
    comp_all[mine] = jnp.concatenate(picked, 0).astype(bf16)
    cp_c = []
    for k in range(1, n_mp):
        c = send(comp_all.at[mine], comp_all.at[mine], cp_s.at[k], cp_r.at[k], mp=mp_peer(k))
        c.start()
        cp_c.append(c)

    arrived(cot_all.at[across], ct_s.at[0], ct_r.at[0], mp=across)
    c = send(cot_all.at[across], cot_all.at[across], ct_s.at[2], ct_r.at[2], mp=sibling)
    c.start()
    ct_c.append(c)

    def use_cotangent(b, start):
        at = pl.ds(pl.multiple_of(b * width, 128), width)
        values = cot_all[b]
        cot_t[at] = values.T
        term = jnp.dot(values, w_out[at], preferred_element_type=f32)
        gact[...] = term if start else gact[...] + term

    use_cotangent(mine, True)
    use_cotangent(across, False)
    arrived(cot_all.at[sibling], ct_s.at[1], ct_r.at[1], mp=sibling)
    use_cotangent(sibling, False)
    diagonal = lax.rem(sibling + 2, n_mp)
    arrived(cot_all.at[diagonal], ct_s.at[2], ct_r.at[2], mp=sibling)
    use_cotangent(diagonal, False)

    for k in range(1, n_mp):
        src = mp_from(k)
        arrived(comp_all.at[src], cp_s.at[k], cp_r.at[k], mp=src)
    everything = jnp.concatenate([comp_all[b] for b in range(n_mp)], 0)
    packed[...] = jnp.dot(pick_rows, everything, preferred_element_type=f32).astype(bf16)
    hpad[pad : pad + ROWS] = jnp.dot(packed[...], w_in[...], preferred_element_type=f32).astype(bf16).astype(f32)

    def columns(c):
        return pl.ds(pl.multiple_of(c * 128, 128), 128)

    def conv(values, direction, emit):
        def body(c, carry):
            cs = columns(c)
            weights = taps[:, cs]
            for base in range(0, ROWS, chunk):
                total = jnp.zeros((chunk, 128), f32)
                for j in range(KERNEL):
                    start = pad + base + direction * (j - centre)
                    mask = masks[j if direction == 1 else KERNEL - 1 - j, base : base + chunk]
                    total = total + weights[j : j + 1] * (values[start : start + chunk, cs] * mask)
                emit(base, cs, total)
            return carry

        lax.fori_loop(0, width // 128, body, 0)

    def forward(base, cs, total):
        rows = slice(base, base + chunk)
        gate = 1.0 / (1.0 + jnp.exp(-total))
        act[rows, cs] = (total * gate).astype(bf16)
        gpad[pad + base : pad + base + chunk, cs] = gact[rows, cs] * gate * (1.0 + total * (1.0 - gate))

    conv(hpad, 1, forward)

    def dw_rows(d):
        at = pl.ds(pl.multiple_of(d * block, 64), block)
        return jnp.dot(cot_t[at], act[...], preferred_element_type=f32)

    z_order = [2, 1, 3, 0] if n_z == 4 else list(range(1, n_z)) + [0]
    partner = 2 * zi + 1 - yi
    dy_c, dz_c, pt_c = [], [], []

    def dy_step(kz):
        zt = lax.rem(zi + kz, n_z)
        dy_send[kz] = dw_rows(2 * zt + 1 - yi).astype(bf16)
        c = send(dy_send.at[kz], dy_got.at[kz], dy_s.at[kz], dy_r.at[kz], dp=partner)
        c.start()
        dy_c.append(c)

    def dz_step(kz):
        zt = lax.rem(zi + kz, n_z)
        arrived(dy_got.at[kz], dy_s.at[kz], dy_r.at[kz], dp=partner)
        total = dw_rows(2 * zt + yi) + dy_got[kz].astype(f32)
        if kz:
            dz_send[kz] = total.astype(bf16)
            c = send(dz_send.at[kz], dz_got.at[kz], dz_s.at[kz], dz_r.at[kz], dp=2 * zt + yi)
            c.start()
            dz_c.append(c)
        else:
            dz_own[...] = total

    for kz in z_order[:-2]:
        dy_step(kz)
    for k in [2, 3, 1, 0]:
        at = pl.ds(pl.multiple_of(mp_peer(k) * width, 128), width)
        part[k] = lax.dot_general(
            act[...], w_out[at], (((1,), (1,)), ((), ())), preferred_element_type=f32
        ).astype(bf16)
        if k:
            c = send(part.at[k], part_got.at[k], pt_s.at[k], pt_r.at[k], mp=mp_peer(k))
            c.start()
            pt_c.append(c)

    def backward(c, carry):
        cs = columns(c)
        weights = taps[:, cs]
        for base in range(0, ROWS, chunk):
            rows = slice(base, base + chunk)
            values = hpad[pad + base : pad + base + chunk, cs]
            total = cot_all[mine, rows, cs].astype(f32)
            for j in range(KERNEL):
                start = pad + base - (j - centre)
                taken = gpad[start : start + chunk, cs] * masks[KERNEL - 1 - j, rows]
                total = total + weights[j : j + 1] * taken
                sums = jnp.sum((values * taken).reshape(chunk // 8, 8, 128), axis=0)
                tap_acc[j] = sums if base == 0 else tap_acc[j] + sums
            ghid[rows, cs] = total.astype(bf16)
        for j in range(KERNEL):
            gfull[features + j : features + j + 1, cs] = jnp.sum(tap_acc[j], axis=0, keepdims=True)
        return carry

    tiles = width // 128
    lax.fori_loop(0, tiles - 1, backward, 0)
    dz_step(z_order[0])
    lax.fori_loop(tiles - 1, tiles, backward, 0)
    gfull[0:features] = lax.dot_general(
        packed[...], ghid[...], (((0,), (0,)), ((), ())), preferred_element_type=f32
    )
    for y in range(2):
        for z in range(n_z):
            at = (y * n_z + z) * strip
            gs[y, z] = gfull[at : at + strip].astype(bf16)
    g_c = []

    def push(src, dst, ssem, rsem, peer):
        c = send(src, dst, ssem, rsem, dp=peer)
        c.start()
        g_c.append(c)

    push(gs.at[1 - yi], gy_got, gy_s.at[0], gy_r.at[0], partner)
    for kz in z_order[-2:]:
        dy_step(kz)
    for kz in z_order[1:-2]:
        dz_step(kz)
    arrived(gy_got, gy_s.at[0], gy_r.at[0], dp=partner)
    for kz in z_order:
        zt = lax.rem(zi + kz, n_z)
        at = pl.ds(pl.multiple_of((yi * n_z + zt) * strip, 16), strip)
        total = gfull[at] + gy_got[zt].astype(f32)
        if kz:
            gz_send[kz] = total.astype(bf16)
            push(gz_send.at[kz], gz_got.at[kz], gz_s.at[kz], gz_r.at[kz], 2 * zt + yi)
    dz_step(z_order[-2])
    for kz in range(1, n_z):
        arrived(gz_got.at[kz], gz_s.at[kz], gz_r.at[kz], dp=2 * lax.rem(zi + n_z - kz, n_z) + yi)
        total = total + gz_got[kz].astype(f32)
    gall[yi, zi] = total.astype(bf16)
    for kz in z_order[:-1]:
        zt = lax.rem(zi + kz, n_z)
        push(gall.at[yi, zi], gall.at[yi, zi], ga_s.at[kz], ga_r.at[kz], 2 * zt + yi)
    push(gall.at[yi, zi], gall.at[yi, zi], gb_s.at[0], gb_r.at[0], partner)
    dz_step(0)

    branch = part[0].astype(f32)
    for k in range(1, n_mp):
        arrived(part_got.at[k], pt_s.at[k], pt_r.at[k], mp=mp_from(k))
        branch = branch + part_got[k].astype(f32)
    out_ref[...] = (hpad[pad : pad + ROWS] + branch).astype(out_ref.dtype)
    for kz in range(1, n_z):
        src = lax.rem(zi + n_z - kz, n_z)
        arrived(gall.at[yi, src], ga_s.at[kz], ga_r.at[kz], dp=2 * src + yi)
        push(gall.at[yi, src], gall.at[yi, src], gb_s.at[kz], gb_r.at[kz], partner)
    total = dz_own[...]
    for kz in range(1, n_z):
        src = 2 * lax.rem(zi + n_z - kz, n_z) + yi
        arrived(dz_got.at[kz], dz_s.at[kz], dz_r.at[kz], dp=src)
        total = total + dz_got[kz].astype(f32)
    gout_ref[...] = scale * total
    for kz in range(n_z):
        src = lax.rem(zi + n_z - kz, n_z)
        arrived(gall.at[1 - yi, src], gb_s.at[kz], gb_r.at[kz], dp=partner)
    for y in range(2):
        for z in range(n_z):
            at = (y * n_z + z) * strip
            values = scale * gall[y, z].astype(f32)
            low = min(max(features - at, 0), strip)
            high = min(max(features + KERNEL - at, 0), strip)
            if low > 0:
                gin_ref[at : at + low] = values[:low]
            if high > low:
                gdep_ref[at + low - features : at + high - features] = values[low:high]
    for c in tab_c + fr_c + ct_c + cp_c + dy_c + pt_c + dz_c + g_c:
        c.wait_send()


def store_kernel(*refs):
    count = len(refs) // 2
    copies = [pltpu.make_async_copy(refs[i], refs[count + i], refs[-1].at[i]) for i in range(count)]
    for c in copies:
        c.start()
    for c in copies:
        c.wait()


def fused(frames, lengths, destinations, offsets, in_weight, depth_weight, out_weight, cotangent):
    n_dp, n_mp = lax.axis_size("dp"), lax.axis_size("mp")
    src_rows, features = frames.shape
    entries = lengths.shape[1]
    width = cotangent.shape[1]
    model = out_weight.shape[0]
    block = model // n_dp
    quarter = src_rows // n_dp // n_mp
    sources = ROWS * n_dp // src_rows
    strip = -(-(features + KERNEL) // (16 * n_dp)) * 16
    n_z = n_dp // 2
    f32, bf16 = jnp.float32, jnp.bfloat16
    vm = pltpu.VMEM
    i32 = jnp.int32
    scratch = [
        vm((features, src_rows), bf16),
        vm((1, entries), i32),
        vm((1, entries), i32),
        vm((1, entries), i32),
        vm((features, width), bf16),
        vm((KERNEL, width), bf16),
        vm((model, width), bf16),
        pltpu.SemaphoreType.DMA((8,)),
        vm((n_dp, 8, entries), f32),
        vm((n_dp, quarter, features), bf16),
        vm((n_dp, quarter, features), bf16),
        vm((n_mp, sources * quarter, features), bf16),
        vm((n_mp, ROWS, width), bf16),
        vm((model, ROWS), bf16),
        vm((ROWS, features), bf16),
        vm((ROWS + 32, 128), f32),
        vm((KERNEL, ROWS, 128), f32),
        vm((32, width), f32),
        vm((ROWS + 32, width), f32),
        vm((ROWS, width), bf16),
        vm((ROWS, width), f32),
        vm((ROWS + 32, width), f32),
        vm((ROWS, width), bf16),
        vm((n_mp, ROWS, width), bf16),
        vm((n_mp, ROWS, width), bf16),
        vm((n_z, block, width), bf16),
        vm((n_z, block, width), bf16),
        vm((n_z, block, width), bf16),
        vm((n_z, block, width), bf16),
        vm((block, width), f32),
        vm((n_dp * strip, width), f32),
        vm((KERNEL, 8, 128), f32),
        vm((2, n_z, strip, width), bf16),
        vm((n_z, strip, width), bf16),
        vm((n_z, strip, width), bf16),
        vm((n_z, strip, width), bf16),
        vm((2, n_z, strip, width), bf16),
    ]
    for count in (n_dp, n_dp, n_mp, n_mp, n_mp, n_z, n_z, 1, n_z, n_z, n_z):
        scratch += [pltpu.SemaphoreType.DMA((count,)), pltpu.SemaphoreType.DMA((count,))]
    whole = pl.BlockSpec(memory_space=pltpu.VMEM)
    remote = pl.BlockSpec(memory_space=pltpu.HBM)
    results = pl.pallas_call(
        functools.partial(fused_kernel, n_dp, n_mp, 1.0 / math.sqrt(n_dp * ROWS)),
        out_shape=(
            jax.ShapeDtypeStruct((ROWS, width), bf16),
            jax.ShapeDtypeStruct((features, width), f32),
            jax.ShapeDtypeStruct((KERNEL, width), f32),
            jax.ShapeDtypeStruct((block, width), f32),
        ),
        in_specs=[remote] * 8,
        out_specs=(whole,) * 4,
        scratch_shapes=scratch,
        compiler_params=pltpu.CompilerParams(
            collective_id=0, has_side_effects=True, vmem_limit_bytes=48 * 1024 * 1024
        ),
    )(frames.T, lengths, destinations, offsets, in_weight, depth_weight, out_weight, cotangent)
    return pl.pallas_call(
        store_kernel,
        out_shape=tuple(jax.ShapeDtypeStruct(r.shape, r.dtype) for r in results),
        in_specs=[whole] * 4,
        out_specs=(remote,) * 4,
        scratch_shapes=[pltpu.SemaphoreType.DMA((4,))],
    )(*results)


def solution(mesh):
    small = mesh.shape["dp"] == 8 and mesh.shape["mp"] == 4
    placed = (
        P("dp", None),
        P("dp", None),
        P("dp", None),
        P("dp", None),
        P(None, "mp"),
        P(None, "mp"),
        P(None, "mp"),
        P("dp", "mp"),
    )
    return jax.shard_map(
        fused if small else per_device,
        mesh=mesh,
        in_specs=placed,
        out_specs=(P("dp", "mp"), P(None, "mp"), P(None, "mp"), P("dp", "mp")),
        check_vma=False,
    )
```

```python
import functools
import math

import jax
import jax.numpy as jnp
from jax import lax
from jax.experimental import pallas as pl
from jax.experimental.pallas import tpu as pltpu
from jax.sharding import PartitionSpec as P

KERNEL = 31
ROWS = 256
MESH = pl.DeviceIdType.MESH


def depth_conv(values, weights, labels, direction):
    center = (KERNEL - 1) // 2
    length = values.shape[0]
    padded = jnp.pad(values, ((center, center), (0, 0)))
    padded_labels = jnp.pad(labels, (center, center), constant_values=-1)
    result = jnp.zeros(values.shape, jnp.float32)
    for tap_index in range(KERNEL):
        start = center + direction * (tap_index - center)
        matches = (padded_labels[start : start + length] == labels)[:, None]
        taken = weights[tap_index][None, :] * padded[start : start + length]
        result = result + jnp.where(matches, taken, jnp.zeros_like(taken))
    return result


def tap_sums(grads, values, labels):
    center = (KERNEL - 1) // 2
    length = values.shape[0]
    padded = jnp.pad(values, ((center, center), (0, 0)))
    padded_labels = jnp.pad(labels, (center, center), constant_values=-1)
    rows_list = []
    for tap_index in range(KERNEL):
        matches = (padded_labels[tap_index : tap_index + length] == labels)[:, None]
        taken = grads * padded[tap_index : tap_index + length]
        rows_list.append(jnp.sum(jnp.where(matches, taken, jnp.zeros_like(taken)), axis=0))
    return jnp.stack(rows_list, 0)


def per_device(
    frames, lengths, destinations, offsets, in_weight, depth_weight, out_weight, cotangent
):
    dp_count = lax.axis_size("dp")
    src_rows = frames.shape[0]
    features = frames.shape[1]
    slot_rows = src_rows // dp_count
    entries = lengths.shape[1]
    lengths_row = lengths[0]
    end_rows = jnp.cumsum(lengths_row, dtype=jnp.int32)
    begins = end_rows - lengths_row
    row_ids = jnp.arange(src_rows, dtype=jnp.int32)
    owner_table = (begins[None, :] <= row_ids[:, None]) & (row_ids[:, None] < end_rows[None, :])
    occupied_rows = jnp.any(owner_table, axis=1)
    onehot = owner_table.astype(jnp.int32)

    def lookup(table):
        return jnp.sum(onehot * table[None, :], axis=1, dtype=jnp.int32)

    owner_index = lookup(jnp.arange(entries, dtype=jnp.int32))
    target = lookup(offsets[0]) + row_ids - lookup(begins)
    dest_row = lookup(destinations[0])
    source = lax.axis_index("dp")
    row_label = source * entries + owner_index
    dump_index = dp_count * slot_rows
    slot_index = jnp.where(occupied_rows, dest_row * slot_rows + row_ids % slot_rows, dump_index)
    send_frames = (
        jnp.zeros((dump_index + 1, features), frames.dtype)
        .at[slot_index]
        .set(frames)[:dump_index]
        .reshape(dp_count, slot_rows, features)
    )
    send_target = (
        jnp.full((dump_index + 1,), ROWS, jnp.int32)
        .at[slot_index]
        .set(target)[:dump_index]
        .reshape(dp_count, slot_rows)
    )
    send_label = (
        jnp.full((dump_index + 1,), -1, jnp.int32)
        .at[slot_index]
        .set(row_label)[:dump_index]
        .reshape(dp_count, slot_rows)
    )
    got_frames, got_target, got_label = (
        lax.all_to_all(send_frames, "dp", split_axis=0, concat_axis=0, tiled=True),
        lax.all_to_all(send_target, "dp", split_axis=0, concat_axis=0, tiled=True),
        lax.all_to_all(send_label, "dp", split_axis=0, concat_axis=0, tiled=True),
    )
    flat_target = got_target.reshape(-1)
    packed = (
        jnp.zeros((ROWS + 1, features), frames.dtype)
        .at[flat_target]
        .set(got_frames.reshape(-1, features))[:ROWS]
    )
    packed_labels = (
        jnp.full((ROWS + 1,), -1, jnp.int32).at[flat_target].set(got_label.reshape(-1))[:ROWS]
    )
    hidden = jnp.dot(packed, in_weight, preferred_element_type=jnp.float32).astype(jnp.bfloat16)
    hidden_wide = hidden.astype(jnp.float32)
    taps = depth_weight.astype(jnp.float32)
    convolved = depth_conv(hidden_wide, taps, packed_labels, 1)
    activated = jax.nn.silu(convolved).astype(jnp.bfloat16)
    partial_sum = lax.dot_general(
        activated, out_weight, (((1,), (1,)), ((), ())), preferred_element_type=jnp.float32
    )
    branch = lax.psum_scatter(
        partial_sum.astype(jnp.bfloat16), "mp", scatter_dimension=1, tiled=True
    ).astype(jnp.float32)
    output = (hidden_wide + branch).astype(jnp.bfloat16)
    cotangent_full = lax.all_gather(cotangent, "mp", axis=1, tiled=True)
    grad_scale = 1.0 / math.sqrt(dp_count * ROWS)
    grad_activated = jnp.dot(cotangent_full, out_weight, preferred_element_type=jnp.float32)
    sigmoid_value = jax.nn.sigmoid(convolved)
    grad_convolved = grad_activated * sigmoid_value * (1.0 + convolved * (1.0 - sigmoid_value))
    grad_hidden = (
        cotangent.astype(jnp.float32) + depth_conv(grad_convolved, taps, packed_labels, -1)
    ).astype(jnp.bfloat16)
    out_weight_gradient = lax.psum_scatter(
        grad_scale
        * lax.dot_general(
            cotangent_full, activated, (((0,), (0,)), ((), ())), preferred_element_type=jnp.float32
        ),
        "dp",
        scatter_dimension=0,
        tiled=True,
    )
    term_in = grad_scale * lax.dot_general(
        packed, grad_hidden, (((0,), (0,)), ((), ())), preferred_element_type=jnp.float32
    )
    term_depth = grad_scale * tap_sums(grad_convolved, hidden_wide, packed_labels)
    in_weight_gradient, depth_gradient = lax.psum((term_in, term_depth), "dp")
    return (output, in_weight_gradient, depth_gradient, out_weight_gradient)


def fused_kernel(
    n_dp, n_mp, scale,
    frames_in, lens_in, dests_in, offs_in, w_in_in, w_depth_in, w_out_in, cot_in,
    out_ref, gin_ref, gdep_ref, gout_ref,
    frames, lens, dests, offs, w_in, w_depth, w_out, in_sem,
    tables, slots, got, comp_all, cot_all, cot_t, packed, lab_pad, masks, taps, hpad, act, gact, gpad, ghid,
    part, part_got, dy_send, dy_got, dz_send, dz_got, dz_own, gfull, tap_acc, gs, gy_got, gz_send, gz_got, gall,
    tab_s, tab_r, fr_s, fr_r, cp_s, cp_r, ct_s, ct_r, pt_s, pt_r, dy_s, dy_r, dz_s, dz_r, gy_s, gy_r, gz_s, gz_r, ga_s, ga_r, gb_s, gb_r,
):
    f32, bf16 = jnp.float32, jnp.bfloat16
    me = lax.axis_index("dp")
    mine = lax.axis_index("mp")
    features, src_rows = frames.shape
    slot_rows = src_rows // n_dp
    quarter = slot_rows // n_mp
    sources = ROWS // slot_rows
    width = cot_all.shape[2]
    entries = lens.shape[1]
    block = gout_ref.shape[0]
    strip = gs.shape[2]
    centre = (KERNEL - 1) // 2
    pad = 16
    n_z = n_dp // 2
    zi, yi = me // 2, lax.rem(me, 2)
    chunk = 64

    def dp_peer(k):
        return lax.rem(me + k, n_dp)

    def dp_from(k):
        return lax.rem(me + n_dp - k, n_dp)

    def mp_peer(k):
        return lax.rem(mine + k, n_mp)

    def mp_from(k):
        return lax.rem(mine + n_mp - k, n_mp)

    def send(src, dst, ssem, rsem, **where):
        return pltpu.make_async_remote_copy(
            src_ref=src, dst_ref=dst, send_sem=ssem, recv_sem=rsem, device_id=where, device_id_type=MESH
        )

    tiles = width // 128
    loads = [
        pltpu.make_async_copy(src, dst, in_sem.at[i])
        for i, (src, dst) in enumerate(
            [(lens_in, lens), (dests_in, dests), (offs_in, offs), (frames_in, frames), (cot_in, cot_all.at[mine]),
             (w_depth_in, w_depth), (w_in_in, w_in), (w_out_in, w_out)]
        )
    ]
    for load in loads:
        load.start()
    barrier = pltpu.get_barrier_semaphore()
    for k in range(1, n_dp):
        pl.semaphore_signal(barrier, inc=1, device_id={"dp": dp_peer(k)}, device_id_type=MESH)
    for k in range(1, n_mp):
        pl.semaphore_signal(barrier, inc=1, device_id={"mp": mp_peer(k)}, device_id_type=MESH)

    for load in loads[:3]:
        load.wait()
    len_f = lens[...].astype(f32)
    dest_f = dests[...].astype(f32)
    off_f = offs[...].astype(f32)
    before = (
        lax.broadcasted_iota(jnp.int32, (entries, entries), 0) < lax.broadcasted_iota(jnp.int32, (entries, entries), 1)
    )
    begin_f = jnp.dot(
        jnp.broadcast_to(len_f, (8, entries)).astype(bf16), jnp.where(before, 1.0, 0.0).astype(bf16),
        preferred_element_type=f32,
    )[0:1]
    tables[me] = jnp.concatenate([len_f, dest_f, off_f, begin_f, jnp.zeros((4, entries), f32)], 0)
    row = lax.broadcasted_iota(jnp.int32, (n_dp * quarter, 1), 0)
    row_dest = (row // quarter).astype(f32)
    row_in = lax.rem(row, quarter).astype(f32)
    first = jnp.min(jnp.where((dest_f == row_dest) & (len_f > 0.0), begin_f, 1e6), axis=1, keepdims=True)
    wanted = first + row_in + (mine * quarter).astype(f32)
    cols = lax.broadcasted_iota(jnp.int32, (n_dp * quarter, src_rows), 1).astype(f32)
    pick = jnp.where(cols == wanted, 1.0, 0.0).astype(bf16)
    loads[3].wait()
    chosen = lax.dot_general(
        pick, frames[...], (((1,), (1,)), ((), ())), preferred_element_type=f32
    ).astype(bf16)
    for d in range(n_dp):
        slots[d] = chosen[d * quarter : (d + 1) * quarter]
    got[me] = slots[me]

    pl.semaphore_wait(barrier, n_dp - 1 + n_mp - 1)
    tab_c, fr_c, ct_c = [], [], []
    for k in range(1, n_dp):
        c = send(tables.at[me], tables.at[me], tab_s.at[k], tab_r.at[k], dp=dp_peer(k))
        c.start()
        tab_c.append(c)
    for k in range(1, n_dp):
        c = send(slots.at[dp_peer(k)], got.at[me], fr_s.at[k], fr_r.at[k], dp=dp_peer(k))
        c.start()
        fr_c.append(c)
    sibling = mine + 1 - 2 * lax.rem(mine, 2)
    across = lax.rem(mine + 2, n_mp)
    for k, peer in ((0, across), (1, sibling)):
        c = send(cot_in, cot_all.at[mine], ct_s.at[k], ct_r.at[k], mp=peer)
        c.start()
        ct_c.append(c)
    for load in loads[4:]:
        load.wait()

    taps[0:KERNEL] = w_depth[...].astype(f32)
    for ref in (hpad, gpad):
        ref[:, 0:pad] = jnp.zeros((tiles, pad, 128), f32)
        ref[:, pad + ROWS :] = jnp.zeros((tiles, pad, 128), f32)
    gfull[...] = jnp.zeros_like(gfull)

    def arrived(dst, ssem, rsem, **where):
        send(dst, dst, ssem, rsem, **where).wait_recv()

    for k in range(1, n_dp):
        src = dp_from(k)
        arrived(tables.at[src], tab_s.at[k], tab_r.at[k], dp=src)

    here = me.astype(f32)
    t_row = lax.broadcasted_iota(jnp.int32, (ROWS, 1), 0).astype(f32)
    lane = lax.broadcasted_iota(jnp.int32, (1, entries), 1).astype(f32)
    shift = jnp.zeros((ROWS, entries), f32)
    order = jnp.zeros((ROWS, entries), f32)
    label = jnp.zeros((ROWS, entries), f32)
    rank = jnp.zeros((1, 1), f32)
    selectors = []
    for s in range(n_dp):
        table = tables[s]
        t_len, t_dest, t_off, t_begin = table[0:1], table[1:2], table[2:3], table[3:4]
        to_me = (t_dest == here) & (t_len > 0.0)
        valid = jnp.max(jnp.where(to_me, 1.0, 0.0), axis=1, keepdims=True)
        match = to_me & (t_off <= t_row) & (t_row < t_off + t_len)
        inside = t_begin - slot_rows * jnp.floor(t_begin / slot_rows)
        shift = shift + jnp.where(match, inside - t_off, 0.0)
        order = order + jnp.where(match, rank, 0.0)
        label = label + jnp.where(match, s * entries + lane, 0.0)
        selectors.append([jnp.where((valid > 0.0) & (rank == r), 1.0, 0.0) for r in range(sources)])
        rank = rank + valid
    q = jnp.sum(shift, axis=1, keepdims=True) + t_row
    rank_of = jnp.sum(order, axis=1, keepdims=True)
    q_part = jnp.floor(q / quarter)
    place = q_part * (sources * quarter) + rank_of * quarter + (q - q_part * quarter)
    spots = lax.broadcasted_iota(jnp.int32, (ROWS, ROWS), 1).astype(f32)
    pick_rows = jnp.where(spots == place, 1.0, 0.0).astype(bf16)
    lab_pad[0:pad] = jnp.full((pad, 128), -1.0, f32)
    lab_pad[pad + ROWS :] = jnp.full((pad, 128), -1.0, f32)
    lab_pad[pad : pad + ROWS] = jnp.broadcast_to(jnp.sum(label, axis=1, keepdims=True), (ROWS, 128))
    for j in range(KERNEL):
        start = pad + j - centre
        masks[j] = jnp.where(lab_pad[start : start + ROWS] == lab_pad[pad : pad + ROWS], 1.0, 0.0)

    for k in range(1, n_dp):
        src = dp_from(k)
        arrived(got.at[src], fr_s.at[k], fr_r.at[k], dp=src)
    picked = [jnp.zeros((quarter, features), f32) for _ in range(sources)]
    for s in range(n_dp):
        rows_s = got[s].astype(f32)
        for r in range(sources):
            picked[r] = picked[r] + selectors[s][r] * rows_s
    comp_all[mine] = jnp.concatenate(picked, 0).astype(bf16)
    cp_c = []
    for k in range(1, n_mp):
        c = send(comp_all.at[mine], comp_all.at[mine], cp_s.at[k], cp_r.at[k], mp=mp_peer(k))
        c.start()
        cp_c.append(c)

    arrived(cot_all.at[across], ct_s.at[0], ct_r.at[0], mp=across)
    c = send(cot_all.at[across], cot_all.at[across], ct_s.at[2], ct_r.at[2], mp=sibling)
    c.start()
    ct_c.append(c)

    def use_cotangent(b, start):
        at = pl.ds(pl.multiple_of(b * width, 128), width)
        values = cot_all[b]
        cot_t[at] = values.T
        term = jnp.dot(values, w_out[at], preferred_element_type=f32)
        gact[...] = term if start else gact[...] + term

    use_cotangent(mine, True)
    use_cotangent(across, False)
    arrived(cot_all.at[sibling], ct_s.at[1], ct_r.at[1], mp=sibling)
    use_cotangent(sibling, False)
    diagonal = lax.rem(sibling + 2, n_mp)
    arrived(cot_all.at[diagonal], ct_s.at[2], ct_r.at[2], mp=sibling)
    use_cotangent(diagonal, False)

    for k in range(1, n_mp):
        src = mp_from(k)
        arrived(comp_all.at[src], cp_s.at[k], cp_r.at[k], mp=src)
    everything = jnp.concatenate([comp_all[b] for b in range(n_mp)], 0)
    packed[...] = jnp.dot(pick_rows, everything, preferred_element_type=f32).astype(bf16)
    hidden = jnp.dot(packed[...], w_in[...], preferred_element_type=f32).astype(bf16).astype(f32)
    for c in range(tiles):
        hpad[c, pad : pad + ROWS] = hidden[:, c * 128 : (c + 1) * 128]

    def columns(c):
        return pl.ds(pl.multiple_of(c * 128, 128), 128)

    partner = 2 * zi + 1 - yi
    dz_c, pt_c = [], []

    z_order = [2, 1, 3, 0]

    def dw_tile(d, c):
        at = pl.ds(pl.multiple_of(d * block, 64), block)
        return jnp.dot(cot_t[at], act[:, columns(c)], preferred_element_type=f32)

    def dy_tile(kz, c):
        return send(dy_send.at[kz, c], dy_got.at[kz, c], dy_s.at[kz, c], dy_r.at[kz, c], dp=partner)

    def dy_step(kz, c):
        dy_send[kz, c] = dw_tile(2 * lax.rem(zi + kz, n_z) + 1 - yi, c).astype(bf16)
        dy_tile(kz, c).start()

    def dz_step(kz):
        zt = lax.rem(zi + kz, n_z)
        for c in range(tiles):
            dy_tile(kz, c).wait_recv()
            total = dw_tile(2 * zt + yi, c) + dy_got[kz, c].astype(f32)
            if kz:
                dz_send[kz, c] = total.astype(bf16)
            else:
                dz_own[c] = total
        if kz:
            c = send(dz_send.at[kz], dz_got.at[kz], dz_s.at[kz], dz_r.at[kz], dp=2 * zt + yi)
            c.start()
            dz_c.append(c)

    def forward(c, carry):
        cs = columns(c)
        weights = taps[:, cs]
        for base in range(0, ROWS, chunk):
            rows = slice(base, base + chunk)
            total = jnp.zeros((chunk, 128), f32)
            for j in range(KERNEL):
                start = pad + base + j - centre
                total = total + weights[j : j + 1] * (hpad[c, start : start + chunk] * masks[j, rows])
            gate = 1.0 / (1.0 + jnp.exp(-total))
            act[rows, cs] = (total * gate).astype(bf16)
            gpad[c, pad + base : pad + base + chunk] = gact[rows, cs] * gate * (1.0 + total * (1.0 - gate))
        for kz in z_order[:-2]:
            dy_step(kz, c)
        return carry

    lax.fori_loop(0, tiles, forward, 0)
    for k in [2, 3, 1, 0]:
        at = pl.ds(pl.multiple_of(mp_peer(k) * width, 128), width)
        part[k] = lax.dot_general(
            act[...], w_out[at], (((1,), (1,)), ((), ())), preferred_element_type=f32
        ).astype(bf16)
        if k:
            c = send(part.at[k], part_got.at[k], pt_s.at[k], pt_r.at[k], mp=mp_peer(k))
            c.start()
            pt_c.append(c)

    def backward(c, carry):
        cs = columns(c)
        weights = taps[:, cs]
        for base in range(0, ROWS, chunk):
            rows = slice(base, base + chunk)
            values = hpad[c, pad + base : pad + base + chunk]
            total = cot_all[mine, rows, cs].astype(f32)
            for j in range(KERNEL):
                start = pad + base - (j - centre)
                taken = gpad[c, start : start + chunk] * masks[KERNEL - 1 - j, rows]
                total = total + weights[j : j + 1] * taken
                sums = jnp.sum((values * taken).reshape(chunk // 8, 8, 128), axis=0)
                tap_acc[j] = sums if base == 0 else tap_acc[j] + sums
            ghid[rows, cs] = total.astype(bf16)
        for j in range(KERNEL):
            gfull[features + j : features + j + 1, cs] = jnp.sum(tap_acc[j], axis=0, keepdims=True)
        return carry

    lax.fori_loop(0, tiles - 1, backward, 0)
    dz_step(z_order[0])
    lax.fori_loop(tiles - 1, tiles, backward, 0)
    gfull[0:features] = lax.dot_general(
        packed[...], ghid[...], (((0,), (0,)), ((), ())), preferred_element_type=f32
    )
    for y in range(2):
        for z in range(n_z):
            at = (y * n_z + z) * strip
            gs[y, z] = gfull[at : at + strip].astype(bf16)
    g_c = []

    def push(src, dst, ssem, rsem, peer):
        c = send(src, dst, ssem, rsem, dp=peer)
        c.start()
        g_c.append(c)

    push(gs.at[1 - yi], gy_got, gy_s.at[0], gy_r.at[0], partner)
    for kz in z_order[-2:]:
        for c in range(tiles):
            dy_step(kz, c)
    for kz in z_order[1:-2]:
        dz_step(kz)
    arrived(gy_got, gy_s.at[0], gy_r.at[0], dp=partner)
    for kz in z_order:
        zt = lax.rem(zi + kz, n_z)
        at = pl.ds(pl.multiple_of((yi * n_z + zt) * strip, 16), strip)
        total = gfull[at] + gy_got[zt].astype(f32)
        if kz:
            gz_send[kz] = total.astype(bf16)
            push(gz_send.at[kz], gz_got.at[kz], gz_s.at[kz], gz_r.at[kz], 2 * zt + yi)
    dz_step(z_order[-2])
    for kz in range(1, n_z):
        arrived(gz_got.at[kz], gz_s.at[kz], gz_r.at[kz], dp=2 * lax.rem(zi + n_z - kz, n_z) + yi)
        total = total + gz_got[kz].astype(f32)
    gall[yi, zi] = total.astype(bf16)
    for kz in z_order[:-1]:
        zt = lax.rem(zi + kz, n_z)
        push(gall.at[yi, zi], gall.at[yi, zi], ga_s.at[kz], ga_r.at[kz], 2 * zt + yi)
    push(gall.at[yi, zi], gall.at[yi, zi], gb_s.at[0], gb_r.at[0], partner)
    dz_step(0)

    branch = part[0].astype(f32)
    for k in range(1, n_mp):
        arrived(part_got.at[k], pt_s.at[k], pt_r.at[k], mp=mp_from(k))
        branch = branch + part_got[k].astype(f32)
    for c in range(tiles):
        part_c = branch[:, c * 128 : (c + 1) * 128]
        out_ref[:, c * 128 : (c + 1) * 128] = (hpad[c, pad : pad + ROWS] + part_c).astype(out_ref.dtype)
    for kz in range(1, n_z):
        src = lax.rem(zi + n_z - kz, n_z)
        arrived(gall.at[yi, src], ga_s.at[kz], ga_r.at[kz], dp=2 * src + yi)
        push(gall.at[yi, src], gall.at[yi, src], gb_s.at[kz], gb_r.at[kz], partner)
    total = dz_own[...]
    for kz in range(1, n_z):
        src = 2 * lax.rem(zi + n_z - kz, n_z) + yi
        arrived(dz_got.at[kz], dz_s.at[kz], dz_r.at[kz], dp=src)
        total = total + dz_got[kz].astype(f32)
    for c in range(tiles):
        gout_ref[:, c * 128 : (c + 1) * 128] = scale * total[c]
    for kz in range(n_z):
        src = lax.rem(zi + n_z - kz, n_z)
        arrived(gall.at[1 - yi, src], gb_s.at[kz], gb_r.at[kz], dp=partner)
    for y in range(2):
        for z in range(n_z):
            at = (y * n_z + z) * strip
            values = scale * gall[y, z].astype(f32)
            low = min(max(features - at, 0), strip)
            high = min(max(features + KERNEL - at, 0), strip)
            if low > 0:
                gin_ref[at : at + low] = values[:low]
            if high > low:
                gdep_ref[at + low - features : at + high - features] = values[low:high]
    for kz in range(n_z):
        for c in range(tiles):
            dy_tile(kz, c).wait_send()
    for c in tab_c + fr_c + ct_c + cp_c + pt_c + dz_c + g_c:
        c.wait_send()


def store_kernel(*refs):
    count = len(refs) // 2
    copies = [pltpu.make_async_copy(refs[i], refs[count + i], refs[-1].at[i]) for i in range(count)]
    for c in copies:
        c.start()
    for c in copies:
        c.wait()


def fused(frames, lengths, destinations, offsets, in_weight, depth_weight, out_weight, cotangent):
    n_dp, n_mp = lax.axis_size("dp"), lax.axis_size("mp")
    src_rows, features = frames.shape
    entries = lengths.shape[1]
    width = cotangent.shape[1]
    model = out_weight.shape[0]
    block = model // n_dp
    quarter = src_rows // n_dp // n_mp
    sources = ROWS * n_dp // src_rows
    strip = -(-(features + KERNEL) // (16 * n_dp)) * 16
    n_z = n_dp // 2
    f32, bf16 = jnp.float32, jnp.bfloat16
    vm = pltpu.VMEM
    i32 = jnp.int32
    tiles = width // 128
    scratch = [
        vm((features, src_rows), bf16),
        vm((1, entries), i32),
        vm((1, entries), i32),
        vm((1, entries), i32),
        vm((features, width), bf16),
        vm((KERNEL, width), bf16),
        vm((model, width), bf16),
        pltpu.SemaphoreType.DMA((8,)),
        vm((n_dp, 8, entries), f32),
        vm((n_dp, quarter, features), bf16),
        vm((n_dp, quarter, features), bf16),
        vm((n_mp, sources * quarter, features), bf16),
        vm((n_mp, ROWS, width), bf16),
        vm((model, ROWS), bf16),
        vm((ROWS, features), bf16),
        vm((ROWS + 32, 128), f32),
        vm((KERNEL, ROWS, 128), f32),
        vm((32, width), f32),
        vm((tiles, ROWS + 32, 128), f32),
        vm((ROWS, width), bf16),
        vm((ROWS, width), f32),
        vm((tiles, ROWS + 32, 128), f32),
        vm((ROWS, width), bf16),
        vm((n_mp, ROWS, width), bf16),
        vm((n_mp, ROWS, width), bf16),
        vm((n_z, tiles, block, 128), bf16),
        vm((n_z, tiles, block, 128), bf16),
        vm((n_z, tiles, block, 128), bf16),
        vm((n_z, tiles, block, 128), bf16),
        vm((tiles, block, 128), f32),
        vm((n_dp * strip, width), f32),
        vm((KERNEL, 8, 128), f32),
        vm((2, n_z, strip, width), bf16),
        vm((n_z, strip, width), bf16),
        vm((n_z, strip, width), bf16),
        vm((n_z, strip, width), bf16),
        vm((2, n_z, strip, width), bf16),
    ]
    for shape in ((n_dp,), (n_dp,), (n_mp,), (n_mp,), (n_mp,), (n_z, tiles), (n_z,), (1,), (n_z,), (n_z,), (n_z,)):
        scratch += [pltpu.SemaphoreType.DMA(shape), pltpu.SemaphoreType.DMA(shape)]
    whole = pl.BlockSpec(memory_space=pltpu.VMEM)
    remote = pl.BlockSpec(memory_space=pl.ANY)
    results = pl.pallas_call(
        functools.partial(fused_kernel, n_dp, n_mp, 1.0 / math.sqrt(n_dp * ROWS)),
        out_shape=(
            jax.ShapeDtypeStruct((ROWS, width), bf16),
            jax.ShapeDtypeStruct((features, width), f32),
            jax.ShapeDtypeStruct((KERNEL, width), f32),
            jax.ShapeDtypeStruct((block, width), f32),
        ),
        in_specs=[remote] * 8,
        out_specs=(whole,) * 4,
        scratch_shapes=scratch,
        compiler_params=pltpu.CompilerParams(
            collective_id=0, has_side_effects=True, vmem_limit_bytes=62 * 1024 * 1024
        ),
    )(frames.T, lengths, destinations, offsets, in_weight, depth_weight, out_weight, cotangent)
    return pl.pallas_call(
        store_kernel,
        out_shape=tuple(jax.ShapeDtypeStruct(r.shape, r.dtype) for r in results),
        in_specs=[remote] * 4,
        out_specs=(remote,) * 4,
        scratch_shapes=[pltpu.SemaphoreType.DMA((4,))],
        compiler_params=pltpu.CompilerParams(vmem_limit_bytes=62 * 1024 * 1024),
    )(*results)


def solution(mesh):
    small = mesh.shape["dp"] == 8 and mesh.shape["mp"] == 4
    placed = (
        P("dp", None),
        P("dp", None),
        P("dp", None),
        P("dp", None),
        P(None, "mp"),
        P(None, "mp"),
        P(None, "mp"),
        P("dp", "mp"),
    )
    return jax.shard_map(
        fused if small else per_device,
        mesh=mesh,
        in_specs=placed,
        out_specs=(P("dp", "mp"), P(None, "mp"), P(None, "mp"), P("dp", "mp")),
        check_vma=False,
    )
```

```python
import functools
import math

import jax
import jax.numpy as jnp
from jax import lax
from jax.experimental import pallas as pl
from jax.experimental.pallas import tpu as pltpu
from jax.sharding import PartitionSpec as P

KERNEL = 31
ROWS = 256
MESH = pl.DeviceIdType.MESH


def depth_conv(values, weights, labels, direction):
    center = (KERNEL - 1) // 2
    length = values.shape[0]
    padded = jnp.pad(values, ((center, center), (0, 0)))
    padded_labels = jnp.pad(labels, (center, center), constant_values=-1)
    result = jnp.zeros(values.shape, jnp.float32)
    for tap_index in range(KERNEL):
        start = center + direction * (tap_index - center)
        matches = (padded_labels[start : start + length] == labels)[:, None]
        taken = weights[tap_index][None, :] * padded[start : start + length]
        result = result + jnp.where(matches, taken, jnp.zeros_like(taken))
    return result


def tap_sums(grads, values, labels):
    center = (KERNEL - 1) // 2
    length = values.shape[0]
    padded = jnp.pad(values, ((center, center), (0, 0)))
    padded_labels = jnp.pad(labels, (center, center), constant_values=-1)
    rows_list = []
    for tap_index in range(KERNEL):
        matches = (padded_labels[tap_index : tap_index + length] == labels)[:, None]
        taken = grads * padded[tap_index : tap_index + length]
        rows_list.append(jnp.sum(jnp.where(matches, taken, jnp.zeros_like(taken)), axis=0))
    return jnp.stack(rows_list, 0)


def per_device(
    frames, lengths, destinations, offsets, in_weight, depth_weight, out_weight, cotangent
):
    dp_count = lax.axis_size("dp")
    src_rows = frames.shape[0]
    features = frames.shape[1]
    slot_rows = src_rows // dp_count
    entries = lengths.shape[1]
    lengths_row = lengths[0]
    end_rows = jnp.cumsum(lengths_row, dtype=jnp.int32)
    begins = end_rows - lengths_row
    row_ids = jnp.arange(src_rows, dtype=jnp.int32)
    owner_table = (begins[None, :] <= row_ids[:, None]) & (row_ids[:, None] < end_rows[None, :])
    occupied_rows = jnp.any(owner_table, axis=1)
    onehot = owner_table.astype(jnp.int32)

    def lookup(table):
        return jnp.sum(onehot * table[None, :], axis=1, dtype=jnp.int32)

    owner_index = lookup(jnp.arange(entries, dtype=jnp.int32))
    target = lookup(offsets[0]) + row_ids - lookup(begins)
    dest_row = lookup(destinations[0])
    source = lax.axis_index("dp")
    row_label = source * entries + owner_index
    dump_index = dp_count * slot_rows
    slot_index = jnp.where(occupied_rows, dest_row * slot_rows + row_ids % slot_rows, dump_index)
    send_frames = (
        jnp.zeros((dump_index + 1, features), frames.dtype)
        .at[slot_index]
        .set(frames)[:dump_index]
        .reshape(dp_count, slot_rows, features)
    )
    send_target = (
        jnp.full((dump_index + 1,), ROWS, jnp.int32)
        .at[slot_index]
        .set(target)[:dump_index]
        .reshape(dp_count, slot_rows)
    )
    send_label = (
        jnp.full((dump_index + 1,), -1, jnp.int32)
        .at[slot_index]
        .set(row_label)[:dump_index]
        .reshape(dp_count, slot_rows)
    )
    got_frames, got_target, got_label = (
        lax.all_to_all(send_frames, "dp", split_axis=0, concat_axis=0, tiled=True),
        lax.all_to_all(send_target, "dp", split_axis=0, concat_axis=0, tiled=True),
        lax.all_to_all(send_label, "dp", split_axis=0, concat_axis=0, tiled=True),
    )
    flat_target = got_target.reshape(-1)
    packed = (
        jnp.zeros((ROWS + 1, features), frames.dtype)
        .at[flat_target]
        .set(got_frames.reshape(-1, features))[:ROWS]
    )
    packed_labels = (
        jnp.full((ROWS + 1,), -1, jnp.int32).at[flat_target].set(got_label.reshape(-1))[:ROWS]
    )
    hidden = jnp.dot(packed, in_weight, preferred_element_type=jnp.float32).astype(jnp.bfloat16)
    hidden_wide = hidden.astype(jnp.float32)
    taps = depth_weight.astype(jnp.float32)
    convolved = depth_conv(hidden_wide, taps, packed_labels, 1)
    activated = jax.nn.silu(convolved).astype(jnp.bfloat16)
    partial_sum = lax.dot_general(
        activated, out_weight, (((1,), (1,)), ((), ())), preferred_element_type=jnp.float32
    )
    branch = lax.psum_scatter(
        partial_sum.astype(jnp.bfloat16), "mp", scatter_dimension=1, tiled=True
    ).astype(jnp.float32)
    output = (hidden_wide + branch).astype(jnp.bfloat16)
    cotangent_full = lax.all_gather(cotangent, "mp", axis=1, tiled=True)
    grad_scale = 1.0 / math.sqrt(dp_count * ROWS)
    grad_activated = jnp.dot(cotangent_full, out_weight, preferred_element_type=jnp.float32)
    sigmoid_value = jax.nn.sigmoid(convolved)
    grad_convolved = grad_activated * sigmoid_value * (1.0 + convolved * (1.0 - sigmoid_value))
    grad_hidden = (
        cotangent.astype(jnp.float32) + depth_conv(grad_convolved, taps, packed_labels, -1)
    ).astype(jnp.bfloat16)
    out_weight_gradient = lax.psum_scatter(
        grad_scale
        * lax.dot_general(
            cotangent_full, activated, (((0,), (0,)), ((), ())), preferred_element_type=jnp.float32
        ),
        "dp",
        scatter_dimension=0,
        tiled=True,
    )
    term_in = grad_scale * lax.dot_general(
        packed, grad_hidden, (((0,), (0,)), ((), ())), preferred_element_type=jnp.float32
    )
    term_depth = grad_scale * tap_sums(grad_convolved, hidden_wide, packed_labels)
    in_weight_gradient, depth_gradient = lax.psum((term_in, term_depth), "dp")
    return (output, in_weight_gradient, depth_gradient, out_weight_gradient)


def fused_kernel(
    n_dp, n_mp, scale,
    frames_in, lens_in, dests_in, offs_in, w_in_in, w_depth_in, w_out_in, cot_in,
    out_ref, gin_ref, gdep_ref, gout_ref,
    frames, lens, dests, offs, w_in, w_depth, w_out, in_sem,
    tables, slots, got, comp_all, cot_all, cot_t, packed, lab_pad, masks, taps, hpad, act, gact, gpad, ghid,
    part, part_got, dy_send, dy_got, dz_send, dz_got, dz_own, gfull, tap_acc, gs, gy_got, gz_send, gz_got, gall,
    tab_s, tab_r, fr_s, fr_r, cp_s, cp_r, ct_s, ct_r, pt_s, pt_r, dy_s, dy_r, dz_s, dz_r, gy_s, gy_r, gz_s, gz_r, ga_s, ga_r, gb_s, gb_r,
):
    f32, bf16 = jnp.float32, jnp.bfloat16
    me = lax.axis_index("dp")
    mine = lax.axis_index("mp")
    features, src_rows = frames.shape
    slot_rows = src_rows // n_dp
    quarter = slot_rows // n_mp
    sources = ROWS // slot_rows
    width = cot_all.shape[2]
    entries = lens.shape[1]
    block = gout_ref.shape[0]
    strip = gs.shape[2]
    centre = (KERNEL - 1) // 2
    pad = 16
    n_z = n_dp // 2
    zi, yi = me // 2, lax.rem(me, 2)
    chunk = 64

    def dp_peer(k):
        return lax.rem(me + k, n_dp)

    def dp_from(k):
        return lax.rem(me + n_dp - k, n_dp)

    def mp_peer(k):
        return lax.rem(mine + k, n_mp)

    def mp_from(k):
        return lax.rem(mine + n_mp - k, n_mp)

    def send(src, dst, ssem, rsem, **where):
        return pltpu.make_async_remote_copy(
            src_ref=src, dst_ref=dst, send_sem=ssem, recv_sem=rsem, device_id=where, device_id_type=MESH
        )

    tiles = width // 128
    loads = [
        pltpu.make_async_copy(src, dst, in_sem.at[i])
        for i, (src, dst) in enumerate(
            [(lens_in, lens), (dests_in, dests), (offs_in, offs), (frames_in, frames), (cot_in, cot_all.at[mine]),
             (w_depth_in, w_depth), (w_in_in, w_in), (w_out_in, w_out)]
        )
    ]
    for load in loads:
        load.start()
    barrier = pltpu.get_barrier_semaphore()
    for k in range(1, n_dp):
        pl.semaphore_signal(barrier, inc=1, device_id={"dp": dp_peer(k)}, device_id_type=MESH)
    for k in range(1, n_mp):
        pl.semaphore_signal(barrier, inc=1, device_id={"mp": mp_peer(k)}, device_id_type=MESH)

    for load in loads[:3]:
        load.wait()
    len_f = lens[...].astype(f32)
    dest_f = dests[...].astype(f32)
    off_f = offs[...].astype(f32)
    before = (
        lax.broadcasted_iota(jnp.int32, (entries, entries), 0) < lax.broadcasted_iota(jnp.int32, (entries, entries), 1)
    )
    begin_f = jnp.dot(
        jnp.broadcast_to(len_f, (8, entries)).astype(bf16), jnp.where(before, 1.0, 0.0).astype(bf16),
        preferred_element_type=f32,
    )[0:1]
    tables[me] = jnp.concatenate([len_f, dest_f, off_f, begin_f, jnp.zeros((4, entries), f32)], 0)
    row = lax.broadcasted_iota(jnp.int32, (n_dp * quarter, 1), 0)
    row_dest = (row // quarter).astype(f32)
    row_in = lax.rem(row, quarter).astype(f32)
    first = jnp.min(jnp.where((dest_f == row_dest) & (len_f > 0.0), begin_f, 1e6), axis=1, keepdims=True)
    wanted = first + row_in + (mine * quarter).astype(f32)
    cols = lax.broadcasted_iota(jnp.int32, (n_dp * quarter, src_rows), 1).astype(f32)
    pick = jnp.where(cols == wanted, 1.0, 0.0).astype(bf16)
    loads[3].wait()
    chosen = lax.dot_general(
        pick, frames[...], (((1,), (1,)), ((), ())), preferred_element_type=f32
    ).astype(bf16)
    for d in range(n_dp):
        slots[d] = chosen[d * quarter : (d + 1) * quarter]
    got[me] = slots[me]

    pl.semaphore_wait(barrier, n_dp - 1 + n_mp - 1)
    tab_c, fr_c, ct_c = [], [], []
    for k in range(1, n_dp):
        c = send(tables.at[me], tables.at[me], tab_s.at[k], tab_r.at[k], dp=dp_peer(k))
        c.start()
        tab_c.append(c)
    for k in range(1, n_dp):
        c = send(slots.at[dp_peer(k)], got.at[me], fr_s.at[k], fr_r.at[k], dp=dp_peer(k))
        c.start()
        fr_c.append(c)
    sibling = mine + 1 - 2 * lax.rem(mine, 2)
    across = lax.rem(mine + 2, n_mp)
    for k, peer in ((0, across), (1, sibling)):
        c = send(cot_in, cot_all.at[mine], ct_s.at[k], ct_r.at[k], mp=peer)
        c.start()
        ct_c.append(c)
    for load in loads[4:]:
        load.wait()

    taps[0:KERNEL] = w_depth[...].astype(f32)
    for ref in (hpad, gpad):
        ref[:, 0:pad] = jnp.zeros((tiles, pad, 128), f32)
        ref[:, pad + ROWS :] = jnp.zeros((tiles, pad, 128), f32)
    gfull[...] = jnp.zeros_like(gfull)

    def arrived(dst, ssem, rsem, **where):
        send(dst, dst, ssem, rsem, **where).wait_recv()

    for k in range(1, n_dp):
        src = dp_from(k)
        arrived(tables.at[src], tab_s.at[k], tab_r.at[k], dp=src)

    here = me.astype(f32)
    t_row = lax.broadcasted_iota(jnp.int32, (ROWS, 1), 0).astype(f32)
    lane = lax.broadcasted_iota(jnp.int32, (1, entries), 1).astype(f32)
    shift = jnp.zeros((ROWS, entries), f32)
    order = jnp.zeros((ROWS, entries), f32)
    label = jnp.zeros((ROWS, entries), f32)
    rank = jnp.zeros((1, 1), f32)
    selectors = []
    for s in range(n_dp):
        table = tables[s]
        t_len, t_dest, t_off, t_begin = table[0:1], table[1:2], table[2:3], table[3:4]
        to_me = (t_dest == here) & (t_len > 0.0)
        valid = jnp.max(jnp.where(to_me, 1.0, 0.0), axis=1, keepdims=True)
        match = to_me & (t_off <= t_row) & (t_row < t_off + t_len)
        inside = t_begin - slot_rows * jnp.floor(t_begin / slot_rows)
        shift = shift + jnp.where(match, inside - t_off, 0.0)
        order = order + jnp.where(match, rank, 0.0)
        label = label + jnp.where(match, s * entries + lane, 0.0)
        selectors.append([jnp.where((valid > 0.0) & (rank == r), 1.0, 0.0) for r in range(sources)])
        rank = rank + valid
    q = jnp.sum(shift, axis=1, keepdims=True) + t_row
    rank_of = jnp.sum(order, axis=1, keepdims=True)
    q_part = jnp.floor(q / quarter)
    place = q_part * (sources * quarter) + rank_of * quarter + (q - q_part * quarter)
    spots = lax.broadcasted_iota(jnp.int32, (ROWS, ROWS), 1).astype(f32)
    pick_rows = jnp.where(spots == place, 1.0, 0.0).astype(bf16)
    lab_pad[0:pad] = jnp.full((pad, 128), -1.0, f32)
    lab_pad[pad + ROWS :] = jnp.full((pad, 128), -1.0, f32)
    lab_pad[pad : pad + ROWS] = jnp.broadcast_to(jnp.sum(label, axis=1, keepdims=True), (ROWS, 128))
    for j in range(KERNEL):
        start = pad + j - centre
        masks[j] = jnp.where(lab_pad[start : start + ROWS] == lab_pad[pad : pad + ROWS], 1.0, 0.0)

    for k in range(1, n_dp):
        src = dp_from(k)
        arrived(got.at[src], fr_s.at[k], fr_r.at[k], dp=src)
    picked = [jnp.zeros((quarter, features), f32) for _ in range(sources)]
    for s in range(n_dp):
        rows_s = got[s].astype(f32)
        for r in range(sources):
            picked[r] = picked[r] + selectors[s][r] * rows_s
    comp_all[mine] = jnp.concatenate(picked, 0).astype(bf16)
    cp_c = []
    for k in range(1, n_mp):
        c = send(comp_all.at[mine], comp_all.at[mine], cp_s.at[k], cp_r.at[k], mp=mp_peer(k))
        c.start()
        cp_c.append(c)

    arrived(cot_all.at[across], ct_s.at[0], ct_r.at[0], mp=across)
    c = send(cot_all.at[across], cot_all.at[across], ct_s.at[2], ct_r.at[2], mp=sibling)
    c.start()
    ct_c.append(c)

    def use_cotangent(b, start):
        at = pl.ds(pl.multiple_of(b * width, 128), width)
        values = cot_all[b]
        cot_t[at] = values.T
        term = jnp.dot(values, w_out[at], preferred_element_type=f32)
        gact[...] = term if start else gact[...] + term

    use_cotangent(mine, True)
    use_cotangent(across, False)
    arrived(cot_all.at[sibling], ct_s.at[1], ct_r.at[1], mp=sibling)
    use_cotangent(sibling, False)
    diagonal = lax.rem(sibling + 2, n_mp)
    arrived(cot_all.at[diagonal], ct_s.at[2], ct_r.at[2], mp=sibling)
    use_cotangent(diagonal, False)

    for k in range(1, n_mp):
        src = mp_from(k)
        arrived(comp_all.at[src], cp_s.at[k], cp_r.at[k], mp=src)
    everything = jnp.concatenate([comp_all[b] for b in range(n_mp)], 0)
    packed[...] = jnp.dot(pick_rows, everything, preferred_element_type=f32).astype(bf16)
    hidden = jnp.dot(packed[...], w_in[...], preferred_element_type=f32).astype(bf16).astype(f32)
    for c in range(tiles):
        hpad[c, pad : pad + ROWS] = hidden[:, c * 128 : (c + 1) * 128]

    def columns(c):
        return pl.ds(pl.multiple_of(c * 128, 128), 128)

    partner = 2 * zi + 1 - yi
    dz_c, pt_c = [], []

    z_order = [2, 1, 3, 0]

    def dw_tile(d, c):
        at = pl.ds(pl.multiple_of(d * block, 64), block)
        return jnp.dot(cot_t[at], act[:, columns(c)], preferred_element_type=f32)

    def dy_tile(kz, c):
        return send(dy_send.at[kz, c], dy_got.at[kz, c], dy_s.at[kz, c], dy_r.at[kz, c], dp=partner)

    def dy_step(kz, c):
        dy_send[kz, c] = dw_tile(2 * lax.rem(zi + kz, n_z) + 1 - yi, c).astype(bf16)
        dy_tile(kz, c).start()

    def dz_step(kz):
        zt = lax.rem(zi + kz, n_z)
        for c in range(tiles):
            dy_tile(kz, c).wait_recv()
            total = dw_tile(2 * zt + yi, c) + dy_got[kz, c].astype(f32)
            if kz:
                dz_send[kz, c] = total.astype(bf16)
            else:
                dz_own[c] = total
        if kz:
            c = send(dz_send.at[kz], dz_got.at[kz], dz_s.at[kz], dz_r.at[kz], dp=2 * zt + yi)
            c.start()
            dz_c.append(c)

    def forward(c, carry):
        cs = columns(c)
        weights = taps[:, cs]
        for base in range(0, ROWS, chunk):
            rows = slice(base, base + chunk)
            total = jnp.zeros((chunk, 128), f32)
            for j in range(KERNEL):
                start = pad + base + j - centre
                total = total + weights[j : j + 1] * (hpad[c, start : start + chunk] * masks[j, rows])
            gate = 1.0 / (1.0 + jnp.exp(-total))
            act[rows, cs] = (total * gate).astype(bf16)
            gpad[c, pad + base : pad + base + chunk] = gact[rows, cs] * gate * (1.0 + total * (1.0 - gate))
        for kz in z_order[:-2]:
            dy_step(kz, c)
        return carry

    lax.fori_loop(0, tiles, forward, 0)
    for k in [2, 3, 1, 0]:
        at = pl.ds(pl.multiple_of(mp_peer(k) * width, 128), width)
        part[k] = lax.dot_general(
            act[...], w_out[at], (((1,), (1,)), ((), ())), preferred_element_type=f32
        ).astype(bf16)
        if k:
            c = send(part.at[k], part_got.at[k], pt_s.at[k], pt_r.at[k], mp=mp_peer(k))
            c.start()
            pt_c.append(c)

    def backward(c, carry):
        cs = columns(c)
        weights = taps[:, cs]
        for base in range(0, ROWS, chunk):
            rows = slice(base, base + chunk)
            values = hpad[c, pad + base : pad + base + chunk]
            total = cot_all[mine, rows, cs].astype(f32)
            for j in range(KERNEL):
                start = pad + base - (j - centre)
                taken = gpad[c, start : start + chunk] * masks[KERNEL - 1 - j, rows]
                total = total + weights[j : j + 1] * taken
                sums = jnp.sum((values * taken).reshape(chunk // 8, 8, 128), axis=0)
                tap_acc[j] = sums if base == 0 else tap_acc[j] + sums
            ghid[rows, cs] = total.astype(bf16)
        for j in range(KERNEL):
            gfull[features + j : features + j + 1, cs] = jnp.sum(tap_acc[j], axis=0, keepdims=True)
        return carry

    lax.fori_loop(0, tiles - 1, backward, 0)
    dz_step(z_order[0])
    lax.fori_loop(tiles - 1, tiles, backward, 0)
    gfull[0:features] = lax.dot_general(
        packed[...], ghid[...], (((0,), (0,)), ((), ())), preferred_element_type=f32
    )
    for y in range(2):
        for z in range(n_z):
            at = (y * n_z + z) * strip
            gs[y, z] = gfull[at : at + strip].astype(bf16)
    g_c = []

    def push(src, dst, ssem, rsem, peer):
        c = send(src, dst, ssem, rsem, dp=peer)
        c.start()
        g_c.append(c)

    push(gs.at[1 - yi], gy_got, gy_s.at[0], gy_r.at[0], partner)
    for kz in z_order[-2:]:
        for c in range(tiles):
            dy_step(kz, c)
    for kz in z_order[1:-2]:
        dz_step(kz)
    arrived(gy_got, gy_s.at[0], gy_r.at[0], dp=partner)
    for kz in z_order:
        zt = lax.rem(zi + kz, n_z)
        at = pl.ds(pl.multiple_of((yi * n_z + zt) * strip, 16), strip)
        total = gfull[at] + gy_got[zt].astype(f32)
        if kz:
            gz_send[kz] = total.astype(bf16)
            push(gz_send.at[kz], gz_got.at[kz], gz_s.at[kz], gz_r.at[kz], 2 * zt + yi)
    dz_step(z_order[-2])
    for kz in range(1, n_z):
        arrived(gz_got.at[kz], gz_s.at[kz], gz_r.at[kz], dp=2 * lax.rem(zi + n_z - kz, n_z) + yi)
        total = total + gz_got[kz].astype(f32)
    gall[yi, zi] = total.astype(bf16)
    for kz in z_order[:-1]:
        zt = lax.rem(zi + kz, n_z)
        push(gall.at[yi, zi], gall.at[yi, zi], ga_s.at[kz], ga_r.at[kz], 2 * zt + yi)
    push(gall.at[yi, zi], gall.at[yi, zi], gb_s.at[0], gb_r.at[0], partner)
    dz_step(0)

    branch = part[0].astype(f32)
    for k in range(1, n_mp):
        arrived(part_got.at[k], pt_s.at[k], pt_r.at[k], mp=mp_from(k))
        branch = branch + part_got[k].astype(f32)
    for c in range(tiles):
        part_c = branch[:, c * 128 : (c + 1) * 128]
        out_ref[:, c * 128 : (c + 1) * 128] = (hpad[c, pad : pad + ROWS] + part_c).astype(out_ref.dtype)
    for kz in range(1, n_z):
        src = lax.rem(zi + n_z - kz, n_z)
        arrived(gall.at[yi, src], ga_s.at[kz], ga_r.at[kz], dp=2 * src + yi)
        push(gall.at[yi, src], gall.at[yi, src], gb_s.at[kz], gb_r.at[kz], partner)
    total = dz_own[...]
    for kz in range(1, n_z):
        src = 2 * lax.rem(zi + n_z - kz, n_z) + yi
        arrived(dz_got.at[kz], dz_s.at[kz], dz_r.at[kz], dp=src)
        total = total + dz_got[kz].astype(f32)
    for c in range(tiles):
        gout_ref[:, c * 128 : (c + 1) * 128] = scale * total[c]
    for kz in range(n_z):
        src = lax.rem(zi + n_z - kz, n_z)
        arrived(gall.at[1 - yi, src], gb_s.at[kz], gb_r.at[kz], dp=partner)
    for y in range(2):
        for z in range(n_z):
            at = (y * n_z + z) * strip
            values = scale * gall[y, z].astype(f32)
            low = min(max(features - at, 0), strip)
            high = min(max(features + KERNEL - at, 0), strip)
            if low > 0:
                gin_ref[at : at + low] = values[:low]
            if high > low:
                gdep_ref[at + low - features : at + high - features] = values[low:high]
    for kz in range(n_z):
        for c in range(tiles):
            dy_tile(kz, c).wait_send()
    for c in tab_c + fr_c + ct_c + cp_c + pt_c + dz_c + g_c:
        c.wait_send()


def store_kernel(*refs):
    count = len(refs) // 2
    copies = [pltpu.make_async_copy(refs[i], refs[count + i], refs[-1].at[i]) for i in range(count)]
    for c in copies:
        c.start()
    for c in copies:
        c.wait()


def fused(frames, lengths, destinations, offsets, in_weight, depth_weight, out_weight, cotangent):
    n_dp, n_mp = lax.axis_size("dp"), lax.axis_size("mp")
    src_rows, features = frames.shape
    entries = lengths.shape[1]
    width = cotangent.shape[1]
    model = out_weight.shape[0]
    block = model // n_dp
    quarter = src_rows // n_dp // n_mp
    sources = ROWS * n_dp // src_rows
    strip = -(-(features + KERNEL) // (16 * n_dp)) * 16
    n_z = n_dp // 2
    f32, bf16 = jnp.float32, jnp.bfloat16
    vm = pltpu.VMEM
    i32 = jnp.int32
    tiles = width // 128
    scratch = [
        vm((features, src_rows), bf16),
        vm((1, entries), i32),
        vm((1, entries), i32),
        vm((1, entries), i32),
        vm((features, width), bf16),
        vm((KERNEL, width), bf16),
        vm((model, width), bf16),
        pltpu.SemaphoreType.DMA((8,)),
        vm((n_dp, 8, entries), f32),
        vm((n_dp, quarter, features), bf16),
        vm((n_dp, quarter, features), bf16),
        vm((n_mp, sources * quarter, features), bf16),
        vm((n_mp, ROWS, width), bf16),
        vm((model, ROWS), bf16),
        vm((ROWS, features), bf16),
        vm((ROWS + 32, 128), f32),
        vm((KERNEL, ROWS, 128), f32),
        vm((32, width), f32),
        vm((tiles, ROWS + 32, 128), f32),
        vm((ROWS, width), bf16),
        vm((ROWS, width), f32),
        vm((tiles, ROWS + 32, 128), f32),
        vm((ROWS, width), bf16),
        vm((n_mp, ROWS, width), bf16),
        vm((n_mp, ROWS, width), bf16),
        vm((n_z, tiles, block, 128), bf16),
        vm((n_z, tiles, block, 128), bf16),
        vm((n_z, tiles, block, 128), bf16),
        vm((n_z, tiles, block, 128), bf16),
        vm((tiles, block, 128), f32),
        vm((n_dp * strip, width), f32),
        vm((KERNEL, 8, 128), f32),
        vm((2, n_z, strip, width), bf16),
        vm((n_z, strip, width), bf16),
        vm((n_z, strip, width), bf16),
        vm((n_z, strip, width), bf16),
        vm((2, n_z, strip, width), bf16),
    ]
    for shape in ((n_dp,), (n_dp,), (n_mp,), (n_mp,), (n_mp,), (n_z, tiles), (n_z,), (1,), (n_z,), (n_z,), (n_z,)):
        scratch += [pltpu.SemaphoreType.DMA(shape), pltpu.SemaphoreType.DMA(shape)]
    whole = pl.BlockSpec(memory_space=pltpu.VMEM)
    remote = pl.BlockSpec(memory_space=pl.ANY)
    results = pl.pallas_call(
        functools.partial(fused_kernel, n_dp, n_mp, 1.0 / math.sqrt(n_dp * ROWS)),
        out_shape=(
            jax.ShapeDtypeStruct((ROWS, width), bf16),
            jax.ShapeDtypeStruct((features, width), f32),
            jax.ShapeDtypeStruct((KERNEL, width), f32),
            jax.ShapeDtypeStruct((block, width), f32),
        ),
        in_specs=[remote] * 8,
        out_specs=(whole,) * 4,
        scratch_shapes=scratch,
        compiler_params=pltpu.CompilerParams(
            collective_id=0, has_side_effects=True, vmem_limit_bytes=62 * 1024 * 1024
        ),
    )(frames.T, lengths, destinations, offsets, in_weight, depth_weight, out_weight, cotangent)
    return pl.pallas_call(
        store_kernel,
        out_shape=tuple(jax.ShapeDtypeStruct(r.shape, r.dtype) for r in results),
        in_specs=[whole] * 4,
        out_specs=(remote,) * 4,
        scratch_shapes=[pltpu.SemaphoreType.DMA((4,))],
        compiler_params=pltpu.CompilerParams(vmem_limit_bytes=62 * 1024 * 1024),
    )(*results)


def solution(mesh):
    small = mesh.shape["dp"] == 8 and mesh.shape["mp"] == 4
    placed = (
        P("dp", None),
        P("dp", None),
        P("dp", None),
        P("dp", None),
        P(None, "mp"),
        P(None, "mp"),
        P(None, "mp"),
        P("dp", "mp"),
    )
    return jax.shard_map(
        fused if small else per_device,
        mesh=mesh,
        in_specs=placed,
        out_specs=(P("dp", "mp"), P(None, "mp"), P(None, "mp"), P("dp", "mp")),
        check_vma=False,
    )
```

```python
import functools
import math

import jax
import jax.numpy as jnp
from jax import lax
from jax.experimental import pallas as pl
from jax.experimental.pallas import tpu as pltpu
from jax.sharding import PartitionSpec as P

KERNEL = 31
ROWS = 256
MESH = pl.DeviceIdType.MESH


def depth_conv(values, weights, labels, direction):
    center = (KERNEL - 1) // 2
    length = values.shape[0]
    padded = jnp.pad(values, ((center, center), (0, 0)))
    padded_labels = jnp.pad(labels, (center, center), constant_values=-1)
    result = jnp.zeros(values.shape, jnp.float32)
    for tap_index in range(KERNEL):
        start = center + direction * (tap_index - center)
        matches = (padded_labels[start : start + length] == labels)[:, None]
        taken = weights[tap_index][None, :] * padded[start : start + length]
        result = result + jnp.where(matches, taken, jnp.zeros_like(taken))
    return result


def tap_sums(grads, values, labels):
    center = (KERNEL - 1) // 2
    length = values.shape[0]
    padded = jnp.pad(values, ((center, center), (0, 0)))
    padded_labels = jnp.pad(labels, (center, center), constant_values=-1)
    rows_list = []
    for tap_index in range(KERNEL):
        matches = (padded_labels[tap_index : tap_index + length] == labels)[:, None]
        taken = grads * padded[tap_index : tap_index + length]
        rows_list.append(jnp.sum(jnp.where(matches, taken, jnp.zeros_like(taken)), axis=0))
    return jnp.stack(rows_list, 0)


def per_device(
    frames, lengths, destinations, offsets, in_weight, depth_weight, out_weight, cotangent
):
    dp_count = lax.axis_size("dp")
    src_rows = frames.shape[0]
    features = frames.shape[1]
    slot_rows = src_rows // dp_count
    entries = lengths.shape[1]
    lengths_row = lengths[0]
    end_rows = jnp.cumsum(lengths_row, dtype=jnp.int32)
    begins = end_rows - lengths_row
    row_ids = jnp.arange(src_rows, dtype=jnp.int32)
    owner_table = (begins[None, :] <= row_ids[:, None]) & (row_ids[:, None] < end_rows[None, :])
    occupied_rows = jnp.any(owner_table, axis=1)
    onehot = owner_table.astype(jnp.int32)

    def lookup(table):
        return jnp.sum(onehot * table[None, :], axis=1, dtype=jnp.int32)

    owner_index = lookup(jnp.arange(entries, dtype=jnp.int32))
    target = lookup(offsets[0]) + row_ids - lookup(begins)
    dest_row = lookup(destinations[0])
    source = lax.axis_index("dp")
    row_label = source * entries + owner_index
    dump_index = dp_count * slot_rows
    slot_index = jnp.where(occupied_rows, dest_row * slot_rows + row_ids % slot_rows, dump_index)
    send_frames = (
        jnp.zeros((dump_index + 1, features), frames.dtype)
        .at[slot_index]
        .set(frames)[:dump_index]
        .reshape(dp_count, slot_rows, features)
    )
    send_target = (
        jnp.full((dump_index + 1,), ROWS, jnp.int32)
        .at[slot_index]
        .set(target)[:dump_index]
        .reshape(dp_count, slot_rows)
    )
    send_label = (
        jnp.full((dump_index + 1,), -1, jnp.int32)
        .at[slot_index]
        .set(row_label)[:dump_index]
        .reshape(dp_count, slot_rows)
    )
    got_frames, got_target, got_label = (
        lax.all_to_all(send_frames, "dp", split_axis=0, concat_axis=0, tiled=True),
        lax.all_to_all(send_target, "dp", split_axis=0, concat_axis=0, tiled=True),
        lax.all_to_all(send_label, "dp", split_axis=0, concat_axis=0, tiled=True),
    )
    flat_target = got_target.reshape(-1)
    packed = (
        jnp.zeros((ROWS + 1, features), frames.dtype)
        .at[flat_target]
        .set(got_frames.reshape(-1, features))[:ROWS]
    )
    packed_labels = (
        jnp.full((ROWS + 1,), -1, jnp.int32).at[flat_target].set(got_label.reshape(-1))[:ROWS]
    )
    hidden = jnp.dot(packed, in_weight, preferred_element_type=jnp.float32).astype(jnp.bfloat16)
    hidden_wide = hidden.astype(jnp.float32)
    taps = depth_weight.astype(jnp.float32)
    convolved = depth_conv(hidden_wide, taps, packed_labels, 1)
    activated = jax.nn.silu(convolved).astype(jnp.bfloat16)
    partial_sum = lax.dot_general(
        activated, out_weight, (((1,), (1,)), ((), ())), preferred_element_type=jnp.float32
    )
    branch = lax.psum_scatter(
        partial_sum.astype(jnp.bfloat16), "mp", scatter_dimension=1, tiled=True
    ).astype(jnp.float32)
    output = (hidden_wide + branch).astype(jnp.bfloat16)
    cotangent_full = lax.all_gather(cotangent, "mp", axis=1, tiled=True)
    grad_scale = 1.0 / math.sqrt(dp_count * ROWS)
    grad_activated = jnp.dot(cotangent_full, out_weight, preferred_element_type=jnp.float32)
    sigmoid_value = jax.nn.sigmoid(convolved)
    grad_convolved = grad_activated * sigmoid_value * (1.0 + convolved * (1.0 - sigmoid_value))
    grad_hidden = (
        cotangent.astype(jnp.float32) + depth_conv(grad_convolved, taps, packed_labels, -1)
    ).astype(jnp.bfloat16)
    out_weight_gradient = lax.psum_scatter(
        grad_scale
        * lax.dot_general(
            cotangent_full, activated, (((0,), (0,)), ((), ())), preferred_element_type=jnp.float32
        ),
        "dp",
        scatter_dimension=0,
        tiled=True,
    )
    term_in = grad_scale * lax.dot_general(
        packed, grad_hidden, (((0,), (0,)), ((), ())), preferred_element_type=jnp.float32
    )
    term_depth = grad_scale * tap_sums(grad_convolved, hidden_wide, packed_labels)
    in_weight_gradient, depth_gradient = lax.psum((term_in, term_depth), "dp")
    return (output, in_weight_gradient, depth_gradient, out_weight_gradient)


def fused_kernel(
    n_dp, n_mp, scale,
    frames_in, lens_in, dests_in, offs_in, w_in_in, w_depth_in, w_out_in, cot_in,
    out_ref, gin_ref, gdep_ref, gout_ref,
    frames, lens, dests, offs, w_in, w_depth, w_out, in_sem,
    tables, slots, got, comp_all, cot_all, cot_t, packed, lab_pad, masks, taps, hpad, act, pact, own_t, pcot, gact, gpad, ghid,
    part, part_got, dz_send, dz_got, dz_own, gfull, tap_acc, gs, gy_got, gz_send, gz_got, gall,
    tab_s, tab_r, fr_s, fr_r, cp_s, cp_r, ct_s, ct_r, pc_s, pc_r, pt_s, pt_r, ac_s, ac_r, dz_s, dz_r, gy_s, gy_r, gz_s, gz_r, ga_s, ga_r, gb_s, gb_r,
):
    f32, bf16 = jnp.float32, jnp.bfloat16
    me = lax.axis_index("dp")
    mine = lax.axis_index("mp")
    features, src_rows = frames.shape
    slot_rows = src_rows // n_dp
    quarter = slot_rows // n_mp
    sources = ROWS // slot_rows
    width = cot_all.shape[2]
    entries = lens.shape[1]
    block = gout_ref.shape[0]
    strip = gs.shape[2]
    centre = (KERNEL - 1) // 2
    pad = 16
    n_z = n_dp // 2
    zi, yi = me // 2, lax.rem(me, 2)
    chunk = 64

    def dp_peer(k):
        return lax.rem(me + k, n_dp)

    def dp_from(k):
        return lax.rem(me + n_dp - k, n_dp)

    def mp_peer(k):
        return lax.rem(mine + k, n_mp)

    def mp_from(k):
        return lax.rem(mine + n_mp - k, n_mp)

    def send(src, dst, ssem, rsem, **where):
        return pltpu.make_async_remote_copy(
            src_ref=src, dst_ref=dst, send_sem=ssem, recv_sem=rsem, device_id=where, device_id_type=MESH
        )

    tiles = width // 128
    loads = [
        pltpu.make_async_copy(src, dst, in_sem.at[i])
        for i, (src, dst) in enumerate(
            [(lens_in, lens), (dests_in, dests), (offs_in, offs), (frames_in, frames), (cot_in, cot_all.at[mine]),
             (w_depth_in, w_depth), (w_in_in, w_in), (w_out_in, w_out)]
        )
    ]
    for load in loads:
        load.start()
    barrier = pltpu.get_barrier_semaphore()
    for k in range(1, n_dp):
        pl.semaphore_signal(barrier, inc=1, device_id={"dp": dp_peer(k)}, device_id_type=MESH)
    for k in range(1, n_mp):
        pl.semaphore_signal(barrier, inc=1, device_id={"mp": mp_peer(k)}, device_id_type=MESH)

    for load in loads[:3]:
        load.wait()
    len_f = lens[...].astype(f32)
    dest_f = dests[...].astype(f32)
    off_f = offs[...].astype(f32)
    before = (
        lax.broadcasted_iota(jnp.int32, (entries, entries), 0) < lax.broadcasted_iota(jnp.int32, (entries, entries), 1)
    )
    begin_f = jnp.dot(
        jnp.broadcast_to(len_f, (8, entries)).astype(bf16), jnp.where(before, 1.0, 0.0).astype(bf16),
        preferred_element_type=f32,
    )[0:1]
    tables[me] = jnp.concatenate([len_f, dest_f, off_f, begin_f, jnp.zeros((4, entries), f32)], 0)
    row = lax.broadcasted_iota(jnp.int32, (n_dp * quarter, 1), 0)
    row_dest = (row // quarter).astype(f32)
    row_in = lax.rem(row, quarter).astype(f32)
    first = jnp.min(jnp.where((dest_f == row_dest) & (len_f > 0.0), begin_f, 1e6), axis=1, keepdims=True)
    wanted = first + row_in + (mine * quarter).astype(f32)
    cols = lax.broadcasted_iota(jnp.int32, (n_dp * quarter, src_rows), 1).astype(f32)
    pick = jnp.where(cols == wanted, 1.0, 0.0).astype(bf16)
    loads[3].wait()
    chosen = lax.dot_general(
        pick, frames[...], (((1,), (1,)), ((), ())), preferred_element_type=f32
    ).astype(bf16)
    for d in range(n_dp):
        slots[d] = chosen[d * quarter : (d + 1) * quarter]
    got[me] = slots[me]

    pl.semaphore_wait(barrier, n_dp - 1 + n_mp - 1)
    tab_c, fr_c, ct_c = [], [], []
    for k in range(1, n_dp):
        c = send(tables.at[me], tables.at[me], tab_s.at[k], tab_r.at[k], dp=dp_peer(k))
        c.start()
        tab_c.append(c)
    for k in range(1, n_dp):
        c = send(slots.at[dp_peer(k)], got.at[me], fr_s.at[k], fr_r.at[k], dp=dp_peer(k))
        c.start()
        fr_c.append(c)
    sibling = mine + 1 - 2 * lax.rem(mine, 2)
    across = lax.rem(mine + 2, n_mp)
    for k, peer in ((0, across), (1, sibling)):
        c = send(cot_in, cot_all.at[mine], ct_s.at[k], ct_r.at[k], mp=peer)
        c.start()
        ct_c.append(c)
    for load in loads[4:]:
        load.wait()
    partner = 2 * zi + 1 - yi
    own_t[...] = cot_all[mine].T.reshape(2, block, ROWS)
    c = send(own_t.at[1 - yi], pcot.at[mine], pc_s.at[0], pc_r.at[0], dp=partner)
    c.start()
    ct_c.append(c)

    taps[0:KERNEL] = w_depth[...].astype(f32)
    for ref in (hpad, gpad):
        ref[:, 0:pad] = jnp.zeros((tiles, pad, 128), f32)
        ref[:, pad + ROWS :] = jnp.zeros((tiles, pad, 128), f32)
    gfull[...] = jnp.zeros_like(gfull)

    def arrived(dst, ssem, rsem, **where):
        send(dst, dst, ssem, rsem, **where).wait_recv()

    for k in range(1, n_dp):
        src = dp_from(k)
        arrived(tables.at[src], tab_s.at[k], tab_r.at[k], dp=src)

    here = me.astype(f32)
    t_row = lax.broadcasted_iota(jnp.int32, (ROWS, 1), 0).astype(f32)
    lane = lax.broadcasted_iota(jnp.int32, (1, entries), 1).astype(f32)
    shift = jnp.zeros((ROWS, entries), f32)
    order = jnp.zeros((ROWS, entries), f32)
    label = jnp.zeros((ROWS, entries), f32)
    rank = jnp.zeros((1, 1), f32)
    selectors = []
    for s in range(n_dp):
        table = tables[s]
        t_len, t_dest, t_off, t_begin = table[0:1], table[1:2], table[2:3], table[3:4]
        to_me = (t_dest == here) & (t_len > 0.0)
        valid = jnp.max(jnp.where(to_me, 1.0, 0.0), axis=1, keepdims=True)
        match = to_me & (t_off <= t_row) & (t_row < t_off + t_len)
        inside = t_begin - slot_rows * jnp.floor(t_begin / slot_rows)
        shift = shift + jnp.where(match, inside - t_off, 0.0)
        order = order + jnp.where(match, rank, 0.0)
        label = label + jnp.where(match, s * entries + lane, 0.0)
        selectors.append([jnp.where((valid > 0.0) & (rank == r), 1.0, 0.0) for r in range(sources)])
        rank = rank + valid
    q = jnp.sum(shift, axis=1, keepdims=True) + t_row
    rank_of = jnp.sum(order, axis=1, keepdims=True)
    q_part = jnp.floor(q / quarter)
    place = q_part * (sources * quarter) + rank_of * quarter + (q - q_part * quarter)
    spots = lax.broadcasted_iota(jnp.int32, (ROWS, ROWS), 1).astype(f32)
    pick_rows = jnp.where(spots == place, 1.0, 0.0).astype(bf16)
    lab_pad[0:pad] = jnp.full((pad, 128), -1.0, f32)
    lab_pad[pad + ROWS :] = jnp.full((pad, 128), -1.0, f32)
    lab_pad[pad : pad + ROWS] = jnp.broadcast_to(jnp.sum(label, axis=1, keepdims=True), (ROWS, 128))
    for j in range(KERNEL):
        start = pad + j - centre
        masks[j] = jnp.where(lab_pad[start : start + ROWS] == lab_pad[pad : pad + ROWS], 1.0, 0.0)

    for k in range(1, n_dp):
        src = dp_from(k)
        arrived(got.at[src], fr_s.at[k], fr_r.at[k], dp=src)
    picked = [jnp.zeros((quarter, features), f32) for _ in range(sources)]
    for s in range(n_dp):
        rows_s = got[s].astype(f32)
        for r in range(sources):
            picked[r] = picked[r] + selectors[s][r] * rows_s
    comp_all[mine] = jnp.concatenate(picked, 0).astype(bf16)
    cp_c = []
    for k in range(1, n_mp):
        c = send(comp_all.at[mine], comp_all.at[mine], cp_s.at[k], cp_r.at[k], mp=mp_peer(k))
        c.start()
        cp_c.append(c)

    arrived(pcot.at[mine], pc_s.at[0], pc_r.at[0], dp=partner)
    for k in range(1, n_mp):
        c = send(pcot.at[mine], pcot.at[mine], pc_s.at[k], pc_r.at[k], mp=mp_peer(k))
        c.start()
        ct_c.append(c)

    arrived(cot_all.at[across], ct_s.at[0], ct_r.at[0], mp=across)
    c = send(cot_all.at[across], cot_all.at[across], ct_s.at[2], ct_r.at[2], mp=sibling)
    c.start()
    ct_c.append(c)

    def use_cotangent(b, start):
        at = pl.ds(pl.multiple_of(b * width, 128), width)
        values = cot_all[b]
        cot_t[at] = values.T
        term = jnp.dot(values, w_out[at], preferred_element_type=f32)
        gact[...] = term if start else gact[...] + term

    use_cotangent(mine, True)
    use_cotangent(across, False)
    arrived(cot_all.at[sibling], ct_s.at[1], ct_r.at[1], mp=sibling)
    use_cotangent(sibling, False)
    diagonal = lax.rem(sibling + 2, n_mp)
    arrived(cot_all.at[diagonal], ct_s.at[2], ct_r.at[2], mp=sibling)
    use_cotangent(diagonal, False)

    for k in range(1, n_mp):
        src = mp_from(k)
        arrived(comp_all.at[src], cp_s.at[k], cp_r.at[k], mp=src)
    everything = jnp.concatenate([comp_all[b] for b in range(n_mp)], 0)
    packed[...] = jnp.dot(pick_rows, everything, preferred_element_type=f32).astype(bf16)
    hidden = jnp.dot(packed[...], w_in[...], preferred_element_type=f32).astype(bf16).astype(f32)
    for c in range(tiles):
        hpad[c, pad : pad + ROWS] = hidden[:, c * 128 : (c + 1) * 128]

    def columns(c):
        return pl.ds(pl.multiple_of(c * 128, 128), 128)

    dz_c, pt_c = [], []

    z_order = [2, 1, 3, 0]

    def act_tile(c):
        return send(act.at[c], pact.at[c], ac_s.at[c], ac_r.at[c], dp=partner)

    def dz_step(kz):
        zt = lax.rem(zi + kz, n_z)
        at = pl.ds(pl.multiple_of((2 * zt + yi) * block, 64), block)
        for c in range(tiles):
            total = jnp.dot(cot_t[at], act[c], preferred_element_type=f32)
            total = total + jnp.dot(pcot[zt], pact[c], preferred_element_type=f32)
            if kz:
                dz_send[kz, c] = total.astype(bf16)
            else:
                dz_own[c] = total
        if kz:
            c = send(dz_send.at[kz], dz_got.at[kz], dz_s.at[kz], dz_r.at[kz], dp=2 * zt + yi)
            c.start()
            dz_c.append(c)

    def forward(c, carry):
        cs = columns(c)
        weights = taps[:, cs]
        for base in range(0, ROWS, chunk):
            rows = slice(base, base + chunk)
            total = jnp.zeros((chunk, 128), f32)
            for j in range(KERNEL):
                start = pad + base + j - centre
                total = total + weights[j : j + 1] * (hpad[c, start : start + chunk] * masks[j, rows])
            gate = 1.0 / (1.0 + jnp.exp(-total))
            act[c, rows] = (total * gate).astype(bf16)
            gpad[c, pad + base : pad + base + chunk] = gact[rows, cs] * gate * (1.0 + total * (1.0 - gate))
        act_tile(c).start()
        return carry

    lax.fori_loop(0, tiles, forward, 0)
    activated = jnp.concatenate([act[c] for c in range(tiles)], 1)
    for k in [2, 3, 1, 0]:
        at = pl.ds(pl.multiple_of(mp_peer(k) * width, 128), width)
        part[k] = lax.dot_general(
            activated, w_out[at], (((1,), (1,)), ((), ())), preferred_element_type=f32
        ).astype(bf16)
        if k:
            c = send(part.at[k], part_got.at[k], pt_s.at[k], pt_r.at[k], mp=mp_peer(k))
            c.start()
            pt_c.append(c)

    for k in range(1, n_mp):
        src = mp_from(k)
        arrived(pcot.at[src], pc_s.at[k], pc_r.at[k], mp=src)
    for c in range(tiles):
        act_tile(c).wait_recv()
    for kz in z_order[:-2]:
        dz_step(kz)

    def backward(c, carry):
        cs = columns(c)
        weights = taps[:, cs]
        for base in range(0, ROWS, chunk):
            rows = slice(base, base + chunk)
            values = hpad[c, pad + base : pad + base + chunk]
            total = cot_all[mine, rows, cs].astype(f32)
            for j in range(KERNEL):
                start = pad + base - (j - centre)
                taken = gpad[c, start : start + chunk] * masks[KERNEL - 1 - j, rows]
                total = total + weights[j : j + 1] * taken
                sums = jnp.sum((values * taken).reshape(chunk // 8, 8, 128), axis=0)
                tap_acc[j] = sums if base == 0 else tap_acc[j] + sums
            ghid[rows, cs] = total.astype(bf16)
        for j in range(KERNEL):
            gfull[features + j : features + j + 1, cs] = jnp.sum(tap_acc[j], axis=0, keepdims=True)
        return carry

    lax.fori_loop(0, tiles, backward, 0)
    gfull[0:features] = lax.dot_general(
        packed[...], ghid[...], (((0,), (0,)), ((), ())), preferred_element_type=f32
    )
    for y in range(2):
        for z in range(n_z):
            at = (y * n_z + z) * strip
            gs[y, z] = gfull[at : at + strip].astype(bf16)
    g_c = []

    def push(src, dst, ssem, rsem, peer):
        c = send(src, dst, ssem, rsem, dp=peer)
        c.start()
        g_c.append(c)

    push(gs.at[1 - yi], gy_got, gy_s.at[0], gy_r.at[0], partner)
    arrived(gy_got, gy_s.at[0], gy_r.at[0], dp=partner)
    for kz in z_order:
        zt = lax.rem(zi + kz, n_z)
        at = pl.ds(pl.multiple_of((yi * n_z + zt) * strip, 16), strip)
        total = gfull[at] + gy_got[zt].astype(f32)
        if kz:
            gz_send[kz] = total.astype(bf16)
            push(gz_send.at[kz], gz_got.at[kz], gz_s.at[kz], gz_r.at[kz], 2 * zt + yi)
    dz_step(z_order[-2])
    for kz in range(1, n_z):
        arrived(gz_got.at[kz], gz_s.at[kz], gz_r.at[kz], dp=2 * lax.rem(zi + n_z - kz, n_z) + yi)
        total = total + gz_got[kz].astype(f32)
    gall[yi, zi] = total.astype(bf16)
    for kz in z_order[:-1]:
        zt = lax.rem(zi + kz, n_z)
        push(gall.at[yi, zi], gall.at[yi, zi], ga_s.at[kz], ga_r.at[kz], 2 * zt + yi)
    push(gall.at[yi, zi], gall.at[yi, zi], gb_s.at[0], gb_r.at[0], partner)
    dz_step(0)

    branch = part[0].astype(f32)
    for k in range(1, n_mp):
        arrived(part_got.at[k], pt_s.at[k], pt_r.at[k], mp=mp_from(k))
        branch = branch + part_got[k].astype(f32)
    for c in range(tiles):
        part_c = branch[:, c * 128 : (c + 1) * 128]
        out_ref[:, c * 128 : (c + 1) * 128] = (hpad[c, pad : pad + ROWS] + part_c).astype(out_ref.dtype)
    for kz in range(1, n_z):
        src = lax.rem(zi + n_z - kz, n_z)
        arrived(gall.at[yi, src], ga_s.at[kz], ga_r.at[kz], dp=2 * src + yi)
        push(gall.at[yi, src], gall.at[yi, src], gb_s.at[kz], gb_r.at[kz], partner)
    total = dz_own[...]
    for kz in range(1, n_z):
        src = 2 * lax.rem(zi + n_z - kz, n_z) + yi
        arrived(dz_got.at[kz], dz_s.at[kz], dz_r.at[kz], dp=src)
        total = total + dz_got[kz].astype(f32)
    for c in range(tiles):
        gout_ref[:, c * 128 : (c + 1) * 128] = scale * total[c]
    for kz in range(n_z):
        src = lax.rem(zi + n_z - kz, n_z)
        arrived(gall.at[1 - yi, src], gb_s.at[kz], gb_r.at[kz], dp=partner)
    for y in range(2):
        for z in range(n_z):
            at = (y * n_z + z) * strip
            values = scale * gall[y, z].astype(f32)
            low = min(max(features - at, 0), strip)
            high = min(max(features + KERNEL - at, 0), strip)
            if low > 0:
                gin_ref[at : at + low] = values[:low]
            if high > low:
                gdep_ref[at + low - features : at + high - features] = values[low:high]
    for c in range(tiles):
        act_tile(c).wait_send()
    for c in tab_c + fr_c + ct_c + cp_c + pt_c + dz_c + g_c:
        c.wait_send()


def store_kernel(*refs):
    count = len(refs) // 2
    copies = [pltpu.make_async_copy(refs[i], refs[count + i], refs[-1].at[i]) for i in range(count)]
    for c in copies:
        c.start()
    for c in copies:
        c.wait()


def fused(frames, lengths, destinations, offsets, in_weight, depth_weight, out_weight, cotangent):
    n_dp, n_mp = lax.axis_size("dp"), lax.axis_size("mp")
    src_rows, features = frames.shape
    entries = lengths.shape[1]
    width = cotangent.shape[1]
    model = out_weight.shape[0]
    block = model // n_dp
    quarter = src_rows // n_dp // n_mp
    sources = ROWS * n_dp // src_rows
    strip = -(-(features + KERNEL) // (16 * n_dp)) * 16
    n_z = n_dp // 2
    f32, bf16 = jnp.float32, jnp.bfloat16
    vm = pltpu.VMEM
    i32 = jnp.int32
    tiles = width // 128
    scratch = [
        vm((features, src_rows), bf16),
        vm((1, entries), i32),
        vm((1, entries), i32),
        vm((1, entries), i32),
        vm((features, width), bf16),
        vm((KERNEL, width), bf16),
        vm((model, width), bf16),
        pltpu.SemaphoreType.DMA((8,)),
        vm((n_dp, 8, entries), f32),
        vm((n_dp, quarter, features), bf16),
        vm((n_dp, quarter, features), bf16),
        vm((n_mp, sources * quarter, features), bf16),
        vm((n_mp, ROWS, width), bf16),
        vm((model, ROWS), bf16),
        vm((ROWS, features), bf16),
        vm((ROWS + 32, 128), f32),
        vm((KERNEL, ROWS, 128), f32),
        vm((32, width), f32),
        vm((tiles, ROWS + 32, 128), f32),
        vm((tiles, ROWS, 128), bf16),
        vm((tiles, ROWS, 128), bf16),
        vm((2, block, ROWS), bf16),
        vm((n_mp, block, ROWS), bf16),
        vm((ROWS, width), f32),
        vm((tiles, ROWS + 32, 128), f32),
        vm((ROWS, width), bf16),
        vm((n_mp, ROWS, width), bf16),
        vm((n_mp, ROWS, width), bf16),
        vm((n_z, tiles, block, 128), bf16),
        vm((n_z, tiles, block, 128), bf16),
        vm((tiles, block, 128), f32),
        vm((n_dp * strip, width), f32),
        vm((KERNEL, 8, 128), f32),
        vm((2, n_z, strip, width), bf16),
        vm((n_z, strip, width), bf16),
        vm((n_z, strip, width), bf16),
        vm((n_z, strip, width), bf16),
        vm((2, n_z, strip, width), bf16),
    ]
    for shape in ((n_dp,), (n_dp,), (n_mp,), (n_mp,), (n_mp,), (n_mp,), (tiles,), (n_z,), (1,), (n_z,), (n_z,), (n_z,)):
        scratch += [pltpu.SemaphoreType.DMA(shape), pltpu.SemaphoreType.DMA(shape)]
    whole = pl.BlockSpec(memory_space=pltpu.VMEM)
    remote = pl.BlockSpec(memory_space=pl.ANY)
    results = pl.pallas_call(
        functools.partial(fused_kernel, n_dp, n_mp, 1.0 / math.sqrt(n_dp * ROWS)),
        out_shape=(
            jax.ShapeDtypeStruct((ROWS, width), bf16),
            jax.ShapeDtypeStruct((features, width), f32),
            jax.ShapeDtypeStruct((KERNEL, width), f32),
            jax.ShapeDtypeStruct((block, width), f32),
        ),
        in_specs=[remote] * 8,
        out_specs=(whole,) * 4,
        scratch_shapes=scratch,
        compiler_params=pltpu.CompilerParams(
            collective_id=0, has_side_effects=True, vmem_limit_bytes=62 * 1024 * 1024
        ),
    )(frames.T, lengths, destinations, offsets, in_weight, depth_weight, out_weight, cotangent)
    return pl.pallas_call(
        store_kernel,
        out_shape=tuple(jax.ShapeDtypeStruct(r.shape, r.dtype) for r in results),
        in_specs=[whole] * 4,
        out_specs=(remote,) * 4,
        scratch_shapes=[pltpu.SemaphoreType.DMA((4,))],
        compiler_params=pltpu.CompilerParams(vmem_limit_bytes=62 * 1024 * 1024),
    )(*results)


def solution(mesh):
    small = mesh.shape["dp"] == 2 * mesh.shape["mp"] == 8
    placed = (
        P("dp", None),
        P("dp", None),
        P("dp", None),
        P("dp", None),
        P(None, "mp"),
        P(None, "mp"),
        P(None, "mp"),
        P("dp", "mp"),
    )
    return jax.shard_map(
        fused if small else per_device,
        mesh=mesh,
        in_specs=placed,
        out_specs=(P("dp", "mp"), P(None, "mp"), P(None, "mp"), P("dp", "mp")),
        check_vma=False,
    )
```

```python
import functools
import math

import jax
import jax.numpy as jnp
from jax import lax
from jax.experimental import pallas as pl
from jax.experimental.pallas import tpu as pltpu
from jax.sharding import PartitionSpec as P

KERNEL = 31
ROWS = 256
MESH = pl.DeviceIdType.MESH


def depth_conv(values, weights, labels, direction):
    center = (KERNEL - 1) // 2
    length = values.shape[0]
    padded = jnp.pad(values, ((center, center), (0, 0)))
    padded_labels = jnp.pad(labels, (center, center), constant_values=-1)
    result = jnp.zeros(values.shape, jnp.float32)
    for tap_index in range(KERNEL):
        start = center + direction * (tap_index - center)
        matches = (padded_labels[start : start + length] == labels)[:, None]
        taken = weights[tap_index][None, :] * padded[start : start + length]
        result = result + jnp.where(matches, taken, jnp.zeros_like(taken))
    return result


def tap_sums(grads, values, labels):
    center = (KERNEL - 1) // 2
    length = values.shape[0]
    padded = jnp.pad(values, ((center, center), (0, 0)))
    padded_labels = jnp.pad(labels, (center, center), constant_values=-1)
    rows_list = []
    for tap_index in range(KERNEL):
        matches = (padded_labels[tap_index : tap_index + length] == labels)[:, None]
        taken = grads * padded[tap_index : tap_index + length]
        rows_list.append(jnp.sum(jnp.where(matches, taken, jnp.zeros_like(taken)), axis=0))
    return jnp.stack(rows_list, 0)


def per_device(
    frames, lengths, destinations, offsets, in_weight, depth_weight, out_weight, cotangent
):
    dp_count = lax.axis_size("dp")
    src_rows = frames.shape[0]
    features = frames.shape[1]
    slot_rows = src_rows // dp_count
    entries = lengths.shape[1]
    lengths_row = lengths[0]
    end_rows = jnp.cumsum(lengths_row, dtype=jnp.int32)
    begins = end_rows - lengths_row
    row_ids = jnp.arange(src_rows, dtype=jnp.int32)
    owner_table = (begins[None, :] <= row_ids[:, None]) & (row_ids[:, None] < end_rows[None, :])
    occupied_rows = jnp.any(owner_table, axis=1)
    onehot = owner_table.astype(jnp.int32)

    def lookup(table):
        return jnp.sum(onehot * table[None, :], axis=1, dtype=jnp.int32)

    owner_index = lookup(jnp.arange(entries, dtype=jnp.int32))
    target = lookup(offsets[0]) + row_ids - lookup(begins)
    dest_row = lookup(destinations[0])
    source = lax.axis_index("dp")
    row_label = source * entries + owner_index
    dump_index = dp_count * slot_rows
    slot_index = jnp.where(occupied_rows, dest_row * slot_rows + row_ids % slot_rows, dump_index)
    send_frames = (
        jnp.zeros((dump_index + 1, features), frames.dtype)
        .at[slot_index]
        .set(frames)[:dump_index]
        .reshape(dp_count, slot_rows, features)
    )
    send_target = (
        jnp.full((dump_index + 1,), ROWS, jnp.int32)
        .at[slot_index]
        .set(target)[:dump_index]
        .reshape(dp_count, slot_rows)
    )
    send_label = (
        jnp.full((dump_index + 1,), -1, jnp.int32)
        .at[slot_index]
        .set(row_label)[:dump_index]
        .reshape(dp_count, slot_rows)
    )
    got_frames, got_target, got_label = (
        lax.all_to_all(send_frames, "dp", split_axis=0, concat_axis=0, tiled=True),
        lax.all_to_all(send_target, "dp", split_axis=0, concat_axis=0, tiled=True),
        lax.all_to_all(send_label, "dp", split_axis=0, concat_axis=0, tiled=True),
    )
    flat_target = got_target.reshape(-1)
    packed = (
        jnp.zeros((ROWS + 1, features), frames.dtype)
        .at[flat_target]
        .set(got_frames.reshape(-1, features))[:ROWS]
    )
    packed_labels = (
        jnp.full((ROWS + 1,), -1, jnp.int32).at[flat_target].set(got_label.reshape(-1))[:ROWS]
    )
    hidden = jnp.dot(packed, in_weight, preferred_element_type=jnp.float32).astype(jnp.bfloat16)
    hidden_wide = hidden.astype(jnp.float32)
    taps = depth_weight.astype(jnp.float32)
    convolved = depth_conv(hidden_wide, taps, packed_labels, 1)
    activated = jax.nn.silu(convolved).astype(jnp.bfloat16)
    partial_sum = lax.dot_general(
        activated, out_weight, (((1,), (1,)), ((), ())), preferred_element_type=jnp.float32
    )
    branch = lax.psum_scatter(
        partial_sum.astype(jnp.bfloat16), "mp", scatter_dimension=1, tiled=True
    ).astype(jnp.float32)
    output = (hidden_wide + branch).astype(jnp.bfloat16)
    cotangent_full = lax.all_gather(cotangent, "mp", axis=1, tiled=True)
    grad_scale = 1.0 / math.sqrt(dp_count * ROWS)
    grad_activated = jnp.dot(cotangent_full, out_weight, preferred_element_type=jnp.float32)
    sigmoid_value = jax.nn.sigmoid(convolved)
    grad_convolved = grad_activated * sigmoid_value * (1.0 + convolved * (1.0 - sigmoid_value))
    grad_hidden = (
        cotangent.astype(jnp.float32) + depth_conv(grad_convolved, taps, packed_labels, -1)
    ).astype(jnp.bfloat16)
    out_weight_gradient = lax.psum_scatter(
        grad_scale
        * lax.dot_general(
            cotangent_full, activated, (((0,), (0,)), ((), ())), preferred_element_type=jnp.float32
        ),
        "dp",
        scatter_dimension=0,
        tiled=True,
    )
    term_in = grad_scale * lax.dot_general(
        packed, grad_hidden, (((0,), (0,)), ((), ())), preferred_element_type=jnp.float32
    )
    term_depth = grad_scale * tap_sums(grad_convolved, hidden_wide, packed_labels)
    in_weight_gradient, depth_gradient = lax.psum((term_in, term_depth), "dp")
    return (output, in_weight_gradient, depth_gradient, out_weight_gradient)


def fused_kernel(
    n_dp, n_mp, scale,
    frames_in, lens_in, dests_in, offs_in, w_in_in, w_depth_in, w_out_in, cot_in,
    out_ref, gin_ref, gdep_ref, gout_ref,
    frames, lens, dests, offs, w_in, w_depth, w_out, in_sem,
    tables, slots, got, comp_all, cot_all, cot_t, packed_t, lab_pad, masks, taps, hpad, act, pact, own_t, pcot, gact, gpad, ghid,
    part, part_got, dz_send, dz_got, dz_own, gfull, g_own, tap_acc, gs, gy_got, gz_send, gz_got, gall,
    tab_s, tab_r, fr_s, fr_r, cp_s, cp_r, ct_s, ct_r, pc_s, pc_r, pt_s, pt_r, ac_s, ac_r, dz_s, dz_r, gy_s, gy_r, gz_s, gz_r, ga_s, ga_r, gb_s, gb_r,
):
    f32, bf16 = jnp.float32, jnp.bfloat16
    me = lax.axis_index("dp")
    mine = lax.axis_index("mp")
    features, src_rows = frames.shape
    slot_rows = src_rows // n_dp
    quarter = slot_rows // n_mp
    sources = ROWS // slot_rows
    width = cot_all.shape[2]
    entries = lens.shape[1]
    block = gout_ref.shape[0]
    strip = gs.shape[3]
    centre = (KERNEL - 1) // 2
    pad = 16
    n_z = n_dp // 2
    zi, yi = me // 2, lax.rem(me, 2)
    chunk = 64

    def dp_peer(k):
        return lax.rem(me + k, n_dp)

    def dp_from(k):
        return lax.rem(me + n_dp - k, n_dp)

    def mp_peer(k):
        return lax.rem(mine + k, n_mp)

    def mp_from(k):
        return lax.rem(mine + n_mp - k, n_mp)

    def send(src, dst, ssem, rsem, **where):
        return pltpu.make_async_remote_copy(
            src_ref=src, dst_ref=dst, send_sem=ssem, recv_sem=rsem, device_id=where, device_id_type=MESH
        )

    tiles = width // 128
    loads = [
        pltpu.make_async_copy(src, dst, in_sem.at[i])
        for i, (src, dst) in enumerate(
            [(lens_in, lens), (dests_in, dests), (offs_in, offs), (frames_in, frames), (cot_in, cot_all.at[mine]),
             (w_depth_in, w_depth), (w_in_in, w_in), (w_out_in, w_out)]
        )
    ]
    for load in loads:
        load.start()
    barrier = pltpu.get_barrier_semaphore()
    for k in range(1, n_dp):
        pl.semaphore_signal(barrier, inc=1, device_id={"dp": dp_peer(k)}, device_id_type=MESH)
    for k in range(1, n_mp):
        pl.semaphore_signal(barrier, inc=1, device_id={"mp": mp_peer(k)}, device_id_type=MESH)

    for load in loads[:3]:
        load.wait()
    len_f = lens[...].astype(f32)
    dest_f = dests[...].astype(f32)
    off_f = offs[...].astype(f32)
    before = (
        lax.broadcasted_iota(jnp.int32, (entries, entries), 0) < lax.broadcasted_iota(jnp.int32, (entries, entries), 1)
    )
    begin_f = jnp.dot(
        jnp.broadcast_to(len_f, (8, entries)).astype(bf16), jnp.where(before, 1.0, 0.0).astype(bf16),
        preferred_element_type=f32,
    )[0:1]
    tables[me] = jnp.concatenate([len_f, dest_f, off_f, begin_f, jnp.zeros((4, entries), f32)], 0)
    row = lax.broadcasted_iota(jnp.int32, (n_dp * quarter, 1), 0)
    row_dest = (row // quarter).astype(f32)
    row_in = lax.rem(row, quarter).astype(f32)
    first = jnp.min(jnp.where((dest_f == row_dest) & (len_f > 0.0), begin_f, 1e6), axis=1, keepdims=True)
    wanted = first + row_in + (mine * quarter).astype(f32)
    cols = lax.broadcasted_iota(jnp.int32, (n_dp * quarter, src_rows), 1).astype(f32)
    pick = jnp.where(cols == wanted, 1.0, 0.0).astype(bf16)
    loads[3].wait()
    chosen = lax.dot_general(
        pick, frames[...], (((1,), (1,)), ((), ())), preferred_element_type=f32
    ).astype(bf16)
    for d in range(n_dp):
        slots[d] = chosen[d * quarter : (d + 1) * quarter]
    got[me] = slots[me]

    pl.semaphore_wait(barrier, n_dp - 1 + n_mp - 1)
    tab_c, fr_c, ct_c = [], [], []
    for k in range(1, n_dp):
        c = send(tables.at[me], tables.at[me], tab_s.at[k], tab_r.at[k], dp=dp_peer(k))
        c.start()
        tab_c.append(c)
    for k in range(1, n_dp):
        c = send(slots.at[dp_peer(k)], got.at[me], fr_s.at[k], fr_r.at[k], dp=dp_peer(k))
        c.start()
        fr_c.append(c)
    sibling = mine + 1 - 2 * lax.rem(mine, 2)
    across = lax.rem(mine + 2, n_mp)
    for k, peer in ((0, across), (1, sibling)):
        c = send(cot_in, cot_all.at[mine], ct_s.at[k], ct_r.at[k], mp=peer)
        c.start()
        ct_c.append(c)
    for load in loads[4:]:
        load.wait()
    partner = 2 * zi + 1 - yi
    own_t[...] = cot_all[mine].T.reshape(2, block, ROWS)
    c = send(own_t.at[1 - yi], pcot.at[mine], pc_s.at[0], pc_r.at[0], dp=partner)
    c.start()
    ct_c.append(c)

    taps[0:KERNEL] = w_depth[...].astype(f32)
    for ref in (hpad, gpad):
        ref[:, 0:pad] = jnp.zeros((tiles, pad, 128), f32)
        ref[:, pad + ROWS :] = jnp.zeros((tiles, pad, 128), f32)
    gfull[...] = jnp.zeros_like(gfull)

    def arrived(dst, ssem, rsem, **where):
        send(dst, dst, ssem, rsem, **where).wait_recv()

    for k in range(1, n_dp):
        src = dp_from(k)
        arrived(tables.at[src], tab_s.at[k], tab_r.at[k], dp=src)

    here = me.astype(f32)
    t_row = lax.broadcasted_iota(jnp.int32, (ROWS, 1), 0).astype(f32)
    lane = lax.broadcasted_iota(jnp.int32, (1, entries), 1).astype(f32)
    shift = jnp.zeros((ROWS, entries), f32)
    order = jnp.zeros((ROWS, entries), f32)
    label = jnp.zeros((ROWS, entries), f32)
    rank = jnp.zeros((1, 1), f32)
    selectors = []
    for s in range(n_dp):
        table = tables[s]
        t_len, t_dest, t_off, t_begin = table[0:1], table[1:2], table[2:3], table[3:4]
        to_me = (t_dest == here) & (t_len > 0.0)
        valid = jnp.max(jnp.where(to_me, 1.0, 0.0), axis=1, keepdims=True)
        match = to_me & (t_off <= t_row) & (t_row < t_off + t_len)
        inside = t_begin - slot_rows * jnp.floor(t_begin / slot_rows)
        shift = shift + jnp.where(match, inside - t_off, 0.0)
        order = order + jnp.where(match, rank, 0.0)
        label = label + jnp.where(match, s * entries + lane, 0.0)
        selectors.append([jnp.where((valid > 0.0) & (rank == r), 1.0, 0.0) for r in range(sources)])
        rank = rank + valid
    q = jnp.sum(shift, axis=1, keepdims=True) + t_row
    rank_of = jnp.sum(order, axis=1, keepdims=True)
    q_part = jnp.floor(q / quarter)
    place = q_part * (sources * quarter) + rank_of * quarter + (q - q_part * quarter)
    spots = lax.broadcasted_iota(jnp.int32, (ROWS, ROWS), 1).astype(f32)
    pick_rows = jnp.where(spots == place, 1.0, 0.0).astype(bf16)
    lab_pad[0:pad] = jnp.full((pad, 128), -1.0, f32)
    lab_pad[pad + ROWS :] = jnp.full((pad, 128), -1.0, f32)
    lab_pad[pad : pad + ROWS] = jnp.broadcast_to(jnp.sum(label, axis=1, keepdims=True), (ROWS, 128))
    for j in range(KERNEL):
        start = pad + j - centre
        masks[j] = jnp.where(lab_pad[start : start + ROWS] == lab_pad[pad : pad + ROWS], 1.0, 0.0)

    for k in range(1, n_dp):
        src = dp_from(k)
        arrived(got.at[src], fr_s.at[k], fr_r.at[k], dp=src)
    picked = [jnp.zeros((quarter, features), f32) for _ in range(sources)]
    for s in range(n_dp):
        rows_s = got[s].astype(f32)
        for r in range(sources):
            picked[r] = picked[r] + selectors[s][r] * rows_s
    comp_all[mine] = jnp.concatenate(picked, 0).astype(bf16)
    cp_c = []
    for k in range(1, n_mp):
        c = send(comp_all.at[mine], comp_all.at[mine], cp_s.at[k], cp_r.at[k], mp=mp_peer(k))
        c.start()
        cp_c.append(c)

    arrived(pcot.at[mine], pc_s.at[0], pc_r.at[0], dp=partner)
    for k in range(1, n_mp):
        c = send(pcot.at[mine], pcot.at[mine], pc_s.at[k], pc_r.at[k], mp=mp_peer(k))
        c.start()
        ct_c.append(c)

    arrived(cot_all.at[across], ct_s.at[0], ct_r.at[0], mp=across)
    c = send(cot_all.at[across], cot_all.at[across], ct_s.at[2], ct_r.at[2], mp=sibling)
    c.start()
    ct_c.append(c)

    def use_cotangent(b, start):
        at = pl.ds(pl.multiple_of(b * width, 128), width)
        values = cot_all[b]
        cot_t[at] = values.T
        term = jnp.dot(values, w_out[at], preferred_element_type=f32)
        gact[...] = term if start else gact[...] + term

    use_cotangent(mine, True)
    use_cotangent(across, False)
    arrived(cot_all.at[sibling], ct_s.at[1], ct_r.at[1], mp=sibling)
    use_cotangent(sibling, False)
    diagonal = lax.rem(sibling + 2, n_mp)
    arrived(cot_all.at[diagonal], ct_s.at[2], ct_r.at[2], mp=sibling)
    use_cotangent(diagonal, False)

    for k in range(1, n_mp):
        src = mp_from(k)
        arrived(comp_all.at[src], cp_s.at[k], cp_r.at[k], mp=src)
    everything = jnp.concatenate([comp_all[b] for b in range(n_mp)], 0)
    packed = jnp.dot(pick_rows, everything, preferred_element_type=f32).astype(bf16)
    packed_t[...] = packed.T
    hidden = jnp.dot(packed, w_in[...], preferred_element_type=f32).astype(bf16).astype(f32)
    for c in range(tiles):
        hpad[c, pad : pad + ROWS] = hidden[:, c * 128 : (c + 1) * 128]

    def columns(c):
        return pl.ds(pl.multiple_of(c * 128, 128), 128)

    dz_c, pt_c = [], []

    z_order = [2, 1, 3, 0]

    def act_tile(c):
        return send(act.at[c], pact.at[c], ac_s.at[c], ac_r.at[c], dp=partner)

    def dz_step(kz):
        zt = lax.rem(zi + kz, n_z)
        at = pl.ds(pl.multiple_of((2 * zt + yi) * block, 64), block)
        for c in range(tiles):
            total = jnp.dot(cot_t[at], act[c], preferred_element_type=f32)
            total = total + jnp.dot(pcot[zt], pact[c], preferred_element_type=f32)
            if kz:
                dz_send[kz, c] = total.astype(bf16)
            else:
                dz_own[c] = total
        if kz:
            c = send(dz_send.at[kz], dz_got.at[kz], dz_s.at[kz], dz_r.at[kz], dp=2 * zt + yi)
            c.start()
            dz_c.append(c)

    def forward(c, carry):
        cs = columns(c)
        weights = taps[:, cs]
        for base in range(0, ROWS, chunk):
            rows = slice(base, base + chunk)
            total = jnp.zeros((chunk, 128), f32)
            for j in range(KERNEL):
                start = pad + base + j - centre
                total = total + weights[j : j + 1] * (hpad[c, start : start + chunk] * masks[j, rows])
            gate = 1.0 / (1.0 + jnp.exp(-total))
            act[c, rows] = (total * gate).astype(bf16)
            gpad[c, pad + base : pad + base + chunk] = gact[rows, cs] * gate * (1.0 + total * (1.0 - gate))
        act_tile(c).start()
        return carry

    lax.fori_loop(0, tiles, forward, 0)
    activated = jnp.concatenate([act[c] for c in range(tiles)], 1)
    for k in [2, 3, 1, 0]:
        at = pl.ds(pl.multiple_of(mp_peer(k) * width, 128), width)
        part[k] = lax.dot_general(
            activated, w_out[at], (((1,), (1,)), ((), ())), preferred_element_type=f32
        ).astype(bf16)
        if k:
            c = send(part.at[k], part_got.at[k], pt_s.at[k], pt_r.at[k], mp=mp_peer(k))
            c.start()
            pt_c.append(c)

    for k in range(1, n_mp):
        src = mp_from(k)
        arrived(pcot.at[src], pc_s.at[k], pc_r.at[k], mp=src)
    for c in range(tiles):
        act_tile(c).wait_recv()
    for kz in z_order[:-2]:
        dz_step(kz)

    g_c = []

    def push(src, dst, ssem, rsem, peer):
        c = send(src, dst, ssem, rsem, dp=peer)
        c.start()
        g_c.append(c)

    def backward(c):
        cs = slice(c * 128, (c + 1) * 128)
        weights = taps[:, cs]
        for base in range(0, ROWS, chunk):
            rows = slice(base, base + chunk)
            values = hpad[c, pad + base : pad + base + chunk]
            total = cot_all[mine, rows, cs].astype(f32)
            for j in range(KERNEL):
                start = pad + base - (j - centre)
                taken = gpad[c, start : start + chunk] * masks[KERNEL - 1 - j, rows]
                total = total + weights[j : j + 1] * taken
                sums = jnp.sum((values * taken).reshape(chunk // 8, 8, 128), axis=0)
                tap_acc[j] = sums if base == 0 else tap_acc[j] + sums
            ghid[rows, cs] = total.astype(bf16)
        for j in range(KERNEL):
            gfull[c, features + j : features + j + 1] = jnp.sum(tap_acc[j], axis=0, keepdims=True)
        gfull[c, 0:features] = jnp.dot(packed_t[...], ghid[:, cs], preferred_element_type=f32)
        for y in range(2):
            for z in range(n_z):
                at = (y * n_z + z) * strip
                gs[c, y, z] = gfull[c, at : at + strip].astype(bf16)
        push(gs.at[c, 1 - yi], gy_got.at[c], gy_s.at[c], gy_r.at[c], partner)

    def over_z(c):
        arrived(gy_got.at[c], gy_s.at[c], gy_r.at[c], dp=partner)
        for kz in z_order:
            zt = lax.rem(zi + kz, n_z)
            at = pl.ds(pl.multiple_of((yi * n_z + zt) * strip, 16), strip)
            total = gfull[c, at] + gy_got[c, zt].astype(f32)
            if kz:
                gz_send[c, kz] = total.astype(bf16)
                push(gz_send.at[c, kz], gz_got.at[c, kz], gz_s.at[c, kz], gz_r.at[c, kz], 2 * zt + yi)
            else:
                g_own[c] = total

    def back_z(c):
        total = g_own[c]
        for kz in range(1, n_z):
            src = 2 * lax.rem(zi + n_z - kz, n_z) + yi
            arrived(gz_got.at[c, kz], gz_s.at[c, kz], gz_r.at[c, kz], dp=src)
            total = total + gz_got[c, kz].astype(f32)
        gall[c, yi, zi] = total.astype(bf16)
        mine_at = gall.at[c, yi, zi]
        for kz in z_order[:-1]:
            push(mine_at, mine_at, ga_s.at[c, kz], ga_r.at[c, kz], 2 * lax.rem(zi + kz, n_z) + yi)
        push(mine_at, mine_at, gb_s.at[c, 0], gb_r.at[c, 0], partner)

    def back_y(c):
        for kz in range(1, n_z):
            src = lax.rem(zi + n_z - kz, n_z)
            arrived(gall.at[c, yi, src], ga_s.at[c, kz], ga_r.at[c, kz], dp=2 * src + yi)
            push(gall.at[c, yi, src], gall.at[c, yi, src], gb_s.at[c, kz], gb_r.at[c, kz], partner)

    for c in range(tiles):
        backward(c)
        if c:
            over_z(c - 1)
    dz_step(z_order[-2])
    for c in range(tiles):
        back_z(c)
        if c == tiles - 2:
            over_z(tiles - 1)
        if c:
            back_y(c - 1)
    dz_step(0)

    branch = part[0].astype(f32)
    for k in range(1, n_mp):
        arrived(part_got.at[k], pt_s.at[k], pt_r.at[k], mp=mp_from(k))
        branch = branch + part_got[k].astype(f32)
    for c in range(tiles):
        part_c = branch[:, c * 128 : (c + 1) * 128]
        out_ref[:, c * 128 : (c + 1) * 128] = (hpad[c, pad : pad + ROWS] + part_c).astype(out_ref.dtype)
    back_y(tiles - 1)
    total = dz_own[...]
    for kz in range(1, n_z):
        src = 2 * lax.rem(zi + n_z - kz, n_z) + yi
        arrived(dz_got.at[kz], dz_s.at[kz], dz_r.at[kz], dp=src)
        total = total + dz_got[kz].astype(f32)
    for c in range(tiles):
        gout_ref[:, c * 128 : (c + 1) * 128] = scale * total[c]
    for c in range(tiles):
        cs = slice(c * 128, (c + 1) * 128)
        for kz in range(n_z):
            src = lax.rem(zi + n_z - kz, n_z)
            arrived(gall.at[c, 1 - yi, src], gb_s.at[c, kz], gb_r.at[c, kz], dp=partner)
        for y in range(2):
            for z in range(n_z):
                at = (y * n_z + z) * strip
                values = scale * gall[c, y, z].astype(f32)
                low = min(max(features - at, 0), strip)
                high = min(max(features + KERNEL - at, 0), strip)
                if low > 0:
                    gin_ref[at : at + low, cs] = values[:low]
                if high > low:
                    gdep_ref[at + low - features : at + high - features, cs] = values[low:high]
    for c in range(tiles):
        act_tile(c).wait_send()
    for c in tab_c + fr_c + ct_c + cp_c + pt_c + dz_c + g_c:
        c.wait_send()


def store_kernel(*refs):
    count = len(refs) // 2
    copies = [pltpu.make_async_copy(refs[i], refs[count + i], refs[-1].at[i]) for i in range(count)]
    for c in copies:
        c.start()
    for c in copies:
        c.wait()


def fused(frames, lengths, destinations, offsets, in_weight, depth_weight, out_weight, cotangent):
    n_dp, n_mp = lax.axis_size("dp"), lax.axis_size("mp")
    src_rows, features = frames.shape
    entries = lengths.shape[1]
    width = cotangent.shape[1]
    model = out_weight.shape[0]
    block = model // n_dp
    quarter = src_rows // n_dp // n_mp
    sources = ROWS * n_dp // src_rows
    strip = -(-(features + KERNEL) // (16 * n_dp)) * 16
    n_z = n_dp // 2
    f32, bf16 = jnp.float32, jnp.bfloat16
    vm = pltpu.VMEM
    i32 = jnp.int32
    tiles = width // 128
    scratch = [
        vm((features, src_rows), bf16),
        vm((1, entries), i32),
        vm((1, entries), i32),
        vm((1, entries), i32),
        vm((features, width), bf16),
        vm((KERNEL, width), bf16),
        vm((model, width), bf16),
        pltpu.SemaphoreType.DMA((8,)),
        vm((n_dp, 8, entries), f32),
        vm((n_dp, quarter, features), bf16),
        vm((n_dp, quarter, features), bf16),
        vm((n_mp, sources * quarter, features), bf16),
        vm((n_mp, ROWS, width), bf16),
        vm((model, ROWS), bf16),
        vm((features, ROWS), bf16),
        vm((ROWS + 32, 128), f32),
        vm((KERNEL, ROWS, 128), f32),
        vm((32, width), f32),
        vm((tiles, ROWS + 32, 128), f32),
        vm((tiles, ROWS, 128), bf16),
        vm((tiles, ROWS, 128), bf16),
        vm((2, block, ROWS), bf16),
        vm((n_mp, block, ROWS), bf16),
        vm((ROWS, width), f32),
        vm((tiles, ROWS + 32, 128), f32),
        vm((ROWS, width), bf16),
        vm((n_mp, ROWS, width), bf16),
        vm((n_mp, ROWS, width), bf16),
        vm((n_z, tiles, block, 128), bf16),
        vm((n_z, tiles, block, 128), bf16),
        vm((tiles, block, 128), f32),
        vm((tiles, n_dp * strip, 128), f32),
        vm((tiles, strip, 128), f32),
        vm((KERNEL, 8, 128), f32),
        vm((tiles, 2, n_z, strip, 128), bf16),
        vm((tiles, n_z, strip, 128), bf16),
        vm((tiles, n_z, strip, 128), bf16),
        vm((tiles, n_z, strip, 128), bf16),
        vm((tiles, 2, n_z, strip, 128), bf16),
    ]
    for shape in ((n_dp,), (n_dp,), (n_mp,), (n_mp,), (n_mp,), (n_mp,), (tiles,), (n_z,), (tiles,)) + ((tiles, n_z),) * 3:
        scratch += [pltpu.SemaphoreType.DMA(shape), pltpu.SemaphoreType.DMA(shape)]
    whole = pl.BlockSpec(memory_space=pltpu.VMEM)
    remote = pl.BlockSpec(memory_space=pl.ANY)
    results = pl.pallas_call(
        functools.partial(fused_kernel, n_dp, n_mp, 1.0 / math.sqrt(n_dp * ROWS)),
        out_shape=(
            jax.ShapeDtypeStruct((ROWS, width), bf16),
            jax.ShapeDtypeStruct((features, width), f32),
            jax.ShapeDtypeStruct((KERNEL, width), f32),
            jax.ShapeDtypeStruct((block, width), f32),
        ),
        in_specs=[remote] * 8,
        out_specs=(whole,) * 4,
        scratch_shapes=scratch,
        compiler_params=pltpu.CompilerParams(
            collective_id=0, has_side_effects=True, vmem_limit_bytes=62 * 1024 * 1024
        ),
    )(frames.T, lengths, destinations, offsets, in_weight, depth_weight, out_weight, cotangent)
    return pl.pallas_call(
        store_kernel,
        out_shape=tuple(jax.ShapeDtypeStruct(r.shape, r.dtype) for r in results),
        in_specs=[whole] * 4,
        out_specs=(remote,) * 4,
        scratch_shapes=[pltpu.SemaphoreType.DMA((4,))],
        compiler_params=pltpu.CompilerParams(vmem_limit_bytes=62 * 1024 * 1024),
    )(*results)


def solution(mesh):
    small = mesh.shape["dp"] == 2 * mesh.shape["mp"] == 8
    placed = (
        P("dp", None),
        P("dp", None),
        P("dp", None),
        P("dp", None),
        P(None, "mp"),
        P(None, "mp"),
        P(None, "mp"),
        P("dp", "mp"),
    )
    return jax.shard_map(
        fused if small else per_device,
        mesh=mesh,
        in_specs=placed,
        out_specs=(P("dp", "mp"), P(None, "mp"), P(None, "mp"), P("dp", "mp")),
        check_vma=False,
    )
```

```python
import functools
import math

import jax
import jax.numpy as jnp
from jax import lax
from jax.experimental import pallas as pl
from jax.experimental.pallas import tpu as pltpu
from jax.sharding import PartitionSpec as P

KERNEL = 31
ROWS = 256
MESH = pl.DeviceIdType.MESH


def depth_conv(values, weights, labels, direction):
    center = (KERNEL - 1) // 2
    length = values.shape[0]
    padded = jnp.pad(values, ((center, center), (0, 0)))
    padded_labels = jnp.pad(labels, (center, center), constant_values=-1)
    result = jnp.zeros(values.shape, jnp.float32)
    for tap_index in range(KERNEL):
        start = center + direction * (tap_index - center)
        matches = (padded_labels[start : start + length] == labels)[:, None]
        taken = weights[tap_index][None, :] * padded[start : start + length]
        result = result + jnp.where(matches, taken, jnp.zeros_like(taken))
    return result


def tap_sums(grads, values, labels):
    center = (KERNEL - 1) // 2
    length = values.shape[0]
    padded = jnp.pad(values, ((center, center), (0, 0)))
    padded_labels = jnp.pad(labels, (center, center), constant_values=-1)
    rows_list = []
    for tap_index in range(KERNEL):
        matches = (padded_labels[tap_index : tap_index + length] == labels)[:, None]
        taken = grads * padded[tap_index : tap_index + length]
        rows_list.append(jnp.sum(jnp.where(matches, taken, jnp.zeros_like(taken)), axis=0))
    return jnp.stack(rows_list, 0)


def per_device(
    frames, lengths, destinations, offsets, in_weight, depth_weight, out_weight, cotangent
):
    dp_count = lax.axis_size("dp")
    src_rows = frames.shape[0]
    features = frames.shape[1]
    slot_rows = src_rows // dp_count
    entries = lengths.shape[1]
    lengths_row = lengths[0]
    end_rows = jnp.cumsum(lengths_row, dtype=jnp.int32)
    begins = end_rows - lengths_row
    row_ids = jnp.arange(src_rows, dtype=jnp.int32)
    owner_table = (begins[None, :] <= row_ids[:, None]) & (row_ids[:, None] < end_rows[None, :])
    occupied_rows = jnp.any(owner_table, axis=1)
    onehot = owner_table.astype(jnp.int32)

    def lookup(table):
        return jnp.sum(onehot * table[None, :], axis=1, dtype=jnp.int32)

    owner_index = lookup(jnp.arange(entries, dtype=jnp.int32))
    target = lookup(offsets[0]) + row_ids - lookup(begins)
    dest_row = lookup(destinations[0])
    source = lax.axis_index("dp")
    row_label = source * entries + owner_index
    dump_index = dp_count * slot_rows
    slot_index = jnp.where(occupied_rows, dest_row * slot_rows + row_ids % slot_rows, dump_index)
    send_frames = (
        jnp.zeros((dump_index + 1, features), frames.dtype)
        .at[slot_index]
        .set(frames)[:dump_index]
        .reshape(dp_count, slot_rows, features)
    )
    send_target = (
        jnp.full((dump_index + 1,), ROWS, jnp.int32)
        .at[slot_index]
        .set(target)[:dump_index]
        .reshape(dp_count, slot_rows)
    )
    send_label = (
        jnp.full((dump_index + 1,), -1, jnp.int32)
        .at[slot_index]
        .set(row_label)[:dump_index]
        .reshape(dp_count, slot_rows)
    )
    got_frames, got_target, got_label = (
        lax.all_to_all(send_frames, "dp", split_axis=0, concat_axis=0, tiled=True),
        lax.all_to_all(send_target, "dp", split_axis=0, concat_axis=0, tiled=True),
        lax.all_to_all(send_label, "dp", split_axis=0, concat_axis=0, tiled=True),
    )
    flat_target = got_target.reshape(-1)
    packed = (
        jnp.zeros((ROWS + 1, features), frames.dtype)
        .at[flat_target]
        .set(got_frames.reshape(-1, features))[:ROWS]
    )
    packed_labels = (
        jnp.full((ROWS + 1,), -1, jnp.int32).at[flat_target].set(got_label.reshape(-1))[:ROWS]
    )
    hidden = jnp.dot(packed, in_weight, preferred_element_type=jnp.float32).astype(jnp.bfloat16)
    hidden_wide = hidden.astype(jnp.float32)
    taps = depth_weight.astype(jnp.float32)
    convolved = depth_conv(hidden_wide, taps, packed_labels, 1)
    activated = jax.nn.silu(convolved).astype(jnp.bfloat16)
    partial_sum = lax.dot_general(
        activated, out_weight, (((1,), (1,)), ((), ())), preferred_element_type=jnp.float32
    )
    branch = lax.psum_scatter(
        partial_sum.astype(jnp.bfloat16), "mp", scatter_dimension=1, tiled=True
    ).astype(jnp.float32)
    output = (hidden_wide + branch).astype(jnp.bfloat16)
    cotangent_full = lax.all_gather(cotangent, "mp", axis=1, tiled=True)
    grad_scale = 1.0 / math.sqrt(dp_count * ROWS)
    grad_activated = jnp.dot(cotangent_full, out_weight, preferred_element_type=jnp.float32)
    sigmoid_value = jax.nn.sigmoid(convolved)
    grad_convolved = grad_activated * sigmoid_value * (1.0 + convolved * (1.0 - sigmoid_value))
    grad_hidden = (
        cotangent.astype(jnp.float32) + depth_conv(grad_convolved, taps, packed_labels, -1)
    ).astype(jnp.bfloat16)
    out_weight_gradient = lax.psum_scatter(
        grad_scale
        * lax.dot_general(
            cotangent_full, activated, (((0,), (0,)), ((), ())), preferred_element_type=jnp.float32
        ),
        "dp",
        scatter_dimension=0,
        tiled=True,
    )
    term_in = grad_scale * lax.dot_general(
        packed, grad_hidden, (((0,), (0,)), ((), ())), preferred_element_type=jnp.float32
    )
    term_depth = grad_scale * tap_sums(grad_convolved, hidden_wide, packed_labels)
    in_weight_gradient, depth_gradient = lax.psum((term_in, term_depth), "dp")
    return (output, in_weight_gradient, depth_gradient, out_weight_gradient)


def fused_kernel(
    n_dp, n_mp, scale,
    frames_in, lens_in, dests_in, offs_in, w_in_in, w_depth_in, w_out_in, cot_in,
    out_ref, gin_ref, gdep_ref, gout_ref,
    frames, lens, dests, offs, w_in, w_depth, w_out, in_sem,
    tables, slots, got, comp_all, cot_all, cot_t, packed, lab_pad, masks, taps, hpad, act, pact, own_t, pcot, gact, gpad, ghid,
    part, part_got, dz_send, dz_got, dz_own, gfull, tap_acc, gs, gy_got, gz_send, gz_got, gall,
    tab_s, tab_r, fr_s, fr_r, cp_s, cp_r, ct_s, ct_r, pc_s, pc_r, pt_s, pt_r, ac_s, ac_r, dz_s, dz_r, gy_s, gy_r, gz_s, gz_r, ga_s, ga_r, gb_s, gb_r,
):
    f32, bf16 = jnp.float32, jnp.bfloat16
    me = lax.axis_index("dp")
    mine = lax.axis_index("mp")
    features, src_rows = frames.shape
    slot_rows = src_rows // n_dp
    quarter = slot_rows // n_mp
    sources = ROWS // slot_rows
    width = cot_all.shape[2]
    entries = lens.shape[1]
    block = gout_ref.shape[0]
    strip = gs.shape[2]
    centre = (KERNEL - 1) // 2
    pad = 16
    n_z = n_dp // 2
    zi, yi = me // 2, lax.rem(me, 2)
    chunk = 64

    def dp_peer(k):
        return lax.rem(me + k, n_dp)

    def dp_from(k):
        return lax.rem(me + n_dp - k, n_dp)

    def mp_peer(k):
        return lax.rem(mine + k, n_mp)

    def mp_from(k):
        return lax.rem(mine + n_mp - k, n_mp)

    def send(src, dst, ssem, rsem, **where):
        return pltpu.make_async_remote_copy(
            src_ref=src, dst_ref=dst, send_sem=ssem, recv_sem=rsem, device_id=where, device_id_type=MESH
        )

    tiles = width // 128
    loads = [
        pltpu.make_async_copy(src, dst, in_sem.at[i])
        for i, (src, dst) in enumerate(
            [(lens_in, lens), (dests_in, dests), (offs_in, offs), (frames_in, frames), (cot_in, cot_all.at[mine]),
             (w_depth_in, w_depth), (w_in_in, w_in), (w_out_in, w_out)]
        )
    ]
    for load in loads:
        load.start()
    barrier = pltpu.get_barrier_semaphore()
    for k in range(1, n_dp):
        pl.semaphore_signal(barrier, inc=1, device_id={"dp": dp_peer(k)}, device_id_type=MESH)
    for k in range(1, n_mp):
        pl.semaphore_signal(barrier, inc=1, device_id={"mp": mp_peer(k)}, device_id_type=MESH)

    for load in loads[:3]:
        load.wait()
    len_f = lens[...].astype(f32)
    dest_f = dests[...].astype(f32)
    off_f = offs[...].astype(f32)
    before = (
        lax.broadcasted_iota(jnp.int32, (entries, entries), 0) < lax.broadcasted_iota(jnp.int32, (entries, entries), 1)
    )
    begin_f = jnp.dot(
        jnp.broadcast_to(len_f, (8, entries)).astype(bf16), jnp.where(before, 1.0, 0.0).astype(bf16),
        preferred_element_type=f32,
    )[0:1]
    tables[me] = jnp.concatenate([len_f, dest_f, off_f, begin_f, jnp.zeros((4, entries), f32)], 0)
    row = lax.broadcasted_iota(jnp.int32, (n_dp * quarter, 1), 0)
    row_dest = (row // quarter).astype(f32)
    row_in = lax.rem(row, quarter).astype(f32)
    first = jnp.min(jnp.where((dest_f == row_dest) & (len_f > 0.0), begin_f, 1e6), axis=1, keepdims=True)
    wanted = first + row_in + (mine * quarter).astype(f32)
    cols = lax.broadcasted_iota(jnp.int32, (n_dp * quarter, src_rows), 1).astype(f32)
    pick = jnp.where(cols == wanted, 1.0, 0.0).astype(bf16)
    loads[3].wait()
    chosen = lax.dot_general(
        pick, frames[...], (((1,), (1,)), ((), ())), preferred_element_type=f32
    ).astype(bf16)
    for d in range(n_dp):
        slots[d] = chosen[d * quarter : (d + 1) * quarter]
    got[me] = slots[me]

    pl.semaphore_wait(barrier, n_dp - 1 + n_mp - 1)
    tab_c, fr_c, ct_c = [], [], []
    for k in range(1, n_dp):
        c = send(tables.at[me], tables.at[me], tab_s.at[k], tab_r.at[k], dp=dp_peer(k))
        c.start()
        tab_c.append(c)
    for k in range(1, n_dp):
        c = send(slots.at[dp_peer(k)], got.at[me], fr_s.at[k], fr_r.at[k], dp=dp_peer(k))
        c.start()
        fr_c.append(c)
    sibling = mine + 1 - 2 * lax.rem(mine, 2)
    across = lax.rem(mine + 2, n_mp)
    for k, peer in ((0, across), (1, sibling)):
        c = send(cot_in, cot_all.at[mine], ct_s.at[k], ct_r.at[k], mp=peer)
        c.start()
        ct_c.append(c)
    for load in loads[4:]:
        load.wait()
    partner = 2 * zi + 1 - yi
    own_t[...] = cot_all[mine].T.reshape(2, block, ROWS)
    c = send(own_t.at[1 - yi], pcot.at[mine], pc_s.at[0], pc_r.at[0], dp=partner)
    c.start()
    ct_c.append(c)

    taps[0:KERNEL] = w_depth[...].astype(f32)
    for ref in (hpad, gpad):
        ref[:, 0:pad] = jnp.zeros((tiles, pad, 128), f32)
        ref[:, pad + ROWS :] = jnp.zeros((tiles, pad, 128), f32)
    gfull[...] = jnp.zeros_like(gfull)

    def arrived(dst, ssem, rsem, **where):
        send(dst, dst, ssem, rsem, **where).wait_recv()

    for k in range(1, n_dp):
        src = dp_from(k)
        arrived(tables.at[src], tab_s.at[k], tab_r.at[k], dp=src)

    here = me.astype(f32)
    t_row = lax.broadcasted_iota(jnp.int32, (ROWS, 1), 0).astype(f32)
    lane = lax.broadcasted_iota(jnp.int32, (1, entries), 1).astype(f32)
    shift = jnp.zeros((ROWS, entries), f32)
    order = jnp.zeros((ROWS, entries), f32)
    label = jnp.zeros((ROWS, entries), f32)
    rank = jnp.zeros((1, 1), f32)
    selectors = []
    for s in range(n_dp):
        table = tables[s]
        t_len, t_dest, t_off, t_begin = table[0:1], table[1:2], table[2:3], table[3:4]
        to_me = (t_dest == here) & (t_len > 0.0)
        valid = jnp.max(jnp.where(to_me, 1.0, 0.0), axis=1, keepdims=True)
        match = to_me & (t_off <= t_row) & (t_row < t_off + t_len)
        inside = t_begin - slot_rows * jnp.floor(t_begin / slot_rows)
        shift = shift + jnp.where(match, inside - t_off, 0.0)
        order = order + jnp.where(match, rank, 0.0)
        label = label + jnp.where(match, s * entries + lane, 0.0)
        selectors.append([jnp.where((valid > 0.0) & (rank == r), 1.0, 0.0) for r in range(sources)])
        rank = rank + valid
    q = jnp.sum(shift, axis=1, keepdims=True) + t_row
    rank_of = jnp.sum(order, axis=1, keepdims=True)
    q_part = jnp.floor(q / quarter)
    place = q_part * (sources * quarter) + rank_of * quarter + (q - q_part * quarter)
    spots = lax.broadcasted_iota(jnp.int32, (ROWS, ROWS), 1).astype(f32)
    pick_rows = jnp.where(spots == place, 1.0, 0.0).astype(bf16)
    lab_pad[0:pad] = jnp.full((pad, 128), -1.0, f32)
    lab_pad[pad + ROWS :] = jnp.full((pad, 128), -1.0, f32)
    lab_pad[pad : pad + ROWS] = jnp.broadcast_to(jnp.sum(label, axis=1, keepdims=True), (ROWS, 128))
    for j in range(KERNEL):
        start = pad + j - centre
        masks[j] = jnp.where(lab_pad[start : start + ROWS] == lab_pad[pad : pad + ROWS], 1.0, 0.0)

    for k in range(1, n_dp):
        src = dp_from(k)
        arrived(got.at[src], fr_s.at[k], fr_r.at[k], dp=src)
    picked = [jnp.zeros((quarter, features), f32) for _ in range(sources)]
    for s in range(n_dp):
        rows_s = got[s].astype(f32)
        for r in range(sources):
            picked[r] = picked[r] + selectors[s][r] * rows_s
    comp_all[mine] = jnp.concatenate(picked, 0).astype(bf16)
    cp_c = []
    for k in range(1, n_mp):
        c = send(comp_all.at[mine], comp_all.at[mine], cp_s.at[k], cp_r.at[k], mp=mp_peer(k))
        c.start()
        cp_c.append(c)

    arrived(pcot.at[mine], pc_s.at[0], pc_r.at[0], dp=partner)
    for k in range(1, n_mp):
        c = send(pcot.at[mine], pcot.at[mine], pc_s.at[k], pc_r.at[k], mp=mp_peer(k))
        c.start()
        ct_c.append(c)

    arrived(cot_all.at[across], ct_s.at[0], ct_r.at[0], mp=across)
    c = send(cot_all.at[across], cot_all.at[across], ct_s.at[2], ct_r.at[2], mp=sibling)
    c.start()
    ct_c.append(c)

    def use_cotangent(b, start):
        at = pl.ds(pl.multiple_of(b * width, 128), width)
        values = cot_all[b]
        cot_t[at] = values.T
        term = jnp.dot(values, w_out[at], preferred_element_type=f32)
        gact[...] = term if start else gact[...] + term

    use_cotangent(mine, True)
    use_cotangent(across, False)
    arrived(cot_all.at[sibling], ct_s.at[1], ct_r.at[1], mp=sibling)
    use_cotangent(sibling, False)
    diagonal = lax.rem(sibling + 2, n_mp)
    arrived(cot_all.at[diagonal], ct_s.at[2], ct_r.at[2], mp=sibling)
    use_cotangent(diagonal, False)

    for k in range(1, n_mp):
        src = mp_from(k)
        arrived(comp_all.at[src], cp_s.at[k], cp_r.at[k], mp=src)
    everything = jnp.concatenate([comp_all[b] for b in range(n_mp)], 0)
    packed[...] = jnp.dot(pick_rows, everything, preferred_element_type=f32).astype(bf16)
    hidden = jnp.dot(packed[...], w_in[...], preferred_element_type=f32).astype(bf16).astype(f32)
    for c in range(tiles):
        hpad[c, pad : pad + ROWS] = hidden[:, c * 128 : (c + 1) * 128]

    def columns(c):
        return pl.ds(pl.multiple_of(c * 128, 128), 128)

    dz_c, pt_c = [], []

    z_order = [2, 1, 3, 0]

    def act_tile(c):
        return send(act.at[c], pact.at[c], ac_s.at[c], ac_r.at[c], dp=partner)

    def dz_step(kz):
        zt = lax.rem(zi + kz, n_z)
        at = pl.ds(pl.multiple_of((2 * zt + yi) * block, 64), block)
        for c in range(tiles):
            total = jnp.dot(cot_t[at], act[c], preferred_element_type=f32)
            total = total + jnp.dot(pcot[zt], pact[c], preferred_element_type=f32)
            if kz:
                dz_send[kz, c] = total.astype(bf16)
            else:
                dz_own[c] = total
        if kz:
            c = send(dz_send.at[kz], dz_got.at[kz], dz_s.at[kz], dz_r.at[kz], dp=2 * zt + yi)
            c.start()
            dz_c.append(c)

    def forward(c, carry):
        cs = columns(c)
        weights = taps[:, cs]
        for base in range(0, ROWS, chunk):
            rows = slice(base, base + chunk)
            total = jnp.zeros((chunk, 128), f32)
            for j in range(KERNEL):
                start = pad + base + j - centre
                total = total + weights[j : j + 1] * (hpad[c, start : start + chunk] * masks[j, rows])
            gate = 1.0 / (1.0 + jnp.exp(-total))
            act[c, rows] = (total * gate).astype(bf16)
            gpad[c, pad + base : pad + base + chunk] = gact[rows, cs] * gate * (1.0 + total * (1.0 - gate))
        act_tile(c).start()
        return carry

    lax.fori_loop(0, tiles, forward, 0)
    def backward(c, carry):
        cs = columns(c)
        weights = taps[:, cs]
        for base in range(0, ROWS, chunk):
            rows = slice(base, base + chunk)
            values = hpad[c, pad + base : pad + base + chunk]
            total = cot_all[mine, rows, cs].astype(f32)
            for j in range(KERNEL):
                start = pad + base - (j - centre)
                taken = gpad[c, start : start + chunk] * masks[KERNEL - 1 - j, rows]
                total = total + weights[j : j + 1] * taken
                sums = jnp.sum((values * taken).reshape(chunk // 8, 8, 128), axis=0)
                tap_acc[j] = sums if base == 0 else tap_acc[j] + sums
            ghid[rows, cs] = total.astype(bf16)
        for j in range(KERNEL):
            gfull[features + j : features + j + 1, cs] = jnp.sum(tap_acc[j], axis=0, keepdims=True)
        return carry

    lax.fori_loop(0, 1, backward, 0)
    for k in range(1, n_mp):
        src = mp_from(k)
        arrived(pcot.at[src], pc_s.at[k], pc_r.at[k], mp=src)
    for c in range(tiles):
        act_tile(c).wait_recv()
    dz_step(z_order[0])
    lax.fori_loop(1, tiles, backward, 0)
    gfull[0:features] = lax.dot_general(
        packed[...], ghid[...], (((0,), (0,)), ((), ())), preferred_element_type=f32
    )
    for y in range(2):
        for z in range(n_z):
            at = (y * n_z + z) * strip
            gs[y, z] = gfull[at : at + strip].astype(bf16)
    g_c = []

    def push(src, dst, ssem, rsem, peer):
        c = send(src, dst, ssem, rsem, dp=peer)
        c.start()
        g_c.append(c)

    push(gs.at[1 - yi], gy_got, gy_s.at[0], gy_r.at[0], partner)
    dz_step(z_order[1])
    activated = jnp.concatenate([act[c] for c in range(tiles)], 1)
    for k in [2, 3, 1, 0]:
        at = pl.ds(pl.multiple_of(mp_peer(k) * width, 128), width)
        part[k] = lax.dot_general(
            activated, w_out[at], (((1,), (1,)), ((), ())), preferred_element_type=f32
        ).astype(bf16)
        if k:
            c = send(part.at[k], part_got.at[k], pt_s.at[k], pt_r.at[k], mp=mp_peer(k))
            c.start()
            pt_c.append(c)

    arrived(gy_got, gy_s.at[0], gy_r.at[0], dp=partner)
    for kz in z_order:
        zt = lax.rem(zi + kz, n_z)
        at = pl.ds(pl.multiple_of((yi * n_z + zt) * strip, 16), strip)
        total = gfull[at] + gy_got[zt].astype(f32)
        if kz:
            gz_send[kz] = total.astype(bf16)
            push(gz_send.at[kz], gz_got.at[kz], gz_s.at[kz], gz_r.at[kz], 2 * zt + yi)
    dz_step(z_order[-2])
    for kz in range(1, n_z):
        arrived(gz_got.at[kz], gz_s.at[kz], gz_r.at[kz], dp=2 * lax.rem(zi + n_z - kz, n_z) + yi)
        total = total + gz_got[kz].astype(f32)
    gall[yi, zi] = total.astype(bf16)
    for kz in z_order[:-1]:
        zt = lax.rem(zi + kz, n_z)
        push(gall.at[yi, zi], gall.at[yi, zi], ga_s.at[kz], ga_r.at[kz], 2 * zt + yi)
    push(gall.at[yi, zi], gall.at[yi, zi], gb_s.at[0], gb_r.at[0], partner)
    dz_step(0)

    branch = part[0].astype(f32)
    for k in range(1, n_mp):
        arrived(part_got.at[k], pt_s.at[k], pt_r.at[k], mp=mp_from(k))
        branch = branch + part_got[k].astype(f32)
    for c in range(tiles):
        part_c = branch[:, c * 128 : (c + 1) * 128]
        out_ref[:, c * 128 : (c + 1) * 128] = (hpad[c, pad : pad + ROWS] + part_c).astype(out_ref.dtype)
    for kz in range(1, n_z):
        src = lax.rem(zi + n_z - kz, n_z)
        arrived(gall.at[yi, src], ga_s.at[kz], ga_r.at[kz], dp=2 * src + yi)
        push(gall.at[yi, src], gall.at[yi, src], gb_s.at[kz], gb_r.at[kz], partner)
    total = dz_own[...]
    for kz in range(1, n_z):
        src = 2 * lax.rem(zi + n_z - kz, n_z) + yi
        arrived(dz_got.at[kz], dz_s.at[kz], dz_r.at[kz], dp=src)
        total = total + dz_got[kz].astype(f32)
    for c in range(tiles):
        gout_ref[:, c * 128 : (c + 1) * 128] = scale * total[c]
    for kz in range(n_z):
        src = lax.rem(zi + n_z - kz, n_z)
        arrived(gall.at[1 - yi, src], gb_s.at[kz], gb_r.at[kz], dp=partner)
    for y in range(2):
        for z in range(n_z):
            at = (y * n_z + z) * strip
            values = scale * gall[y, z].astype(f32)
            low = min(max(features - at, 0), strip)
            high = min(max(features + KERNEL - at, 0), strip)
            if low > 0:
                gin_ref[at : at + low] = values[:low]
            if high > low:
                gdep_ref[at + low - features : at + high - features] = values[low:high]
    for c in range(tiles):
        act_tile(c).wait_send()
    for c in tab_c + fr_c + ct_c + cp_c + pt_c + dz_c + g_c:
        c.wait_send()


def store_kernel(*refs):
    count = len(refs) // 2
    copies = [pltpu.make_async_copy(refs[i], refs[count + i], refs[-1].at[i]) for i in range(count)]
    for c in copies:
        c.start()
    for c in copies:
        c.wait()


def fused(frames, lengths, destinations, offsets, in_weight, depth_weight, out_weight, cotangent):
    n_dp, n_mp = lax.axis_size("dp"), lax.axis_size("mp")
    src_rows, features = frames.shape
    entries = lengths.shape[1]
    width = cotangent.shape[1]
    model = out_weight.shape[0]
    block = model // n_dp
    quarter = src_rows // n_dp // n_mp
    sources = ROWS * n_dp // src_rows
    strip = -(-(features + KERNEL) // (16 * n_dp)) * 16
    n_z = n_dp // 2
    f32, bf16 = jnp.float32, jnp.bfloat16
    vm = pltpu.VMEM
    i32 = jnp.int32
    tiles = width // 128
    scratch = [
        vm((features, src_rows), bf16),
        vm((1, entries), i32),
        vm((1, entries), i32),
        vm((1, entries), i32),
        vm((features, width), bf16),
        vm((KERNEL, width), bf16),
        vm((model, width), bf16),
        pltpu.SemaphoreType.DMA((8,)),
        vm((n_dp, 8, entries), f32),
        vm((n_dp, quarter, features), bf16),
        vm((n_dp, quarter, features), bf16),
        vm((n_mp, sources * quarter, features), bf16),
        vm((n_mp, ROWS, width), bf16),
        vm((model, ROWS), bf16),
        vm((ROWS, features), bf16),
        vm((ROWS + 32, 128), f32),
        vm((KERNEL, ROWS, 128), f32),
        vm((32, width), f32),
        vm((tiles, ROWS + 32, 128), f32),
        vm((tiles, ROWS, 128), bf16),
        vm((tiles, ROWS, 128), bf16),
        vm((2, block, ROWS), bf16),
        vm((n_mp, block, ROWS), bf16),
        vm((ROWS, width), f32),
        vm((tiles, ROWS + 32, 128), f32),
        vm((ROWS, width), bf16),
        vm((n_mp, ROWS, width), bf16),
        vm((n_mp, ROWS, width), bf16),
        vm((n_z, tiles, block, 128), bf16),
        vm((n_z, tiles, block, 128), bf16),
        vm((tiles, block, 128), f32),
        vm((n_dp * strip, width), f32),
        vm((KERNEL, 8, 128), f32),
        vm((2, n_z, strip, width), bf16),
        vm((n_z, strip, width), bf16),
        vm((n_z, strip, width), bf16),
        vm((n_z, strip, width), bf16),
        vm((2, n_z, strip, width), bf16),
    ]
    for shape in ((n_dp,), (n_dp,), (n_mp,), (n_mp,), (n_mp,), (n_mp,), (tiles,), (n_z,), (1,), (n_z,), (n_z,), (n_z,)):
        scratch += [pltpu.SemaphoreType.DMA(shape), pltpu.SemaphoreType.DMA(shape)]
    whole = pl.BlockSpec(memory_space=pltpu.VMEM)
    remote = pl.BlockSpec(memory_space=pl.ANY)
    results = pl.pallas_call(
        functools.partial(fused_kernel, n_dp, n_mp, 1.0 / math.sqrt(n_dp * ROWS)),
        out_shape=(
            jax.ShapeDtypeStruct((ROWS, width), bf16),
            jax.ShapeDtypeStruct((features, width), f32),
            jax.ShapeDtypeStruct((KERNEL, width), f32),
            jax.ShapeDtypeStruct((block, width), f32),
        ),
        in_specs=[remote] * 8,
        out_specs=(whole,) * 4,
        scratch_shapes=scratch,
        compiler_params=pltpu.CompilerParams(
            collective_id=0, has_side_effects=True, vmem_limit_bytes=62 * 1024 * 1024
        ),
    )(frames.T, lengths, destinations, offsets, in_weight, depth_weight, out_weight, cotangent)
    return pl.pallas_call(
        store_kernel,
        out_shape=tuple(jax.ShapeDtypeStruct(r.shape, r.dtype) for r in results),
        in_specs=[whole] * 4,
        out_specs=(remote,) * 4,
        scratch_shapes=[pltpu.SemaphoreType.DMA((4,))],
        compiler_params=pltpu.CompilerParams(vmem_limit_bytes=62 * 1024 * 1024),
    )(*results)


def solution(mesh):
    small = mesh.shape["dp"] == 2 * mesh.shape["mp"] == 8
    placed = (
        P("dp", None),
        P("dp", None),
        P("dp", None),
        P("dp", None),
        P(None, "mp"),
        P(None, "mp"),
        P(None, "mp"),
        P("dp", "mp"),
    )
    return jax.shard_map(
        fused if small else per_device,
        mesh=mesh,
        in_specs=placed,
        out_specs=(P("dp", "mp"), P(None, "mp"), P(None, "mp"), P("dp", "mp")),
        check_vma=False,
    )
```
